32 devices in a mesh: section: 2 (over core), dp: 4 (over z), tensor: 4 (over y, x).
Axes of the slice: x: 2, y: 2, z: 4, core: 2. Of those that a mesh axis runs over, the one named last changes fastest.
Arguments:
- tokens: bfloat16 [2, 8192, 768], P(None, ('dp', 'tensor')), may hold values from -6 to 6
- cotangent: bfloat16 [2, 8192, 768], P(None, ('dp', 'tensor')), may hold values from -6 to 6
- segments: int32 [2, 4, 2048], P(None, 'dp'), may hold values from 0 to 2, never falling along the last dimension, each value on 1 to 1536 neighbouring positions
- heads_in: float32 [2, 3, 768, 768], P('section', None, 'dp', 'tensor'), may hold values from -0.21875 to 0.21875
- heads_out: float32 [2, 768, 768], P('section', 'tensor', 'dp'), may hold values from -1.75 to 1.75
- gate_up: float32 [2, 2, 768, 3072], P('section', None, 'dp', 'tensor'), may hold values from -0.21875 to 0.21875
- project_down: float32 [2, 3072, 768], P('section', 'tensor', 'dp'), may hold values from -0.109375 to 0.109375
- norm_gain: float32 [2, 2, 768], P('section'), may hold values from 0.5 to 1.5
- norm_bias: float32 [2, 2, 768], P('section'), may hold values from -3 to 3
- heads_in_first: float32 [2, 3, 768, 768], P('section', None, 'dp', 'tensor'), may hold values from -26.714922 to 26.714922
- heads_in_second: float32 [2, 3, 768, 768], P('section', None, 'dp', 'tensor'), may hold values from 0.8192 to 13.1072
- heads_out_first: float32 [2, 768, 768], P('section', 'tensor', 'dp'), may hold values from -8.448 to 8.448
- heads_out_second: float32 [2, 768, 768], P('section', 'tensor', 'dp'), may hold values from 0.08192 to 1.31072
- gate_up_first: float32 [2, 2, 768, 3072], P('section', None, 'dp', 'tensor'), may hold values from -42.24 to 42.24
- gate_up_second: float32 [2, 2, 768, 3072], P('section', None, 'dp', 'tensor'), may hold values from 2.048 to 32.768
- project_down_first: float32 [2, 3072, 768], P('section', 'tensor', 'dp'), may hold values from -46.271603 to 46.271603
- project_down_second: float32 [2, 3072, 768], P('section', 'tensor', 'dp'), may hold values from 2.4576 to 39.3216
- norm_first: float32 [2, 2, 2, 768], P('section'), may hold values from -84.48 to 84.48
- norm_second: float32 [2, 2, 2, 768], P('section'), may hold values from 8.192 to 131.072
Outputs:
- layer_out: bfloat16 [2, 2, 8192, 768], P('section', None, ('dp', 'tensor'))
- input_grads: float32 [2, 2, 8192, 768], P('section', None, ('dp', 'tensor'))
- heads_in_new: float32 [2, 3, 768, 768], P('section', None, 'dp', 'tensor')
- heads_in_first_new: float32 [2, 3, 768, 768], P('section', None, 'dp', 'tensor')
- heads_in_second_new: float32 [2, 3, 768, 768], P('section', None, 'dp', 'tensor')
- heads_out_new: float32 [2, 768, 768], P('section', 'tensor', 'dp')
- heads_out_first_new: float32 [2, 768, 768], P('section', 'tensor', 'dp')
- heads_out_second_new: float32 [2, 768, 768], P('section', 'tensor', 'dp')
- gate_up_new: float32 [2, 2, 768, 3072], P('section', None, 'dp', 'tensor')
- gate_up_first_new: float32 [2, 2, 768, 3072], P('section', None, 'dp', 'tensor')
- gate_up_second_new: float32 [2, 2, 768, 3072], P('section', None, 'dp', 'tensor')
- project_down_new: float32 [2, 3072, 768], P('section', 'tensor', 'dp')
- project_down_first_new: float32 [2, 3072, 768], P('section', 'tensor', 'dp')
- project_down_second_new: float32 [2, 3072, 768], P('section', 'tensor', 'dp')
- norm_params_new: float32 [2, 2, 2, 768], P('section')
- norm_first_new: float32 [2, 2, 2, 768], P('section')
- norm_second_new: float32 [2, 2, 2, 768], P('section')
- trust_norms: float32 [2, 4, 2], P('section')
The draws below stay inside these ranges and needn't reach their ends.
Inputs may be any that keep to these rules, and one draw needn't show every extreme that they name: `segments`: along each sequence of 2048 rows the numbers never fall; each of the 3 documents has 1 to 1536 rows, and some document has exactly 1536.
All inputs are finite; a program needn't handle non-finite values.
Results may differ from the reference program's by a relative error of at most 0.03.
Values may be sent and summed in bfloat16 or wider, within the bound.
No kernel may reach another device: no remote copies, remote signals or barrier semaphores. Data moves between devices by JAX's collectives and lax.ppermute only.
A program may use at most 320 MiB of HBM per device.

```python
import math
import jax
import jax.numpy as jnp
import numpy as np
from jax import lax

D = 768
FF = 3072
HEAD = 64
MICRO = 2
WINDOW = 1024
BLOCK = 512
DOCS = 3
STEP = 10
LENGTH = 2048
ROWS = 8192
TOKENS = 16384
DOC_MOST = 1536
N_DP = 4


def block_scale(own_key, dims, split, smallest, high):
    level = 1.0
    for axis_at, blocks in split:
        steps = jax.random.uniform(jax.random.fold_in(jax.random.fold_in(own_key, 6), axis_at), (blocks,), jnp.float32, smallest / len(split), high / len(split))
        level = level * jnp.repeat(jnp.exp(steps), dims[axis_at] // blocks).reshape((-1,) + (1,) * (len(dims) - 1 - axis_at))
    return level


def profile(amount, total, reach, slope):
    weights = [(1 << 20) // math.isqrt(rank ** slope) + 1 for rank in range(2, amount + 1)]
    surplus, holding = total - reach - (amount - 1), [1] * (amount - 1)
    while surplus > 0:
        free = [i for i in range(amount - 1) if holding[i] < reach]
        mass, left = sum([weights[i] for i in free]), surplus
        for i in free:
            more = min(reach - holding[i], max(1, left * weights[i] // mass), surplus)
            holding[i] = holding[i] + more
            surplus = surplus - more
    return np.array([reach] + holding)


def uneven_parts(key, count, total, bound, lean):
    if count == 2:
        one = jax.random.randint(key, (), max(1, total - bound), min(bound, total - 1) + 1)
        return jnp.stack([one, total - one])
    lengths = jnp.asarray(profile(count, total, bound, lean), jnp.int32)
    twos = (count - 1) // 2
    donor, receiver = lengths[1:1 + 2 * twos:2], lengths[2:2 + 2 * twos:2]
    slack = jnp.minimum(donor - 1, bound - receiver)
    passed = jax.random.randint(jax.random.fold_in(key, 1), (twos,), 0, 1 << 20) % (slack + 1)
    lengths = lengths.at[1:1 + 2 * twos:2].set(donor - passed).at[2:2 + 2 * twos:2].set(receiver + passed)
    return lengths[jax.random.permutation(jax.random.fold_in(key, 2), count)]


def normal_values(key, extent, scale, limit, cuts=(), kind=jnp.bfloat16):
    level = block_scale(key, extent, cuts, -0.22, 0.18) if cuts else 1.0
    array = jax.random.normal(key, extent, jnp.float32) * scale * level
    return jnp.minimum(jnp.maximum(array, -limit), limit).astype(kind)


def setup_inputs(seed: int = 0) -> dict:
    arg_keys = jax.random.split(jax.random.key(seed), 20)
    tokens = normal_values(arg_keys[0], (MICRO, ROWS, D), 1.0, 6.0, ((1, 16),))
    cotangent = normal_values(arg_keys[1], (MICRO, ROWS, D), 1.0, 6.0, ((1, 16),))
    segments = jax.vmap(lambda own: jnp.searchsorted(jnp.cumsum(uneven_parts(own, DOCS, LENGTH, DOC_MOST, 1)), jnp.arange(LENGTH), side="right"))(jax.random.split(arg_keys[2], MICRO * N_DP)).reshape((MICRO, N_DP, LENGTH)).astype(jnp.int32)
    heads_in = normal_values(arg_keys[3], (2, 3, D, D), D ** -0.5, 0.21875, ((0, 2), (2, 4), (3, 4)), jnp.float32)
    heads_out = normal_values(arg_keys[4], (2, D, D), (D // 64) ** -0.5, 1.75, ((0, 2), (1, 4), (2, 4)), jnp.float32)
    gate_up = normal_values(arg_keys[5], (2, 2, D, FF), D ** -0.5, 0.21875, ((0, 2), (2, 4), (3, 4)), jnp.float32)
    project_down = normal_values(arg_keys[6], (2, FF, D), FF ** -0.5, 0.109375, ((0, 2), (1, 4), (2, 4)), jnp.float32)
    norm_gain = jnp.clip(1.0 + 0.1 * jax.random.normal(arg_keys[7], (2, 2, D), jnp.float32), 0.5, 1.5)
    norm_bias = normal_values(arg_keys[8], (2, 2, D), 0.3, 3.0, ((0, 2),), jnp.float32)
    heads_in_first = normal_values(arg_keys[9], (2, 3, D, D), (0.11 * (0.1 * TOKENS) ** 0.5), 26.714922, ((0, 2), (2, 4), (3, 4)), jnp.float32)
    heads_in_second = jnp.clip(jnp.exp(math.log(13.1072) - 2.7725887 * jax.random.uniform(arg_keys[10], (2, 3, D, D), jnp.float32) ** block_scale(arg_keys[10], (2, 3, D, D), ((0, 2), (2, 4), (3, 4)), -0.2, 0.2)), 0.8192, 13.1072)
    heads_out_first = normal_values(arg_keys[11], (2, D, D), (0.11 * (0.01 * TOKENS) ** 0.5), 8.448, ((0, 2), (1, 4), (2, 4)), jnp.float32)
    heads_out_second = jnp.clip(jnp.exp(math.log(1.31072) - 2.7725887 * jax.random.uniform(arg_keys[12], (2, D, D), jnp.float32) ** block_scale(arg_keys[12], (2, D, D), ((0, 2), (1, 4), (2, 4)), -0.2, 0.2)), 0.08192, 1.31072)
    gate_up_first = normal_values(arg_keys[13], (2, 2, D, FF), (0.11 * (0.25 * TOKENS) ** 0.5), 42.24, ((0, 2), (2, 4), (3, 4)), jnp.float32)
    gate_up_second = jnp.clip(jnp.exp(math.log(32.768) - 2.7725887 * jax.random.uniform(arg_keys[14], (2, 2, D, FF), jnp.float32) ** block_scale(arg_keys[14], (2, 2, D, FF), ((0, 2), (2, 4), (3, 4)), -0.2, 0.2)), 2.048, 32.768)
    project_down_first = normal_values(arg_keys[15], (2, FF, D), (0.11 * (0.3 * TOKENS) ** 0.5), 46.271603, ((0, 2), (1, 4), (2, 4)), jnp.float32)
    project_down_second = jnp.clip(jnp.exp(math.log(39.3216) - 2.7725887 * jax.random.uniform(arg_keys[16], (2, FF, D), jnp.float32) ** block_scale(arg_keys[16], (2, FF, D), ((0, 2), (1, 4), (2, 4)), -0.2, 0.2)), 2.4576, 39.3216)
    norm_first = normal_values(arg_keys[17], (2, 2, 2, D), (0.11 * TOKENS ** 0.5), 84.48, ((0, 2),), jnp.float32)
    norm_second = jnp.clip(jnp.exp(math.log(131.072) - 2.7725887 * jax.random.uniform(arg_keys[18], (2, 2, 2, D), jnp.float32) ** block_scale(arg_keys[18], (2, 2, 2, D), ((0, 2),), -0.2, 0.2)), 8.192, 131.072)
    return dict(tokens=tokens, cotangent=cotangent, segments=segments, heads_in=heads_in, heads_out=heads_out, gate_up=gate_up, project_down=project_down, norm_gain=norm_gain, norm_bias=norm_bias, heads_in_first=heads_in_first, heads_in_second=heads_in_second, heads_out_first=heads_out_first, heads_out_second=heads_out_second, gate_up_first=gate_up_first, gate_up_second=gate_up_second, project_down_first=project_down_first, project_down_second=project_down_second, norm_first=norm_first, norm_second=norm_second)


HIGH = lax.Precision.HIGHEST
BETA_ONE = 0.9
BETA_TWO = 0.999
ADAM_EPS = 1e-06
DECAY_RATE = 0.01
LEARN_RATE = 0.2
NORM_EPS = 1e-05
ROPE_BASE = 1000.0

@jax.custom_vjp
def low(v):
    return lax.optimization_barrier(v.astype(jnp.bfloat16)).astype(jnp.float32)

@jax.custom_vjp
def low_back(v):
    return v

def low_keep(v):
    return (low(v), None)

def low_pass(kept, grad):
    return (grad,)

def back_keep(v):
    return (v, None)

def back_low(kept, grad):
    return (low(grad),)
low.defvjp(low_keep, low_pass)
low_back.defvjp(back_keep, back_low)

def rope_tables(length):
    half_size = HEAD // 2
    freq_vals = ROPE_BASE ** (-jnp.arange(half_size, dtype=jnp.float32) * 2.0 / HEAD)
    angles = jnp.arange(length, dtype=jnp.float32)[:, None] * freq_vals[None, :]
    cos_tab = jnp.concatenate([jnp.cos(angles), jnp.cos(angles)], axis=1)
    sine_tab = jnp.concatenate([jnp.sin(angles), jnp.sin(angles)], axis=1)
    return (cos_tab, sine_tab)

def rotate(values, cos_tab, sine_tab):
    half_size = HEAD // 2
    turned = jnp.concatenate([-values[..., half_size:], values[..., :half_size]], axis=-1)
    return values * cos_tab[:, None, :] + turned * sine_tab[:, None, :]

def layer_norm(values, gain_row, bias_row):
    mean_val = lax.optimization_barrier(jnp.mean(values, axis=-1, keepdims=True))
    centred = values - mean_val
    variance = lax.optimization_barrier(jnp.mean(centred * centred, axis=-1, keepdims=True))
    return centred * lax.rsqrt(variance + NORM_EPS) * gain_row + bias_row

def attention(query_rot, key_rot, value_low, seq_seg):
    length = query_rot.shape[0]
    blocks = length // BLOCK
    positions = jnp.arange(length, dtype=jnp.int32)
    score_scale = HEAD ** (-0.5)

    @jax.checkpoint
    def one_block(block_index):
        row_start = (block_index * BLOCK).astype(jnp.int32)
        query_rows = lax.dynamic_slice_in_dim(query_rot, row_start, BLOCK, 0)
        query_seg = lax.dynamic_slice_in_dim(seq_seg, row_start, BLOCK, 0)
        query_pos = row_start + jnp.arange(BLOCK, dtype=jnp.int32)
        scores = low_back(jnp.einsum('qhd,khd->hqk', query_rows, key_rot, precision=HIGH) * score_scale)
        allowed = (query_seg[:, None] == seq_seg[None, :]) & (jnp.abs(query_pos[:, None] - positions[None, :]) < WINDOW)
        scores = jnp.where(allowed[None], scores, -1e+30)
        top_score = lax.optimization_barrier(jnp.max(scores, axis=-1, keepdims=True))
        exp_scores = jnp.exp(scores - top_score)
        probs_low = low(exp_scores / lax.optimization_barrier(jnp.sum(exp_scores, axis=-1, keepdims=True)))
        return jnp.einsum('hqk,khd->qhd', probs_low, value_low, precision=HIGH)
    head_rows = lax.map(one_block, jnp.arange(blocks, dtype=jnp.int32))
    return head_rows.reshape(length, query_rot.shape[1], HEAD)

def layer(inputs, params, seq_seg):
    in_matrix, out_matrix, gate_matrix, down_matrix, gain_rows, biases = params
    length = inputs.shape[0]
    cos_tab, sine_tab = rope_tables(length)
    projected = low_back(jnp.einsum('ld,cde->lce', low(inputs), low(in_matrix), precision=HIGH))
    query_rot = low(rotate(projected[:, 0].reshape(length, -1, HEAD), cos_tab, sine_tab))
    key_rot = low(rotate(projected[:, 1].reshape(length, -1, HEAD), cos_tab, sine_tab))
    value_low = low(projected[:, 2].reshape(length, -1, HEAD))
    head_rows = low(low_back(attention(query_rot, key_rot, value_low, seq_seg))).reshape(length, -1)
    attn_out = low_back(jnp.dot(head_rows, low(out_matrix), precision=HIGH))
    hidden = layer_norm(inputs + attn_out, gain_rows[0], biases[0])
    gate_vals = low_back(jnp.einsum('ld,cdf->lcf', low(hidden), low(gate_matrix), precision=HIGH))
    inner_act = low(jax.nn.silu(gate_vals[:, 0]) * gate_vals[:, 1])
    ffn_out = low_back(jnp.dot(inner_act, low(down_matrix), precision=HIGH))
    return layer_norm(hidden + ffn_out, gain_rows[1], biases[1])

def lamb(weight, gradient, first_old, second, axes):
    first_new = BETA_ONE * first_old + (1.0 - BETA_ONE) * gradient
    second_new = BETA_TWO * second + (1.0 - BETA_TWO) * gradient * gradient
    update = first_new / (1.0 - BETA_ONE ** STEP) / (jnp.sqrt(second_new / (1.0 - BETA_TWO ** STEP)) + ADAM_EPS) + DECAY_RATE * weight
    weight_norm = jnp.sqrt(lax.optimization_barrier(jnp.sum(weight * weight, axis=axes, keepdims=True)))
    update_norm = jnp.sqrt(lax.optimization_barrier(jnp.sum(update * update, axis=axes, keepdims=True)))
    return (weight - LEARN_RATE * (weight_norm / update_norm) * update, first_new, second_new, weight_norm, update_norm)

def reference(tokens, cotangent, segments, heads_in, heads_out, gate_up, project_down, norm_gain, norm_bias, heads_in_first, heads_in_second, heads_out_first, heads_out_second, gate_up_first, gate_up_second, project_down_first, project_down_second, norm_first, norm_second):
    seq_count = MICRO * N_DP
    length = tokens.shape[1] // N_DP
    feat_width = tokens.shape[2]
    seqs_in = tokens.astype(jnp.float32).reshape(seq_count, length, feat_width)
    seqs_cot = cotangent.astype(jnp.float32).reshape(seq_count, length, feat_width)
    seq_segs = segments.reshape(seq_count, length)
    params = [(heads_in[section_pos], heads_out[section_pos], gate_up[section_pos], project_down[section_pos], norm_gain[section_pos], norm_bias[section_pos]) for section_pos in range(2)]

    def first_pass(running, paired):
        return (running, layer(paired[0], params[0], paired[1]))
    _, outputs_one = lax.scan(first_pass, jnp.float32(0.0), (seqs_in, seq_segs))

    def make_back(layer_params):

        def step_back(running, triple):
            inputs, seq_seg, grads_out = triple

            def apply_layer(values, weights):
                return layer(values, weights, seq_seg)
            result, pullback = jax.vjp(apply_layer, inputs, layer_params)
            grad_in, grad_params = pullback(grads_out)
            return (jax.tree.map(jnp.add, running, grad_params), (result, grad_in))
        return step_back
    zero_grads = jax.tree.map(jnp.zeros_like, params[1])
    grads_two, (outputs_two, back_two) = lax.scan(make_back(params[1]), zero_grads, (low(outputs_one), seq_segs, seqs_cot))
    sent_back = low(back_two)
    grads_one, (_, back_one) = lax.scan(make_back(params[0]), zero_grads, (seqs_in, seq_segs, sent_back))
    layer_out = jnp.stack([outputs_one, outputs_two]).reshape(2, MICRO, N_DP * length, feat_width).astype(jnp.bfloat16)
    input_grads = jnp.stack([back_one, sent_back]).reshape(2, MICRO, N_DP * length, feat_width)
    all_grads = [grads_one, grads_two]
    matrices = [heads_in, heads_out, gate_up, project_down]
    firsts = [heads_in_first, heads_out_first, gate_up_first, project_down_first]
    seconds = [heads_in_second, heads_out_second, gate_up_second, project_down_second]
    results = []
    norm_rows = []
    for matrix_pos in range(4):
        per_section = [lamb(matrices[matrix_pos][section_pos], all_grads[section_pos][matrix_pos], firsts[matrix_pos][section_pos], seconds[matrix_pos][section_pos], None) for section_pos in range(2)]
        results.append(jnp.stack([item[0] for item in per_section]))
        results.append(jnp.stack([item[1] for item in per_section]))
        results.append(jnp.stack([item[2] for item in per_section]))
        norm_rows.append(jnp.stack([jnp.stack([item[3].reshape(()), item[4].reshape(())]) for item in per_section]))
    trust_norms = jnp.stack(norm_rows, axis=1)
    norm_section = []
    for section_pos in range(2):
        weight = jnp.stack([norm_gain[section_pos], norm_bias[section_pos]])
        gradient = jnp.stack([all_grads[section_pos][4], all_grads[section_pos][5]])
        norm_section.append(lamb(weight, gradient, norm_first[section_pos], norm_second[section_pos], -1))
    norm_params_new = jnp.stack([item[0] for item in norm_section])
    norm_first_new = jnp.stack([item[1] for item in norm_section])
    norm_second_new = jnp.stack([item[2] for item in norm_section])
    return (layer_out, input_grads, results[0], results[1], results[2], results[3], results[4], results[5], results[6], results[7], results[8], results[9], results[10], results[11], norm_params_new, norm_first_new, norm_second_new, trust_norms)
```

```python
import functools
import jax
import jax.numpy as jnp
from jax import lax
from jax.experimental import pallas as pl
from jax.experimental.pallas import tpu as pltpu
from jax.sharding import PartitionSpec as P

HEAD = 64
QB = 512
KT = 512


def attn_fwd_kernel(place, spans, near, far, lo, hi, out, lse_out, q_t, k_n, v_t, o_t, *, heads, keys):
    step = pl.program_id(0)
    width = heads * HEAD
    rows = near.shape[1] // 2

    @pl.when(step == 0)
    def _():
        for slab in range(4):
            src = near if slab < 2 else far
            at = (slab % 2) * rows
            start = pl.multiple_of(place[slab] * rows, rows)
            q_t[:, pl.ds(start, rows)] = src[0:width, at : at + rows]
            v_t[:, pl.ds(start, rows)] = src[2 * width : 3 * width, at : at + rows]
            for h in range(heads):
                k_n[h, pl.ds(start, rows), :] = src[width + h * HEAD : width + (h + 1) * HEAD, at : at + rows].T

    q_start = pl.multiple_of(step * QB, QB)
    low, high = lo[:, pl.ds(q_start, QB)], hi[:, pl.ds(q_start, QB)]
    queries = [q_t[h * HEAD : (h + 1) * HEAD, pl.ds(q_start, QB)] for h in range(heads)]

    def tile(t, carry):
        k_start = pl.multiple_of(t * KT, KT)
        pos = k_start + lax.broadcasted_iota(jnp.int32, (KT, QB), 0)
        allowed = (pos >= low) & (pos <= high)
        out_carry = []
        for h in range(heads):
            top, total, acc = carry[h]
            s = jnp.dot(k_n[h, pl.ds(k_start, KT), :], queries[h], preferred_element_type=jnp.float32)
            s = jnp.where(allowed, s, -1e30)
            new_top = jnp.maximum(top, jnp.max(s, axis=0, keepdims=True))
            p = jnp.exp(s - new_top)
            alpha = jnp.exp(top - new_top)
            total = total * alpha + jnp.sum(p, axis=0, keepdims=True)
            acc = acc * alpha + jnp.dot(
                v_t[h * HEAD : (h + 1) * HEAD, pl.ds(k_start, KT)], p.astype(jnp.bfloat16),
                preferred_element_type=jnp.float32)
            out_carry.append((new_top, total, acc))
        return tuple(out_carry)

    init = tuple((jnp.full((1, QB), -1e30, jnp.float32), jnp.zeros((1, QB), jnp.float32),
                  jnp.zeros((HEAD, QB), jnp.float32)) for _ in range(heads))
    done = lax.fori_loop(spans[0, step], spans[1, step], tile, init)
    for h in range(heads):
        top, total, acc = done[h]
        o_t[h * HEAD : (h + 1) * HEAD, pl.ds(q_start, QB)] = (acc / total).astype(jnp.bfloat16)
        lse_out[h : h + 1, pl.ds(q_start, QB)] = top + jnp.log(total)

    @pl.when(step == pl.num_programs(0) - 1)
    def _():
        for slab in range(4):
            start = pl.multiple_of(place[slab] * rows, rows)
            out[slab] = o_t[:, pl.ds(start, rows)]


def attn_fwd(place, spans, near, far, lo, hi, heads):
    length = 2 * near.shape[1]
    rows = near.shape[1] // 2
    width = heads * HEAD
    smem = pl.BlockSpec(memory_space=pltpu.SMEM)
    whole = lambda s: pl.BlockSpec(s, lambda i: (0,) * len(s))
    return pl.pallas_call(
        functools.partial(attn_fwd_kernel, heads=heads, keys=length),
        grid=(length // QB,),
        in_specs=[smem, smem, whole(near.shape), whole(far.shape), whole(lo.shape), whole(hi.shape)],
        out_specs=(whole((4, width, rows)), whole((heads, length))),
        out_shape=(jax.ShapeDtypeStruct((4, width, rows), jnp.bfloat16),
                   jax.ShapeDtypeStruct((heads, length), jnp.float32)),
        scratch_shapes=[
            pltpu.VMEM((width, length), jnp.bfloat16),
            pltpu.VMEM((heads, length, HEAD), jnp.bfloat16),
            pltpu.VMEM((width, length), jnp.bfloat16),
            pltpu.VMEM((width, length), jnp.bfloat16),
        ],
        compiler_params=pltpu.CompilerParams(vmem_limit_bytes=48 << 20),
        cost_estimate=pl.CostEstimate(flops=4 * length * length * width, bytes_accessed=4 * length * width * 2, transcendentals=heads * length * length),
        name="attn_fwd",
    )(place, spans, near, far, lo, hi)


def attn_bwd_kernel(place, spans, near, far, dout, out_t, lse, lo, hi, cos, sin, dproj,
                    q_t, q_n, k_t, k_n, v_n, do_t, do_n, delta, dq_t, dk, dv, *, heads):
    step = pl.program_id(0)
    width = heads * HEAD
    rows = near.shape[1] // 2
    length = 2 * near.shape[1]

    @pl.when(step == 0)
    def _():
        for slab in range(4):
            src = near if slab < 2 else far
            at = (slab % 2) * rows
            start = pl.multiple_of(place[slab] * rows, rows)
            q_t[:, pl.ds(start, rows)] = src[0:width, at : at + rows]
            k_t[:, pl.ds(start, rows)] = src[width : 2 * width, at : at + rows]
            do_t[:, pl.ds(start, rows)] = dout[slab]
            prod = dout[slab].astype(jnp.float32) * out_t[slab].astype(jnp.float32)
            for h in range(heads):
                piece = slice(h * HEAD, (h + 1) * HEAD)
                delta[h : h + 1, pl.ds(start, rows)] = jnp.sum(prod[piece], axis=0, keepdims=True)
                q_n[h, pl.ds(start, rows), :] = src[h * HEAD : (h + 1) * HEAD, at : at + rows].T
                k_n[h, pl.ds(start, rows), :] = src[width + h * HEAD : width + (h + 1) * HEAD, at : at + rows].T
                v_n[h, pl.ds(start, rows), :] = src[2 * width + h * HEAD : 2 * width + (h + 1) * HEAD, at : at + rows].T
                do_n[h, pl.ds(start, rows), :] = dout[slab, piece, :].T
        dk[...] = jnp.zeros_like(dk)
        dv[...] = jnp.zeros_like(dv)

    q_start = pl.multiple_of(step * QB, QB)
    low, high = lo[:, pl.ds(q_start, QB)], hi[:, pl.ds(q_start, QB)]

    def tile(t, carry):
        k_start = pl.multiple_of(t * KT, KT)
        pos = k_start + lax.broadcasted_iota(jnp.int32, (KT, QB), 0)
        allowed = (pos >= low) & (pos <= high)
        new = []
        for h in range(heads):
            piece = slice(h * HEAD, (h + 1) * HEAD)
            qs, ks = pl.ds(q_start, QB), pl.ds(k_start, KT)
            s = jnp.dot(k_n[h, ks, :], q_t[piece, qs], preferred_element_type=jnp.float32)
            p = jnp.where(allowed, jnp.exp(s - lse[h : h + 1, qs]), 0.0)
            dp = jnp.dot(v_n[h, ks, :], do_t[piece, qs], preferred_element_type=jnp.float32)
            ds = (p * (dp - delta[h : h + 1, qs])).astype(jnp.bfloat16)
            dv[h, ks, :] += jnp.dot(p.astype(jnp.bfloat16), do_n[h, qs, :], preferred_element_type=jnp.float32)
            dk[h, ks, :] += jnp.dot(ds, q_n[h, qs, :], preferred_element_type=jnp.float32)
            new.append(carry[h] + jnp.dot(k_t[piece, ks], ds, preferred_element_type=jnp.float32))
        return tuple(new)

    init = tuple(jnp.zeros((HEAD, QB), jnp.float32) for _ in range(heads))
    done = lax.fori_loop(spans[0, step], spans[1, step], tile, init)
    for h in range(heads):
        dq_t[h * HEAD : (h + 1) * HEAD, pl.ds(q_start, QB)] = done[h]

    @pl.when(step == pl.num_programs(0) - 1)
    def _():
        half = HEAD // 2
        for slab in range(4):
            start = pl.multiple_of(place[slab] * rows, rows)
            c, s = cos[:, pl.ds(start, rows)], sin[:, pl.ds(start, rows)]
            for h in range(heads):
                gq = dq_t[h * HEAD : (h + 1) * HEAD, pl.ds(start, rows)] * HEAD**-0.5
                gk = dk[h, pl.ds(start, rows), :].T
                gv = dv[h, pl.ds(start, rows), :].T
                for kind, g in ((0, gq), (1, gk)):
                    g1, g2 = g[:half], g[half:]
                    at = kind * width + h * HEAD
                    dproj[slab, at : at + half, :] = (g1 * c + g2 * s).astype(jnp.bfloat16)
                    dproj[slab, at + half : at + HEAD, :] = (g2 * c - g1 * s).astype(jnp.bfloat16)
                at = 2 * width + h * HEAD
                dproj[slab, at : at + HEAD, :] = gv.astype(jnp.bfloat16)


def attn_bwd(place, spans, near, far, dout, out_t, lse, lo, hi, cos, sin, heads):
    length = 2 * near.shape[1]
    rows = near.shape[1] // 2
    width = heads * HEAD
    smem = pl.BlockSpec(memory_space=pltpu.SMEM)
    whole = lambda a: pl.BlockSpec(a.shape, lambda i: (0,) * len(a.shape))
    ops = (near, far, dout, out_t, lse, lo, hi, cos, sin)
    return pl.pallas_call(
        functools.partial(attn_bwd_kernel, heads=heads),
        grid=(length // QB,),
        in_specs=[smem, smem] + [whole(a) for a in ops],
        out_specs=pl.BlockSpec((4, 3 * width, rows), lambda i: (0, 0, 0)),
        out_shape=jax.ShapeDtypeStruct((4, 3 * width, rows), jnp.bfloat16),
        scratch_shapes=[
            pltpu.VMEM((width, length), jnp.bfloat16),
            pltpu.VMEM((heads, length, HEAD), jnp.bfloat16),
            pltpu.VMEM((width, length), jnp.bfloat16),
            pltpu.VMEM((heads, length, HEAD), jnp.bfloat16),
            pltpu.VMEM((heads, length, HEAD), jnp.bfloat16),
            pltpu.VMEM((width, length), jnp.bfloat16),
            pltpu.VMEM((heads, length, HEAD), jnp.bfloat16),
            pltpu.VMEM((heads, length), jnp.float32),
            pltpu.VMEM((width, length), jnp.float32),
            pltpu.VMEM((heads, length, HEAD), jnp.float32),
            pltpu.VMEM((heads, length, HEAD), jnp.float32),
        ],
        compiler_params=pltpu.CompilerParams(vmem_limit_bytes=56 << 20),
        cost_estimate=pl.CostEstimate(flops=10 * length * length * width, bytes_accessed=12 * length * width * 2, transcendentals=heads * length * length),
        name="attn_bwd",
    )(place, spans, *ops)


def spans_of(seg, window, length):
    pos = jnp.arange(length, dtype=jnp.int32)
    start = jnp.sum((seg[None, :] < jnp.arange(3, dtype=seg.dtype)[:, None]).astype(jnp.int32), axis=1)
    end = jnp.sum((seg[None, :] <= jnp.arange(3, dtype=seg.dtype)[:, None]).astype(jnp.int32), axis=1) - 1
    pick = lambda t: jnp.where(seg == 0, t[0], jnp.where(seg == 1, t[1], t[2]))
    lo = jnp.maximum(pick(start), pos - (window - 1))
    hi = jnp.minimum(pick(end), pos + (window - 1))
    spans = jnp.stack([lo[::QB] // KT, hi[QB - 1 :: QB] // KT + 1])
    return lo[None], hi[None], spans


WINDOW = 1024
STEP = 10

BETA_ONE = 0.9
BETA_TWO = 0.999
ADAM_EPS = 1e-06
DECAY_RATE = 0.01
LEARN_RATE = 0.2
NORM_EPS = 1e-05
ROPE_BASE = 1000.0

bf16 = jnp.bfloat16
f32 = jnp.float32

BOTH = ("section", "tensor")
CELLS = [(c, y, x) for c in range(2) for y in range(2) for x in range(2)]


def number(c, y, x):
    return c * 4 + y * 2 + x


def moves(target):
    return [(number(*cell), number(*target(*cell))) for cell in CELLS]


SWAP = moves(lambda c, y, x: (y, c, x))
SWAP_BACK = moves(lambda c, y, x: (1 - y, c, x))
SWAP_OUT = moves(lambda c, y, x: (y, 1 - c, x))
CORNER = moves(lambda c, y, x: (1 - c, y, 1 - x))


def over_section(v):
    return lax.ppermute(v, "section", [(0, 1), (1, 0)])


def over_x(v):
    return lax.ppermute(v, "tensor", [(0, 1), (1, 0), (2, 3), (3, 2)])


def over_y(v):
    return lax.ppermute(v, "tensor", [(0, 2), (1, 3), (2, 0), (3, 1)])


def over_diag(v):
    return lax.ppermute(v, "tensor", [(0, 3), (1, 2), (2, 1), (3, 0)])


def over_both(v, pairs):
    return lax.ppermute(v, BOTH, pairs)


def over_z(v, k):
    return lax.ppermute(v, "dp", [(i, i ^ k) for i in range(4)])


def gather_dp(piece, axis):
    if lax.axis_size("dp") != 4:
        return lax.all_gather(piece, "dp", axis=axis, tiled=True)
    z = lax.axis_index("dp")
    deep = piece.shape[axis]
    whole = jnp.zeros(piece.shape[:axis] + (4 * deep,) + piece.shape[axis + 1 :], piece.dtype)
    for k in range(4):
        got = piece if k == 0 else over_z(piece, k)
        whole = lax.dynamic_update_slice_in_dim(whole, got, (z ^ k) * deep, axis)
    return whole


def scatter_dp(whole, axis):
    if lax.axis_size("dp") != 4:
        return lax.psum_scatter(whole, "dp", scatter_dimension=axis, tiled=True).astype(f32)
    z = lax.axis_index("dp")
    deep = whole.shape[axis] // 4
    parts = [lax.dynamic_slice_in_dim(whole, (z ^ k) * deep, deep, axis) for k in range(4)]
    got = [parts[0]] + [over_z(parts[k], k) for k in range(1, 4)]
    got = [g.astype(f32) for g in got]
    return (got[0] + got[1]) + (got[2] + got[3])


def chips_total(v):
    v = (v + over_x(v)) + (over_y(v) + over_diag(v))
    if lax.axis_size("dp") != 4:
        return lax.psum(v, "dp")
    return (v + over_z(v, 1)) + (over_z(v, 2) + over_z(v, 3))


def rope_tables(length):
    half_size = HEAD // 2
    freq_vals = ROPE_BASE ** (-jnp.arange(half_size, dtype=f32) * 2.0 / HEAD)
    angles = freq_vals[:, None] * jnp.arange(length, dtype=f32)[None, :]
    return jnp.cos(angles), jnp.sin(angles)


def norm_fwd(values, gain_row, bias_row):
    mean_val = jnp.mean(values, axis=-1, keepdims=True)
    centred = values - mean_val
    variance = jnp.mean(centred * centred, axis=-1, keepdims=True)
    inv_std = lax.rsqrt(variance + NORM_EPS)
    normed = centred * inv_std
    return (normed * gain_row + bias_row, normed, inv_std)


def norm_back(grad_out, normed, inv_std, gain_row):
    grad_gain = jnp.sum(grad_out * normed, axis=0)
    grad_bias = jnp.sum(grad_out, axis=0)
    grad_normed = grad_out * gain_row
    grad_vals = inv_std * (
        grad_normed
        - jnp.mean(grad_normed, axis=-1, keepdims=True)
        - normed * jnp.mean(grad_normed * normed, axis=-1, keepdims=True)
    )
    return (grad_vals, grad_gain, grad_bias)


def dot(spec, a, b):
    return jnp.einsum(spec, a, b, preferred_element_type=f32)


def project_in(rows, matrix, cos, sin):
    width = matrix.shape[1] // 4
    heads = width // HEAD
    got = dot("de,ld->el", matrix[:, : 3 * width], rows)
    length = got.shape[1]
    parts = got.reshape(3, heads, 2, HEAD // 2, length)
    first, second = parts[:2, :, 0], parts[:2, :, 1]
    turned = jnp.stack([first * cos - second * sin, second * cos + first * sin], axis=2).astype(bf16)
    scale = jnp.array([HEAD**-0.5, 1.0], bf16).reshape(2, 1, 1, 1, 1)
    return jnp.concatenate([(turned * scale).reshape(2 * width, length), got[2 * width :].astype(bf16)], axis=0)


def layer_forward(own, weights, gains, biases, env):
    matrix, out_matrix, ffn = weights
    place, spans, low, high, tables = env
    heads = matrix.shape[1] // 4 // HEAD
    across = over_x(own)
    near = jnp.concatenate([own, over_section(own)], axis=0)
    far = jnp.concatenate([across, over_section(across)], axis=0)
    near_qkv = project_in(near, matrix, *tables[0])
    far_qkv = project_in(far, matrix, *tables[1])
    mine, log_sums = attn_fwd(place, spans, near_qkv, far_qkv, low, high, heads)
    all_heads = jnp.concatenate(
        [mine[0], over_section(mine[1]), over_x(mine[2]), over_both(mine[3], CORNER)], axis=0
    )
    mixed = own.astype(f32) + dot("el,ed->ld", all_heads, out_matrix)
    hidden, normed_one, inv_one = norm_fwd(mixed, gains[0], biases[0])
    hidden_low = hidden.astype(bf16)
    hidden_rows = [hidden_low, over_x(hidden_low)]
    partial, acts = [], []
    for rows in hidden_rows:
        total, kept = 0.0, []
        for gate_up_down in ffn:
            gate = dot("ld,df->lf", rows, gate_up_down[0])
            up = dot("ld,df->lf", rows, gate_up_down[1])
            inner = (jax.nn.silu(gate) * up).astype(bf16)
            total = total + dot("lf,df->ld", inner, gate_up_down[2])
            kept.append((gate.astype(bf16), up.astype(bf16), inner))
        partial.append(total)
        acts.append(kept)
    ffn_out = partial[0] + over_x(partial[1].astype(bf16)).astype(f32)
    output, normed_two, inv_two = norm_fwd(hidden + ffn_out, gains[1], biases[1])
    kept = (near, far, near_qkv, far_qkv, mine, log_sums, all_heads, normed_one, inv_one, hidden_rows, acts, normed_two, inv_two)
    return output, kept


def layer_backward(grad_out, kept, weights, gains, env):
    matrix, out_matrix, ffn = weights
    place, spans, low, high, tables = env
    (near, far, near_qkv, far_qkv, mine, log_sums, all_heads, normed_one, inv_one, hidden_rows, acts, normed_two, inv_two) = kept
    width = matrix.shape[1] // 4
    heads = width // HEAD
    grad_mixed, gain_two, bias_two = norm_back(grad_out, normed_two, inv_two, gains[1])
    grad_low = grad_mixed.astype(bf16)
    grad_rows = [grad_low, over_x(grad_low)]
    partial, grads = [], []
    for rows, row_acts in zip(grad_rows, acts):
        total, made = 0.0, []
        for gate_up_down, (gate, up, inner) in zip(ffn, row_acts):
            grad_inner = dot("ld,df->lf", rows, gate_up_down[2])
            gate, up = gate.astype(f32), up.astype(f32)
            sig = jax.nn.sigmoid(gate)
            grad_gate = (grad_inner * up * (sig * (1.0 + gate * (1.0 - sig)))).astype(bf16)
            grad_up = (grad_inner * (gate * sig)).astype(bf16)
            total = total + dot("lf,df->ld", grad_gate, gate_up_down[0]) + dot("lf,df->ld", grad_up, gate_up_down[1])
            made.append((grad_gate, grad_up))
        partial.append(total)
        grads.append(made)
    hidden_sum = partial[0] + over_x(partial[1].astype(bf16)).astype(f32)
    hidden_both = jnp.concatenate(hidden_rows, axis=0)
    grad_both = jnp.concatenate(grad_rows, axis=0)
    ffn_grads = []
    for b in range(2):
        grad_gate, grad_up, inner = (
            jnp.concatenate([grads[r][b][0] for r in range(2)], axis=0),
            jnp.concatenate([grads[r][b][1] for r in range(2)], axis=0),
            jnp.concatenate([acts[r][b][2] for r in range(2)], axis=0),
        )
        ffn_grads.append(
            jnp.stack(
                [
                    dot("ld,lf->df", hidden_both, grad_gate).astype(bf16),
                    dot("ld,lf->df", hidden_both, grad_up).astype(bf16),
                    dot("ld,lf->df", grad_both, inner).astype(bf16),
                ]
            )
        )
    ffn_grad = (ffn_grads[0].astype(f32) + over_section(ffn_grads[1]).astype(f32)).astype(bf16)
    grad_hidden = grad_mixed + hidden_sum
    grad_mixed_one, gain_one, bias_one = norm_back(grad_hidden, normed_one, inv_one, gains[0])
    attn_low = grad_mixed_one.astype(bf16)
    grad_heads = dot("ed,ld->el", out_matrix, attn_low).astype(bf16).reshape(4, width, -1)
    out_grad = dot("el,ld->ed", all_heads, attn_low).astype(bf16).reshape(4, width, -1)
    out_pair = out_grad[::2].astype(f32) + over_section(out_grad[1::2]).astype(f32)
    out_own = out_pair[0] + over_x(out_pair[1].astype(bf16)).astype(f32)
    grad_mine = jnp.stack(
        [grad_heads[0], over_section(grad_heads[1]), over_x(grad_heads[2]), over_both(grad_heads[3], CORNER)]
    )
    cos, sin = env[4][2]
    grad_proj = attn_bwd(place, spans, near_qkv, far_qkv, grad_mine, mine, log_sums, low, high, cos, sin, heads)
    rows_part = [dot("el,de->ld", grad_proj[p], matrix[:, : 3 * width]).astype(bf16) for p in (1, 3, 2, 0)]
    pair = over_section(jnp.stack(rows_part[:2])).astype(f32)
    near_sum = rows_part[3].astype(f32) + pair[0]
    far_sum = (rows_part[2].astype(f32) + pair[1]).astype(bf16)
    rows_sum = near_sum + over_x(far_sum).astype(f32)
    half = near.shape[0] // 2
    slabs = (near[:half], near[half:], far[:half], far[half:])
    in_grad = sum(dot("el,ld->ed", grad_proj[p], slabs[p]) for p in range(4))
    matrix_grad = jnp.concatenate([in_grad, out_own], axis=0).T.astype(bf16)
    norm_grads = jnp.stack([jnp.stack([gain_one, gain_two]), jnp.stack([bias_one, bias_two])])
    return grad_mixed_one + rows_sum, matrix_grad, ffn_grad, norm_grads


def lamb_parts(weight, gradient, first_old, second):
    first_new = BETA_ONE * first_old + (1.0 - BETA_ONE) * gradient
    second_new = BETA_TWO * second + (1.0 - BETA_TWO) * gradient * gradient
    update = (
        first_new
        / (1.0 - BETA_ONE**STEP)
        / (jnp.sqrt(second_new / (1.0 - BETA_TWO**STEP)) + ADAM_EPS)
        + DECAY_RATE * weight
    )
    return (first_new, second_new, update)


def body(
    tokens,
    cotangent,
    segments,
    heads_in,
    heads_out,
    gate_up,
    project_down,
    norm_gain,
    norm_bias,
    heads_in_first,
    heads_in_second,
    heads_out_first,
    heads_out_second,
    gate_up_first,
    gate_up_second,
    project_down_first,
    project_down_second,
    norm_first,
    norm_second,
):
    section = lax.axis_index("section")
    spot = lax.axis_index("tensor")
    y, x = spot // 2, spot % 2
    rows = tokens.shape[1]
    length = segments.shape[-1]
    masters = (heads_in[0], heads_out[0], gate_up[0], project_down[0])
    deep, width = masters[0].shape[1:]

    own = over_both(lax.dynamic_index_in_dim(tokens, section, 0, keepdims=False), SWAP)
    grad_top = over_both(lax.dynamic_index_in_dim(cotangent, section, 0, keepdims=False), SWAP)

    attn_piece = jnp.concatenate(
        [masters[0].transpose(1, 0, 2).reshape(deep, 3 * width), masters[1].T], axis=1
    ).astype(bf16)
    ffn_piece = jnp.concatenate([masters[2], masters[3].T[None]], axis=0).astype(bf16)

    def to_blocks(piece):
        same, other = over_both(piece, SWAP), over_both(piece, SWAP_OUT)
        return jnp.where(y == 0, same, other), jnp.where(y == 0, other, same)

    attn_pieces, ffn_pieces = to_blocks(attn_piece), to_blocks(ffn_piece)
    weights = []
    for layer in range(2):
        matrix = gather_dp(attn_pieces[layer], 0)
        ffn_own = lax.all_gather(ffn_pieces[layer], "dp", axis=1, tiled=True)
        out_own = matrix[:, 3 * width :].T
        pair = jnp.stack([out_own, over_x(out_own)])
        pair_other = over_section(pair)
        out_matrix = jnp.concatenate([pair[0], pair_other[0], pair[1], pair_other[1]], axis=0)
        weights.append((matrix, out_matrix, (ffn_own, over_section(ffn_own))))

    both_params = jnp.stack([norm_gain[0], norm_bias[0]])
    other_params = over_section(both_params)
    params = [
        jnp.where(section == 0, both_params, other_params),
        jnp.where(section == 0, other_params, both_params),
    ]

    block = 2 * section + x
    place = jnp.stack([block, block ^ 2, block ^ 1, block ^ 3]).astype(jnp.int32)
    seq_seg = lax.dynamic_index_in_dim(segments, y, 0, keepdims=False)[0]
    low, high, spans = spans_of(seq_seg, WINDOW, length)
    cos, sin = rope_tables(length)

    def pick(table, slabs):
        return jnp.concatenate(
            [lax.dynamic_slice_in_dim(table, place[s] * rows, rows, 1) for s in slabs], axis=1
        )

    tables = (
        (pick(cos, (0, 1)), pick(sin, (0, 1))),
        (pick(cos, (2, 3)), pick(sin, (2, 3))),
        (cos, sin),
    )
    env = (place, spans, low, high, tables)

    out_zero, kept_zero = layer_forward(own, weights[0], params[0][0], params[0][1], env)
    low_zero = out_zero.astype(bf16)
    out_one, kept_one = layer_forward(low_zero, weights[1], params[1][0], params[1][1], env)
    low_one = out_one.astype(bf16)
    grad_one, matrix_one, ffn_one, norm_one = layer_backward(
        grad_top.astype(f32), kept_one, weights[1], params[1][0], env
    )
    sent = grad_one.astype(bf16)
    grad_zero, matrix_zero, ffn_zero, norm_zero = layer_backward(
        sent.astype(f32), kept_zero, weights[0], params[0][0], env
    )

    def home(zero, one):
        same = over_both(jnp.where(y == 0, zero, one), SWAP)
        other = over_both(jnp.where(y == 0, one, zero), SWAP_BACK)
        return same, other

    def by_micro(zero, one):
        same, other = home(zero, one)
        return jnp.stack([jnp.where(section == 0, same, other), jnp.where(section == 0, other, same)])

    layer_out = by_micro(low_zero, low_one)
    input_grads = by_micro(grad_zero.astype(bf16), sent).astype(f32)

    ffn_shards = [
        lax.psum_scatter(g, "dp", scatter_dimension=1, tiled=True) for g in (ffn_zero, ffn_one)
    ]
    ffn_home = home(*ffn_shards)
    ffn_grad = ffn_home[0].astype(f32) + ffn_home[1].astype(f32)
    attn_shards = [scatter_dp(g, 0).astype(bf16) for g in (matrix_zero, matrix_one)]
    attn_home = home(*attn_shards)
    attn_grad = attn_home[0].astype(f32) + attn_home[1].astype(f32)
    grad_shards = (
        attn_grad[:, : 3 * width].reshape(deep, 3, width).transpose(1, 0, 2),
        attn_grad[:, 3 * width :].T,
        ffn_grad[:2],
        ffn_grad[2].T,
    )
    norm_mine = jnp.where(section == 0, norm_zero, norm_one) + over_section(
        jnp.where(section == 0, norm_one, norm_zero)
    )
    norm_total = chips_total(norm_mine)

    firsts = (heads_in_first[0], heads_out_first[0], gate_up_first[0], project_down_first[0])
    seconds = (heads_in_second[0], heads_out_second[0], gate_up_second[0], project_down_second[0])
    parts = [lamb_parts(masters[i], grad_shards[i], firsts[i], seconds[i]) for i in range(4)]
    squares = jnp.stack(
        [jnp.sum(matrix * matrix) for matrix in masters] + [jnp.sum(item[2] * item[2]) for item in parts]
    )
    square_total = chips_total(jnp.broadcast_to(squares[:, None], (8, 128)))[:, 0]
    weight_norms = jnp.sqrt(square_total[:4])
    update_norms = jnp.sqrt(square_total[-4:])
    new_mats = [
        masters[i] - LEARN_RATE * (weight_norms[i] / update_norms[i]) * parts[i][2] for i in range(4)
    ]
    norm_now = both_params
    norm_first_new, norm_second_new, norm_update = lamb_parts(
        norm_now, norm_total, norm_first[0], norm_second[0]
    )
    norm_wn = jnp.sqrt(jnp.sum(norm_now * norm_now, axis=-1, keepdims=True))
    norm_un = jnp.sqrt(jnp.sum(norm_update * norm_update, axis=-1, keepdims=True))
    norm_params_new = norm_now - LEARN_RATE * (norm_wn / norm_un) * norm_update
    trust_norms = jnp.stack([weight_norms, update_norms], axis=1)
    outs = [layer_out, input_grads]
    for i in range(4):
        outs += [new_mats[i], parts[i][0], parts[i][1]]
    outs += [norm_params_new, norm_first_new, norm_second_new, trust_norms]
    return tuple(item[None] for item in outs)


def solution(mesh):
    rows = P(None, ("dp", "tensor"), None)
    out_rows = P("section", None, ("dp", "tensor"), None)
    columns = P("section", None, "dp", "tensor")
    turned = P("section", "tensor", "dp")
    vectors = P("section", None, None)
    pairs = P("section", None, None, None)
    return jax.shard_map(
        body,
        mesh=mesh,
        in_specs=(rows, rows, P(None, "dp", None), columns, turned, columns, turned, vectors, vectors)
        + (columns, columns, turned, turned, columns, columns, turned, turned, pairs, pairs),
        out_specs=(out_rows, out_rows)
        + (columns,) * 3
        + (turned,) * 3
        + (columns,) * 3
        + (turned,) * 3
        + (pairs,) * 3
        + (vectors,),
        check_vma=False,
    )
```

```python
import functools

import jax
import jax.numpy as jnp
import numpy as np
from jax import lax
from jax.experimental import pallas as pl
from jax.experimental.pallas import tpu as pltpu
from jax.sharding import PartitionSpec as P

HEAD = 64
FQ, FK = 512, 512
BQ, BK = 256, 512
SAFE = 40.0
WINDOW = 1024


def doc_bounds(pos, ends, length):
    start = jnp.where(pos < ends[0], 0, jnp.where(pos < ends[1], ends[0], ends[1]))
    last = jnp.where(pos < ends[0], ends[0], jnp.where(pos < ends[1], ends[1], length)) - 1
    return jnp.maximum(start, pos - (WINDOW - 1)), jnp.minimum(last, pos + (WINDOW - 1))


def key_span(q_start, rows, ends, length, deep):
    low, _ = doc_bounds(q_start, ends, length)
    _, high = doc_bounds(q_start + rows - 1, ends, length)
    first = low // 128 * 128
    tiles = (high + 1 - first + deep - 1) // deep
    return jnp.minimum(first, length - tiles * deep), tiles


def attn_fwd_kernel(place, ends, near, far, matrix, cos, sin, out, lse, qkv, a_t, k_n, o_t, calm, *, heads):
    step = pl.program_id(0)
    width = heads * HEAD
    half = HEAD // 2
    length = qkv.shape[1]
    rows = length // 4

    @pl.when(step == 0)
    def _():
        a_t[...] = matrix[:, : 3 * width].T
        tops = [jnp.zeros((1, rows), jnp.float32) for _ in range(2 * heads)]
        for slab in range(4):
            src = near if slab < 2 else far
            start = pl.multiple_of(place[slab] * rows, rows)
            here = pl.ds(start, rows)
            proj = lax.dot_general(
                a_t[...], src[(slab % 2) * rows : (slab % 2 + 1) * rows, :], (((1,), (1,)), ((), ())),
                preferred_element_type=jnp.float32,
            )
            c, s = cos[:, here], sin[:, here]
            for i in range(2 * heads):
                first, second = proj[i * HEAD : i * HEAD + half], proj[i * HEAD + half : (i + 1) * HEAD]
                turned = jnp.concatenate([first * c - second * s, second * c + first * s], axis=0).astype(jnp.bfloat16)
                if i < heads:
                    turned = turned * jnp.bfloat16(HEAD**-0.5)
                else:
                    k_n[i - heads, here, :] = turned.T
                qkv[i * HEAD : (i + 1) * HEAD, here] = turned
                size = turned.astype(jnp.float32)
                tops[i] = jnp.maximum(tops[i], jnp.sum(size * size, axis=0, keepdims=True))
            qkv[2 * width :, here] = proj[2 * width :].astype(jnp.bfloat16)
        worst = jnp.float32(0.0)
        for h in range(heads):
            worst = jnp.maximum(worst, jnp.max(tops[h]) * jnp.max(tops[heads + h]))
        calm[0] = (worst <= SAFE * SAFE).astype(jnp.int32)

    q_start = pl.multiple_of(step * FQ, FQ)
    here = pl.ds(q_start, FQ)
    low, high = doc_bounds(q_start + lax.broadcasted_iota(jnp.int32, (1, FQ), 1), (ends[0], ends[1]), length)
    first, tiles = key_span(q_start, FQ, (ends[0], ends[1]), length, FK)

    def score(h, keys):
        return jnp.dot(k_n[h, keys, :], qkv[h * HEAD : (h + 1) * HEAD, here], preferred_element_type=jnp.float32)

    def weigh(h, keys, p):
        return jnp.dot(
            qkv[2 * width + h * HEAD : 2 * width + (h + 1) * HEAD, keys], p.astype(jnp.bfloat16),
            preferred_element_type=jnp.float32,
        )

    def mask(t):
        k_start = pl.multiple_of(first + t * FK, 128)
        pos = k_start + lax.broadcasted_iota(jnp.int32, (FK, FQ), 0)
        return pl.ds(k_start, FK), (pos >= low) & (pos <= high)

    def finish(h, total, acc, log_sum):
        o_t[h * HEAD : (h + 1) * HEAD, here] = (acc / total).astype(jnp.bfloat16)
        lse[h : h + 1, here] = log_sum

    @pl.when(calm[0] == 1)
    def _():
        def tile(t, carry):
            keys, allowed = mask(t)
            new = []
            nxt = score(0, keys)
            for h in range(heads):
                total, acc = carry[h]
                s = nxt
                if h + 1 < heads:
                    nxt = score(h + 1, keys)
                p = jnp.where(allowed, jnp.exp(s), 0.0)
                new.append((total + jnp.sum(p, axis=0, keepdims=True), acc + weigh(h, keys, p)))
            return tuple(new)

        init = tuple((jnp.zeros((1, FQ), jnp.float32), jnp.zeros((HEAD, FQ), jnp.float32)) for _ in range(heads))
        for h, (total, acc) in enumerate(lax.fori_loop(0, tiles, tile, init)):
            finish(h, total, acc, jnp.log(total))

    @pl.when(calm[0] == 0)
    def _():
        def tile(t, carry):
            keys, allowed = mask(t)
            new = []
            for h in range(heads):
                top, total, acc = carry[h]
                s = jnp.where(allowed, score(h, keys), -1e30)
                new_top = jnp.maximum(top, jnp.max(s, axis=0, keepdims=True))
                p = jnp.exp(s - new_top)
                alpha = jnp.exp(top - new_top)
                total = total * alpha + jnp.sum(p, axis=0, keepdims=True)
                new.append((new_top, total, acc * alpha + weigh(h, keys, p)))
            return tuple(new)

        init = tuple(
            (jnp.full((1, FQ), -1e30, jnp.float32), jnp.zeros((1, FQ), jnp.float32), jnp.zeros((HEAD, FQ), jnp.float32))
            for _ in range(heads)
        )
        for h, (top, total, acc) in enumerate(lax.fori_loop(0, tiles, tile, init)):
            finish(h, total, acc, top + jnp.log(total))

    @pl.when(step == pl.num_programs(0) - 1)
    def _():
        for slab in range(4):
            out[slab] = o_t[:, pl.ds(pl.multiple_of(place[slab] * rows, rows), rows)]


def whole_spec(a):
    return pl.BlockSpec(a.shape, lambda i: (0,) * len(a.shape))


def attn_fwd(place, ends, near, far, matrix, cos, sin):
    length = 2 * near.shape[0]
    rows = length // 4
    width = matrix.shape[1] // 4
    heads = width // HEAD
    smem = pl.BlockSpec(memory_space=pltpu.SMEM)
    ops = (near, far, matrix, cos, sin)
    outs = (
        jax.ShapeDtypeStruct((4, width, rows), jnp.bfloat16),
        jax.ShapeDtypeStruct((heads, length), jnp.float32),
        jax.ShapeDtypeStruct((3 * width, length), jnp.bfloat16),
    )
    return pl.pallas_call(
        functools.partial(attn_fwd_kernel, heads=heads),
        grid=(length // FQ,),
        in_specs=[smem, smem] + [whole_spec(a) for a in ops],
        out_specs=tuple(whole_spec(o) for o in outs),
        out_shape=outs,
        scratch_shapes=[
            pltpu.VMEM((3 * width, matrix.shape[0]), jnp.bfloat16),
            pltpu.VMEM((heads, length, HEAD), jnp.bfloat16),
            pltpu.VMEM((width, length), jnp.bfloat16),
            pltpu.SMEM((1,), jnp.int32),
        ],
        compiler_params=pltpu.CompilerParams(vmem_limit_bytes=48 << 20),
        cost_estimate=pl.CostEstimate(
            flops=6 * length * length * width, bytes_accessed=16 * length * width, transcendentals=heads * length * length
        ),
        name="attn_fwd",
    )(place, ends, *ops)


def attn_bwd_kernel(place, ends, qkv, dout, out_t, lse, cos, sin, dproj, q_n, k_n, v_n, do_t, do_n, delta, dq_t, dk, dv, *, heads):
    step = pl.program_id(0)
    width = heads * HEAD
    length = qkv.shape[1]
    rows = length // 4
    half = HEAD // 2

    @pl.when(step == 0)
    def _():
        for slab in range(4):
            start = pl.multiple_of(place[slab] * rows, rows)
            do_t[:, pl.ds(start, rows)] = dout[slab]
            prod = dout[slab].astype(jnp.float32) * out_t[slab].astype(jnp.float32)
            for h in range(heads):
                piece = slice(h * HEAD, (h + 1) * HEAD)
                delta[h : h + 1, pl.ds(start, rows)] = jnp.sum(prod[piece], axis=0, keepdims=True)
                do_n[h, pl.ds(start, rows), :] = dout[slab, piece, :].T
        for h in range(heads):
            q_n[h] = qkv[h * HEAD : (h + 1) * HEAD, :].T
            k_n[h] = qkv[width + h * HEAD : width + (h + 1) * HEAD, :].T
            v_n[h] = qkv[2 * width + h * HEAD : 2 * width + (h + 1) * HEAD, :].T
        dk[...] = jnp.zeros_like(dk)
        dv[...] = jnp.zeros_like(dv)

    q_start = pl.multiple_of(step * BQ, BQ)
    qs = pl.ds(q_start, BQ)
    low, high = doc_bounds(q_start + lax.broadcasted_iota(jnp.int32, (1, BQ), 1), (ends[0], ends[1]), length)
    first, tiles = key_span(q_start, BQ, (ends[0], ends[1]), length, BK)

    def tile(t, carry):
        k_start = pl.multiple_of(first + t * BK, 128)
        ks = pl.ds(k_start, BK)
        pos = k_start + lax.broadcasted_iota(jnp.int32, (BK, BQ), 0)
        allowed = (pos >= low) & (pos <= high)
        new = []

        def score(h):
            piece = slice(h * HEAD, (h + 1) * HEAD)
            return (
                jnp.dot(k_n[h, ks, :], qkv[piece, qs], preferred_element_type=jnp.float32),
                jnp.dot(v_n[h, ks, :], do_t[piece, qs], preferred_element_type=jnp.float32),
            )

        nxt = score(0)
        for h in range(heads):
            s, dp = nxt
            if h + 1 < heads:
                nxt = score(h + 1)
            p = jnp.where(allowed, jnp.exp(s - lse[h : h + 1, qs]), 0.0)
            ds = (p * (dp - delta[h : h + 1, qs])).astype(jnp.bfloat16)
            dv[h, ks, :] += jnp.dot(p.astype(jnp.bfloat16), do_n[h, qs, :], preferred_element_type=jnp.float32)
            dk[h, ks, :] += jnp.dot(ds, q_n[h, qs, :], preferred_element_type=jnp.float32)
            new.append(carry[h] + jnp.dot(qkv[width + h * HEAD : width + (h + 1) * HEAD, ks], ds, preferred_element_type=jnp.float32))
        return tuple(new)

    init = tuple(jnp.zeros((HEAD, BQ), jnp.float32) for _ in range(heads))
    done = lax.fori_loop(0, tiles, tile, init)
    for h in range(heads):
        dq_t[h * HEAD : (h + 1) * HEAD, qs] = done[h]

    @pl.when(step == pl.num_programs(0) - 1)
    def _():
        for slab in range(4):
            start = pl.multiple_of(place[slab] * rows, rows)
            c, s = cos[:, pl.ds(start, rows)], sin[:, pl.ds(start, rows)]
            for h in range(heads):
                gq = dq_t[h * HEAD : (h + 1) * HEAD, pl.ds(start, rows)] * HEAD**-0.5
                gk = dk[h, pl.ds(start, rows), :].T
                gv = dv[h, pl.ds(start, rows), :].T
                for kind, g in ((0, gq), (1, gk)):
                    g1, g2 = g[:half], g[half:]
                    at = kind * width + h * HEAD
                    dproj[slab, at : at + half, :] = (g1 * c + g2 * s).astype(jnp.bfloat16)
                    dproj[slab, at + half : at + HEAD, :] = (g2 * c - g1 * s).astype(jnp.bfloat16)
                at = 2 * width + h * HEAD
                dproj[slab, at : at + HEAD, :] = gv.astype(jnp.bfloat16)


def attn_bwd(place, ends, qkv, dout, out_t, lse, cos, sin):
    length = qkv.shape[1]
    rows = length // 4
    width = qkv.shape[0] // 3
    heads = width // HEAD
    smem = pl.BlockSpec(memory_space=pltpu.SMEM)
    ops = (qkv, dout, out_t, lse, cos, sin)
    natural = pltpu.VMEM((heads, length, HEAD), jnp.bfloat16)
    sums = pltpu.VMEM((heads, length, HEAD), jnp.float32)
    return pl.pallas_call(
        functools.partial(attn_bwd_kernel, heads=heads),
        grid=(length // BQ,),
        in_specs=[smem, smem] + [whole_spec(a) for a in ops],
        out_specs=pl.BlockSpec((4, 3 * width, rows), lambda i: (0, 0, 0)),
        out_shape=jax.ShapeDtypeStruct((4, 3 * width, rows), jnp.bfloat16),
        scratch_shapes=[natural, natural, natural, pltpu.VMEM((width, length), jnp.bfloat16), natural]
        + [pltpu.VMEM((heads, length), jnp.float32), pltpu.VMEM((width, length), jnp.float32), sums, sums],
        compiler_params=pltpu.CompilerParams(vmem_limit_bytes=56 << 20),
        cost_estimate=pl.CostEstimate(
            flops=10 * length * length * width, bytes_accessed=24 * length * width, transcendentals=heads * length * length
        ),
        name="attn_bwd",
    )(place, ends, *ops)


FT = 768


def ffn_specs(rows, deep, hidden, step_tiles):
    first = pl.BlockSpec((3, deep, FT), lambda b, j: (0, 0, jnp.where(b == 0, j, step_tiles - 1)))
    second = pl.BlockSpec((3, deep, FT), lambda b, j: (0, 0, jnp.where(b == 0, 0, j)))
    acts = pl.BlockSpec((1, rows, FT), lambda b, j: (b, 0, j))
    whole = pl.BlockSpec((rows, deep), lambda b, j: (0, 0))
    return first, second, acts, whole


NT = (((1,), (1,)), ((), ()))


def ffn_fwd_kernel(rows_ref, first, second, out, gate_out, up_out, total):
    b, j = pl.program_id(0), pl.program_id(1)

    def work(block, fresh):
        h = rows_ref[...]
        gate = jnp.dot(h, block[0], preferred_element_type=jnp.float32)
        up = jnp.dot(h, block[1], preferred_element_type=jnp.float32)
        gate_out[0] = gate.astype(jnp.bfloat16)
        up_out[0] = up.astype(jnp.bfloat16)
        inner = (gate / (1.0 + jnp.exp(-gate)) * up).astype(jnp.bfloat16)
        part = lax.dot_general(inner, block[2], NT, preferred_element_type=jnp.float32)
        total[...] = part if fresh else total[...] + part

    pl.when((b == 0) & (j == 0))(lambda: work(first, True))
    pl.when((b == 0) & (j > 0))(lambda: work(first, False))
    pl.when(b == 1)(lambda: work(second, False))

    @pl.when((b == 1) & (j == pl.num_programs(1) - 1))
    def _():
        out[...] = total[...].astype(out.dtype)


def ffn_fwd(rows, first, second, out_type):
    length, deep = rows.shape
    hidden = first.shape[2]
    tiles = hidden // FT
    w1, w2, acts, whole = ffn_specs(length, deep, hidden, tiles)
    act = jax.ShapeDtypeStruct((2, length, hidden), jnp.bfloat16)
    return pl.pallas_call(
        ffn_fwd_kernel,
        grid=(2, tiles),
        in_specs=[whole, w1, w2],
        out_specs=(whole, acts, acts),
        out_shape=(jax.ShapeDtypeStruct((length, deep), out_type), act, act),
        scratch_shapes=[pltpu.VMEM((length, deep), jnp.float32)],
        compiler_params=pltpu.CompilerParams(vmem_limit_bytes=40 << 20),
        cost_estimate=pl.CostEstimate(
            flops=12 * length * deep * hidden, bytes_accessed=12 * deep * hidden + 8 * length * hidden, transcendentals=2 * length * hidden
        ),
        name="ffn_fwd",
    )(rows, first, second)


def ffn_bwd_kernel(grad_ref, gate_ref, up_ref, first, second, out, grad_gate_out, grad_up_out, inner_out, total):
    b, j = pl.program_id(0), pl.program_id(1)

    def work(block, fresh):
        grad_inner = jnp.dot(grad_ref[...], block[2], preferred_element_type=jnp.float32)
        gate, up = gate_ref[0].astype(jnp.float32), up_ref[0].astype(jnp.float32)
        sig = 1.0 / (1.0 + jnp.exp(-gate))
        act = gate * sig
        grad_gate = (grad_inner * up * (sig + act * (1.0 - sig))).astype(jnp.bfloat16)
        grad_up = (grad_inner * act).astype(jnp.bfloat16)
        grad_gate_out[0] = grad_gate
        grad_up_out[0] = grad_up
        inner_out[0] = (act * up).astype(jnp.bfloat16)
        part = lax.dot_general(grad_gate, block[0], NT, preferred_element_type=jnp.float32)
        part += lax.dot_general(grad_up, block[1], NT, preferred_element_type=jnp.float32)
        total[...] = part if fresh else total[...] + part

    pl.when((b == 0) & (j == 0))(lambda: work(first, True))
    pl.when((b == 0) & (j > 0))(lambda: work(first, False))
    pl.when(b == 1)(lambda: work(second, False))

    @pl.when((b == 1) & (j == pl.num_programs(1) - 1))
    def _():
        out[...] = total[...].astype(out.dtype)


def ffn_bwd(grad, gate, up, first, second, out_type):
    length, deep = grad.shape
    hidden = first.shape[2]
    tiles = hidden // FT
    w1, w2, acts, whole = ffn_specs(length, deep, hidden, tiles)
    act = jax.ShapeDtypeStruct((2, length, hidden), jnp.bfloat16)
    return pl.pallas_call(
        ffn_bwd_kernel,
        grid=(2, tiles),
        in_specs=[whole, acts, acts, w1, w2],
        out_specs=(whole, acts, acts, acts),
        out_shape=(jax.ShapeDtypeStruct((length, deep), out_type), act, act, act),
        scratch_shapes=[pltpu.VMEM((length, deep), jnp.float32)],
        compiler_params=pltpu.CompilerParams(vmem_limit_bytes=40 << 20),
        cost_estimate=pl.CostEstimate(
            flops=12 * length * deep * hidden, bytes_accessed=12 * deep * hidden + 20 * length * hidden, transcendentals=2 * length * hidden
        ),
        name="ffn_bwd",
    )(grad, gate, up, first, second)


def ffn_grads_kernel(h0, h1, g0, g1, gate0, gate1, up0, up1, in0, in1, *rest, slot):
    *other, out, h_t, g_t = rest

    @pl.when(pl.program_id(0) == 0)
    def _():
        rows = h0.shape[0]
        h_t[:, :rows] = h0[...].T
        h_t[:, rows:] = h1[...].T
        g_t[:, :rows] = g0[...].T
        g_t[:, rows:] = g1[...].T

    for i, (left, a, b) in enumerate(((h_t, gate0, gate1), (h_t, up0, up1), (g_t, in0, in1))):
        both = jnp.concatenate([a[0], b[0]], axis=0)
        grad = jnp.dot(left[...], both, preferred_element_type=jnp.float32)
        if other:
            grad += other[0][i].astype(jnp.float32)
        out[i] = grad.astype(jnp.bfloat16)


def ffn_grads(slot, rows, grads, gates, ups, inners, *other):
    length, deep = rows[0].shape
    hidden = gates[0].shape[2]
    whole = pl.BlockSpec((length, deep), lambda j: (0, 0))
    acts = pl.BlockSpec((1, length, FT), lambda j: (slot, 0, j))
    weights = pl.BlockSpec((3, deep, FT), lambda j: (0, 0, j))
    both = pltpu.VMEM((deep, 2 * length), jnp.bfloat16)
    return pl.pallas_call(
        functools.partial(ffn_grads_kernel, slot=slot),
        grid=(hidden // FT,),
        in_specs=[whole] * 4 + [acts] * 6 + [weights] * len(other),
        out_specs=weights,
        out_shape=jax.ShapeDtypeStruct((3, deep, hidden), jnp.bfloat16),
        scratch_shapes=[both, both],
        compiler_params=pltpu.CompilerParams(vmem_limit_bytes=40 << 20),
        cost_estimate=pl.CostEstimate(
            flops=12 * length * deep * hidden, bytes_accessed=6 * deep * hidden + 12 * length * hidden, transcendentals=0
        ),
        name="ffn_grads",
    )(*rows, *grads, *gates, *ups, *inners, *other)


def proj_bwd_kernel(pair_grad, rest_grad, near, far, matrix, out_grad, pair, rest, grad, a_t, total):
    step = pl.program_id(0)
    width3 = total.shape[0]

    @pl.when(step == 0)
    def _():
        a_t[...] = matrix[:, :width3].T
        total[...] = jnp.zeros_like(total)

    def work(made, rows, out):
        total[...] += jnp.dot(made, rows, preferred_element_type=jnp.float32)
        out[0] = jnp.dot(made.T, a_t[...], preferred_element_type=jnp.float32).astype(jnp.bfloat16)

    pl.when(step == 0)(lambda: work(pair_grad[0], far[...], pair))
    pl.when(step == 1)(lambda: work(pair_grad[0], near[...], pair))
    pl.when(step == 2)(lambda: work(rest_grad[0], far[...], rest))
    pl.when(step == 3)(lambda: work(rest_grad[0], near[...], rest))

    @pl.when(step == 3)
    def _():
        grad[...] = jnp.concatenate([total[...], out_grad[...]], axis=0).astype(jnp.bfloat16).T


def proj_bwd(grad_proj, near, far, matrix, out_grad):
    slabs, width3, rows = grad_proj.shape
    features = matrix.shape[0]
    parts = jax.ShapeDtypeStruct((2, rows, features), jnp.bfloat16)
    return pl.pallas_call(
        proj_bwd_kernel,
        grid=(4,),
        in_specs=[
            pl.BlockSpec((1, width3, rows), lambda i: (jnp.where(i == 0, 3, 1), 0, 0)),
            pl.BlockSpec((1, width3, rows), lambda i: (jnp.where(i == 3, 0, 2), 0, 0)),
            pl.BlockSpec((rows, features), lambda i: (jnp.where(i == 3, 0, 1), 0)),
            pl.BlockSpec((rows, features), lambda i: (jnp.where(i == 0, 1, 0), 0)),
            pl.BlockSpec(matrix.shape, lambda i: (0, 0)),
            pl.BlockSpec(out_grad.shape, lambda i: (0, 0)),
        ],
        out_specs=(
            pl.BlockSpec((1, rows, features), lambda i: (jnp.minimum(i, 1), 0, 0)),
            pl.BlockSpec((1, rows, features), lambda i: (jnp.maximum(i - 2, 0), 0, 0)),
            pl.BlockSpec(matrix.shape, lambda i: (0, 0)),
        ),
        out_shape=(parts, parts, jax.ShapeDtypeStruct(matrix.shape, jnp.bfloat16)),
        scratch_shapes=[pltpu.VMEM((width3, features), jnp.bfloat16), pltpu.VMEM((width3, features), jnp.float32)],
        compiler_params=pltpu.CompilerParams(vmem_limit_bytes=40 << 20),
        cost_estimate=pl.CostEstimate(
            flops=16 * rows * features * width3, bytes_accessed=24 * rows * features, transcendentals=0
        ),
        name="proj_bwd",
    )(grad_proj, grad_proj, near, far, matrix, out_grad)


def mean_of(v):
    return jnp.mean(v, axis=-1, keepdims=True)


def mix_fwd_kernel(head0, head1, head2, head3, matrix, out1, out2, out3, rows, params, hidden, low, normed, inv, *, width):
    heads = jnp.concatenate([head0[...], head1[...], head2[...], head3[...]], axis=0).T
    weights = jnp.concatenate([matrix[:, 3 * width :], out1[...], out2[...], out3[...]], axis=1)
    mixed = rows[...].astype(jnp.float32) + lax.dot_general(heads, weights, NT, preferred_element_type=jnp.float32)
    centred = mixed - mean_of(mixed)
    inv_std = lax.rsqrt(mean_of(centred * centred) + NORM_EPS)
    unit = centred * inv_std
    out = unit * params[0:1, :] + params[1:2, :]
    hidden[...] = out
    low[...] = out.astype(jnp.bfloat16)
    normed[...] = unit
    inv[...] = inv_std


def mix_fwd(heads, matrix, outs, near, params):
    width, rows = heads[0].shape
    features = matrix.shape[0]
    whole = lambda a: pl.BlockSpec(a.shape, lambda i: (0,) * len(a.shape))
    block = pl.BlockSpec((rows, features), lambda i: (0, 0))
    shape = lambda t: jax.ShapeDtypeStruct((rows, features), t)
    return pl.pallas_call(
        functools.partial(mix_fwd_kernel, width=width),
        grid=(1,),
        in_specs=[whole(a) for a in (*heads, matrix, *outs)] + [block, whole(params)],
        out_specs=(block, block, block, pl.BlockSpec((rows, 1), lambda i: (0, 0))),
        out_shape=(shape(jnp.float32), shape(jnp.bfloat16), shape(jnp.float32), jax.ShapeDtypeStruct((rows, 1), jnp.float32)),
        compiler_params=pltpu.CompilerParams(vmem_limit_bytes=40 << 20),
        cost_estimate=pl.CostEstimate(
            flops=2 * rows * features * features, bytes_accessed=14 * rows * features + 2 * features * features, transcendentals=rows
        ),
        name="mix_fwd",
    )(*heads, matrix, *outs, near, params)


def mix_bwd_kernel(
    grad_mixed, own_part, far_part, normed, inv, params, head0, head1, head2, head3, matrix, out1, out2, out3,
    grad_out, norms, made0, made1, made2, made3, og0, og1, og2, og3, *, width,
):
    grad = grad_mixed[...] + own_part[...] + far_part[...].astype(jnp.float32)
    unit = normed[...]
    norms[0:1, :] = jnp.sum(grad * unit, axis=0, keepdims=True)
    norms[1:2, :] = jnp.sum(grad, axis=0, keepdims=True)
    grad_unit = grad * params[0:1, :]
    back = inv[...] * (grad_unit - mean_of(grad_unit) - unit * mean_of(grad_unit * unit))
    grad_out[...] = back
    low = back.astype(jnp.bfloat16)
    weights = (matrix[:, 3 * width :], out1[...], out2[...], out3[...])
    for weight, head, made, og in zip(weights, (head0, head1, head2, head3), (made0, made1, made2, made3), (og0, og1, og2, og3)):
        made[...] = lax.dot_general(weight.T, low, NT, preferred_element_type=jnp.float32).astype(jnp.bfloat16)
        og[...] = jnp.dot(head[...], low, preferred_element_type=jnp.float32).astype(jnp.bfloat16)


def mix_bwd(grad_mixed, own_part, far_part, normed, inv, params, heads, matrix, outs):
    width, rows = heads[0].shape
    features = matrix.shape[0]
    whole = lambda a: pl.BlockSpec(a.shape, lambda i: (0,) * len(a.shape))
    shapes = (
        [jax.ShapeDtypeStruct((rows, features), jnp.float32), jax.ShapeDtypeStruct((2, features), jnp.float32)]
        + [jax.ShapeDtypeStruct((width, rows), jnp.bfloat16)] * 4
        + [jax.ShapeDtypeStruct((width, features), jnp.bfloat16)] * 4
    )
    ops = (grad_mixed, own_part, far_part, normed, inv, params, *heads, matrix, *outs)
    got = pl.pallas_call(
        functools.partial(mix_bwd_kernel, width=width),
        grid=(1,),
        in_specs=[whole(a) for a in ops],
        out_specs=tuple(whole(a) for a in shapes),
        out_shape=tuple(shapes),
        compiler_params=pltpu.CompilerParams(vmem_limit_bytes=40 << 20),
        cost_estimate=pl.CostEstimate(
            flops=4 * rows * features * features, bytes_accessed=22 * rows * features + 4 * features * features, transcendentals=0
        ),
        name="mix_bwd",
    )(*ops)
    return got[0], got[1], got[2:6], got[6:10]


def lamb_step(weight, gradient, first_old, second):
    first_new = BETA_ONE * first_old + (1.0 - BETA_ONE) * gradient
    second_new = BETA_TWO * second + (1.0 - BETA_TWO) * gradient * gradient
    update = (
        first_new
        / (1.0 - BETA_ONE**STEP)
        / (jnp.sqrt(second_new / (1.0 - BETA_TWO**STEP)) + ADAM_EPS)
        + DECAY_RATE * weight
    )
    return first_new, second_new, update


def lamb_kernel(same, other, *refs, kinds):
    count = len(kinds)
    olds, news, late = refs[: 3 * count], refs[3 * count : 6 * count], refs[6 * count]
    late[...] = jnp.zeros_like(late)
    for i, (turned, parts) in enumerate(kinds):
        weight, first, second = olds[3 * i : 3 * i + 3]
        first_out, second_out, update_out = news[3 * i : 3 * i + 3]
        row = None
        for at, (index, columns) in enumerate(parts):
            gradient = same[index, :, columns].astype(jnp.float32) + other[index, :, columns].astype(jnp.float32)
            gradient = gradient.T if turned else gradient
            where = (at,) if len(weight.shape) == 3 else (slice(None),)
            first_new, second_new, update = lamb_step(weight[where], gradient, first[where], second[where])
            first_out[where] = first_new
            second_out[where] = second_new
            update_out[where] = update
            sums = jnp.sum(update * update, axis=0, keepdims=True)
            row = sums if row is None else row + sums
        late[i : i + 1, : row.shape[1]] = row


def lamb(same, other, kinds, olds, features):
    whole = lambda a: pl.BlockSpec(a.shape, lambda i: (0,) * len(a.shape))
    shapes = [jax.ShapeDtypeStruct(a.shape, jnp.float32) for a in olds]
    shapes.append(jax.ShapeDtypeStruct((len(kinds), features), jnp.float32))
    ops = (same, other, *olds)
    return pl.pallas_call(
        functools.partial(lamb_kernel, kinds=kinds),
        grid=(1,),
        in_specs=[whole(a) for a in ops],
        out_specs=tuple(whole(a) for a in shapes),
        out_shape=tuple(shapes),
        compiler_params=pltpu.CompilerParams(vmem_limit_bytes=48 << 20),
        cost_estimate=pl.CostEstimate(flops=20 * same.size, bytes_accessed=28 * same.size, transcendentals=same.size),
        name="lamb",
    )(*ops)


def finish_kernel(totals, now, first, second, *refs, count):
    weights, updates = refs[:count], refs[count : 2 * count]
    norm_out, first_out, second_out, trust = refs[2 * count : 2 * count + 4]
    news = refs[2 * count + 4 :]
    first_new, second_new, update = lamb_step(now[...], totals[0:4, :], first[...], second[...])
    norms = [jnp.sqrt(jnp.sum(v * v, axis=-1, keepdims=True)) for v in (now[...], update)]
    norm_out[...] = now[...] - LEARN_RATE * (norms[0] / norms[1]) * update
    first_out[...] = first_new
    second_out[...] = second_new
    sizes = jnp.sqrt(jnp.sum(totals[4:12, :], axis=-1, keepdims=True))
    trust[...] = jnp.concatenate([sizes[0:4], sizes[4:8]], axis=1)
    for i in range(count):
        ratio = LEARN_RATE * (sizes[i : i + 1] / sizes[4 + i : 5 + i])
        for at in range(weights[i].shape[0]) if len(weights[i].shape) == 3 else (slice(None),):
            news[i][at] = weights[i][at] - ratio * updates[i][at]


def finish(totals, now, first, second, weights, updates):
    whole = lambda a: pl.BlockSpec(a.shape, lambda i: (0,) * len(a.shape))
    shapes = [jax.ShapeDtypeStruct(now.shape, jnp.float32)] * 3 + [jax.ShapeDtypeStruct((4, 2), jnp.float32)]
    shapes += [jax.ShapeDtypeStruct(a.shape, jnp.float32) for a in weights]
    ops = (totals, now, first, second, *weights, *updates)
    size = sum(a.size for a in weights)
    return pl.pallas_call(
        functools.partial(finish_kernel, count=len(weights)),
        grid=(1,),
        in_specs=[whole(a) for a in ops],
        out_specs=tuple(whole(a) for a in shapes),
        out_shape=tuple(shapes),
        compiler_params=pltpu.CompilerParams(vmem_limit_bytes=48 << 20),
        cost_estimate=pl.CostEstimate(flops=3 * size, bytes_accessed=12 * size, transcendentals=0),
        name="finish",
    )(*ops)


STEP = 10

BETA_ONE = 0.9
BETA_TWO = 0.999
ADAM_EPS = 1e-06
DECAY_RATE = 0.01
LEARN_RATE = 0.2
NORM_EPS = 1e-05
ROPE_BASE = 1000.0

bf16 = jnp.bfloat16
f32 = jnp.float32

BOTH = ("section", "tensor")
CELLS = [(c, y, x) for c in range(2) for y in range(2) for x in range(2)]


def number(c, y, x):
    return c * 4 + y * 2 + x


def moves(target):
    return [(number(*cell), number(*target(*cell))) for cell in CELLS]


SWAP = moves(lambda c, y, x: (y, c, x))
SWAP_BACK = moves(lambda c, y, x: (1 - y, c, x))
SWAP_OUT = moves(lambda c, y, x: (y, 1 - c, x))
CORNER = moves(lambda c, y, x: (1 - c, y, 1 - x))


def over_section(v):
    return lax.ppermute(v, "section", [(0, 1), (1, 0)])


def over_x(v):
    return lax.ppermute(v, "tensor", [(0, 1), (1, 0), (2, 3), (3, 2)])


def over_y(v):
    return lax.ppermute(v, "tensor", [(0, 2), (1, 3), (2, 0), (3, 1)])


def over_diag(v):
    return lax.ppermute(v, "tensor", [(0, 3), (1, 2), (2, 1), (3, 0)])


def over_both(v, pairs):
    return lax.ppermute(v, BOTH, pairs)


def over_z(v, k):
    return lax.ppermute(v, "dp", [(i, i ^ k) for i in range(4)])


def quad():
    return lax.axis_size("dp") == 4


def gather_later(piece, axis):
    return lax.all_gather(piece, "dp", axis=axis, tiled=True)


def scatter_later(whole, axis):
    return lax.psum_scatter(whole, "dp", scatter_dimension=axis, tiled=True)


def chips_total(v):
    v = (v + over_x(v)) + (over_y(v) + over_diag(v))
    if not quad():
        return lax.psum(v, "dp")
    return (v + over_z(v, 1)) + (over_z(v, 2) + over_z(v, 3))


def rope_tables(length):
    half_size = HEAD // 2
    freq_vals = np.float32(ROPE_BASE) ** (-np.arange(half_size, dtype=np.float32) * np.float32(2.0 / HEAD))
    angles = freq_vals[:, None] * np.arange(length, dtype=np.float32)[None, :]
    return jnp.asarray(np.cos(angles)), jnp.asarray(np.sin(angles))


def norm_fwd(values, gain_row, bias_row):
    mean_val = jnp.mean(values, axis=-1, keepdims=True)
    centred = values - mean_val
    variance = jnp.mean(centred * centred, axis=-1, keepdims=True)
    inv_std = lax.rsqrt(variance + NORM_EPS)
    normed = centred * inv_std
    return (normed * gain_row + bias_row, normed, inv_std)


def norm_back(grad_out, normed, inv_std, gain_row):
    grad_gain = jnp.sum(grad_out * normed, axis=0)
    grad_bias = jnp.sum(grad_out, axis=0)
    grad_normed = grad_out * gain_row
    grad_vals = inv_std * (
        grad_normed
        - jnp.mean(grad_normed, axis=-1, keepdims=True)
        - normed * jnp.mean(grad_normed * normed, axis=-1, keepdims=True)
    )
    return (grad_vals, grad_gain, grad_bias)


def dot(spec, a, b):
    return jnp.einsum(spec, a, b, preferred_element_type=f32)


def after(value, *others):
    return lax.optimization_barrier((value,) + others)[0]


def layer_forward(near, far, matrix, ffn, params, env):
    place, ends, cos, sin = env
    mine, log_sums, qkv = attn_fwd(place, ends, near, far, matrix, cos, sin)
    out_own = matrix[:, 3 * (matrix.shape[1] // 4) :]
    out_across = over_x(out_own)
    outs = (over_section(out_own), out_across, over_section(after(out_across, log_sums)))
    all_heads = [mine[0], over_section(mine[1]), over_x(mine[2]), over_both(mine[3], CORNER)]
    hidden, hidden_low, normed_one, inv_one = mix_fwd(all_heads, matrix, outs, near, params[:, 0])
    ffn = (ffn, over_section(after(ffn, hidden_low)))
    hidden_rows = [hidden_low, over_x(hidden_low)]
    own_part, *own_acts = ffn_fwd(hidden_rows[0], *ffn, f32)
    far_part, *far_acts = ffn_fwd(hidden_rows[1], *ffn, bf16)
    ffn_out = own_part + over_x(far_part).astype(f32)
    output, normed_two, inv_two = norm_fwd(hidden + ffn_out, params[0, 1], params[1, 1])
    kept = (near, far, qkv, mine, log_sums, all_heads, normed_one, inv_one, hidden_rows, (own_acts, far_acts))
    return output.astype(bf16), outs, kept + (normed_two, inv_two, ffn)


def layer_backward(grad_out, kept, matrix, outs, params, env):
    place, ends, cos, sin = env
    (near, far, qkv, mine, log_sums, all_heads, normed_one, inv_one, hidden_rows, acts, normed_two, inv_two, ffn) = kept
    grad_mixed, gain_two, bias_two = norm_back(grad_out, normed_two, inv_two, params[0, 1])
    grad_low = grad_mixed.astype(bf16)
    grad_rows = [grad_low, over_x(grad_low)]
    own_part, *own_grads = ffn_bwd(grad_rows[0], *acts[0], *ffn, f32)
    far_part, *far_grads = ffn_bwd(grad_rows[1], *acts[1], *ffn, bf16)
    made = list(zip(own_grads, far_grads))
    ffn_other = ffn_grads(1, hidden_rows, grad_rows, *made)
    ffn_grad = ffn_grads(0, hidden_rows, grad_rows, *made, over_section(ffn_other))
    grad_mixed_one, norm_one, grad_heads, out_grad = mix_bwd(
        grad_mixed, own_part, over_x(far_part), normed_one, inv_one, params[:, 0], all_heads, matrix, outs
    )
    grad_mine = jnp.stack(
        [grad_heads[0], over_section(grad_heads[1]), over_x(grad_heads[2]), over_both(grad_heads[3], CORNER)]
    )
    out_own = [out_grad[0], over_section(out_grad[1]), over_x(out_grad[2]), over_both(out_grad[3], CORNER)]
    out_own = sum(g.astype(f32) for g in out_own)
    grad_proj = attn_bwd(place, ends, qkv, grad_mine, mine, log_sums, cos, sin)
    pair, rest, matrix_grad = proj_bwd(grad_proj, near, far, matrix, out_own)
    other = over_section(pair).astype(f32)
    far_sum = over_x((rest[0].astype(f32) + other[0]).astype(bf16))
    rows_sum = rest[1].astype(f32) + other[1] + far_sum.astype(f32)
    norm_grads = jnp.stack([jnp.stack([norm_one[0], gain_two]), jnp.stack([norm_one[1], bias_two])])
    return grad_mixed_one + rows_sum, matrix_grad, ffn_grad, norm_grads


def body(
    tokens,
    cotangent,
    segments,
    heads_in,
    heads_out,
    gate_up,
    project_down,
    norm_gain,
    norm_bias,
    heads_in_first,
    heads_in_second,
    heads_out_first,
    heads_out_second,
    gate_up_first,
    gate_up_second,
    project_down_first,
    project_down_second,
    norm_first,
    norm_second,
):
    section = lax.axis_index("section")
    spot = lax.axis_index("tensor")
    y, x = spot // 2, spot % 2
    rows = tokens.shape[1]
    length = segments.shape[-1]
    masters = (heads_in[0], heads_out[0], gate_up[0], project_down[0])
    deep, width = masters[0].shape[1:]

    attn_piece = jnp.concatenate(
        [masters[0].transpose(1, 0, 2).reshape(deep, 3 * width), masters[1].T], axis=1
    ).astype(bf16)
    ffn_piece = jnp.concatenate([masters[2], masters[3].T[None]], axis=0).astype(bf16)

    def to_block(piece, layer):
        got = []
        for to_y in range(2):
            pairs = [(number(layer, c, x), number(c, to_y, x)) for c in range(2) for x in range(2)]
            got.append(over_both(piece, pairs))
        return jnp.where(y == 0, got[0], got[1])

    own = over_both(lax.dynamic_index_in_dim(tokens, section, 0, keepdims=False), SWAP)
    first_matrix = gather_later(to_block(attn_piece, 0), 0)
    ffn_first = gather_later(to_block(after(ffn_piece, own), 0), 1)

    def four_slabs(rows):
        across = over_x(rows)
        return jnp.concatenate([rows, over_section(rows)]), jnp.concatenate([across, over_section(across)])

    both_params = jnp.stack([norm_gain[0], norm_bias[0]])
    other_params = over_section(both_params)
    params = [
        jnp.where(section == 0, both_params, other_params),
        jnp.where(section == 0, other_params, both_params),
    ]

    block = 2 * section + x
    place = jnp.stack([block, block ^ 2, block ^ 1, block ^ 3]).astype(jnp.int32)
    seq_seg = lax.dynamic_index_in_dim(segments, y, 0, keepdims=False)[0]
    ends = jnp.stack([jnp.sum((seq_seg <= d).astype(jnp.int32)) for d in range(2)])
    env = (place, ends) + rope_tables(length)

    near_zero, far_zero = four_slabs(own)
    low_zero, outs_zero, kept_zero = layer_forward(near_zero, far_zero, first_matrix, ffn_first, params[0], env)
    hidden_rows = kept_zero[8]
    second_piece = to_block(after(jnp.concatenate([attn_piece[None], ffn_piece]), ffn_first), 1)
    second_matrix = gather_later(after(second_piece[0], hidden_rows[0]), 0)
    ffn_second = gather_later(after(second_piece[1:], hidden_rows[1]), 1)
    near_one, far_one = four_slabs(low_zero)
    low_one, outs_one, kept_one = layer_forward(near_one, far_one, second_matrix, ffn_second, params[1], env)
    grad_top = over_both(after(lax.dynamic_index_in_dim(cotangent, section, 0, keepdims=False), low_zero), SWAP)
    grad_one, matrix_one, ffn_one, norm_one = layer_backward(
        grad_top.astype(f32), kept_one, second_matrix, outs_one, params[1], env
    )
    sent = grad_one.astype(bf16)
    grad_zero, matrix_zero, ffn_zero, norm_zero = layer_backward(
        sent.astype(f32), kept_zero, first_matrix, outs_zero, params[0], env
    )

    def home(zero, one):
        same = over_both(jnp.where(y == 0, zero, one), SWAP)
        other = over_both(jnp.where(y == 0, one, zero), SWAP_BACK)
        return same, other

    def by_micro(zero, one):
        same, other = home(zero, one)
        return jnp.stack([jnp.where(section == 0, same, other), jnp.where(section == 0, other, same)])

    layer_out = by_micro(low_zero, low_one)

    ffn_home = home(scatter_later(ffn_zero, 1), scatter_later(ffn_one, 1))
    attn_home = home(scatter_later(matrix_zero, 0)[None], scatter_later(matrix_one, 0)[None])
    norm_mine = jnp.where(section == 0, norm_zero, norm_one) + over_section(
        jnp.where(section == 0, norm_one, norm_zero)
    )
    features = norm_mine.shape[-1]
    firsts = (heads_in_first[0], heads_out_first[0], gate_up_first[0], project_down_first[0])
    seconds = (heads_in_second[0], heads_out_second[0], gate_up_second[0], project_down_second[0])
    olds = list(zip(masters, firsts, seconds))

    def squares(matrix):
        row = jnp.sum((matrix * matrix).reshape(-1, matrix.shape[-1]), axis=0)
        return jnp.pad(row, (0, features - row.shape[0]))

    columns = slice(0, masters[2].shape[-1])
    ffn_new = lamb(
        *ffn_home, ((False, ((0, columns), (1, columns))), (True, ((2, columns),))), olds[2] + olds[3], features
    )
    early = jnp.stack([squares(m) for m in masters])
    early = jnp.concatenate([norm_mine.reshape(4, -1), early], axis=0)
    attn_home = lax.optimization_barrier((*attn_home, early, ffn_new[-1]))[:2]
    pieces = tuple((0, slice(i * width, (i + 1) * width)) for i in range(4))
    attn_new = lamb(*attn_home, ((False, pieces[:3]), (True, pieces[3:])), olds[0] + olds[1], features)
    totals = chips_total(jnp.concatenate([early, attn_new[-1], ffn_new[-1]], axis=0))
    made = [attn_new[:3], attn_new[3:6], ffn_new[:3], ffn_new[3:6]]
    norm_shape = both_params.shape
    flat = [v.reshape(4, features) for v in (both_params, norm_first[0], norm_second[0])]
    *norms, trust_norms, in_new, out_new, gate_new, down_new = finish(
        totals, *flat, masters, [m[2] for m in made]
    )
    new_mats = (in_new, out_new, gate_new, down_new)
    input_grads = by_micro(after(grad_zero.astype(bf16), attn_new[-1]), sent).astype(f32)
    outs = [layer_out, input_grads]
    for i in range(4):
        outs += [new_mats[i], made[i][0], made[i][1]]
    outs += [v.reshape(norm_shape) for v in norms] + [trust_norms]
    return tuple(item[None] for item in outs)


def solution(mesh):
    rows = P(None, ("dp", "tensor"), None)
    out_rows = P("section", None, ("dp", "tensor"), None)
    columns = P("section", None, "dp", "tensor")
    turned = P("section", "tensor", "dp")
    vectors = P("section", None, None)
    pairs = P("section", None, None, None)
    return jax.shard_map(
        body,
        mesh=mesh,
        in_specs=(rows, rows, P(None, "dp", None), columns, turned, columns, turned, vectors, vectors)
        + (columns, columns, turned, turned, columns, columns, turned, turned, pairs, pairs),
        out_specs=(out_rows, out_rows)
        + (columns,) * 3
        + (turned,) * 3
        + (columns,) * 3
        + (turned,) * 3
        + (pairs,) * 3
        + (vectors,),
        check_vma=False,
    )
```

```python
import functools

import jax
import jax.numpy as jnp
import numpy as np
from jax import lax
from jax.experimental import pallas as pl
from jax.experimental.pallas import tpu as pltpu
from jax.sharding import PartitionSpec as P

HEAD = 64
FQ, FK = 512, 512
BQ, BK = 256, 512
SAFE = 40.0
WINDOW = 1024


def doc_bounds(pos, ends, length):
    start = jnp.where(pos < ends[0], 0, jnp.where(pos < ends[1], ends[0], ends[1]))
    last = jnp.where(pos < ends[0], ends[0], jnp.where(pos < ends[1], ends[1], length)) - 1
    return jnp.maximum(start, pos - (WINDOW - 1)), jnp.minimum(last, pos + (WINDOW - 1))


def key_span(q_start, rows, ends, length, deep):
    low, _ = doc_bounds(q_start, ends, length)
    _, high = doc_bounds(q_start + rows - 1, ends, length)
    first = low // 128 * 128
    tiles = (high + 1 - first + deep - 1) // deep
    return jnp.minimum(first, length - tiles * deep), tiles


def attn_fwd_kernel(place, ends, slab0, slab1, slab2, slab3, matrix, cos, sin, out0, out1, out2, out3, lse, qkv, a_t, k_n, o_t, calm, *, heads):
    step = pl.program_id(0)
    width = heads * HEAD
    half = HEAD // 2
    length = qkv.shape[1]
    rows = length // 4

    @pl.when(step == 0)
    def _():
        a_t[...] = matrix[:, : 3 * width].T
        tops = [jnp.zeros((1, rows), jnp.float32) for _ in range(2 * heads)]
        for slab, src in enumerate((slab0, slab1, slab2, slab3)):
            start = pl.multiple_of(place[slab] * rows, rows)
            here = pl.ds(start, rows)
            proj = lax.dot_general(a_t[...], src[...], (((1,), (1,)), ((), ())), preferred_element_type=jnp.float32)
            c, s = cos[:, here], sin[:, here]
            for i in range(2 * heads):
                first, second = proj[i * HEAD : i * HEAD + half], proj[i * HEAD + half : (i + 1) * HEAD]
                turned = jnp.concatenate([first * c - second * s, second * c + first * s], axis=0).astype(jnp.bfloat16)
                if i < heads:
                    turned = turned * jnp.bfloat16(HEAD**-0.5)
                else:
                    k_n[i - heads, here, :] = turned.T
                qkv[i * HEAD : (i + 1) * HEAD, here] = turned
                size = turned.astype(jnp.float32)
                tops[i] = jnp.maximum(tops[i], jnp.sum(size * size, axis=0, keepdims=True))
            qkv[2 * width :, here] = proj[2 * width :].astype(jnp.bfloat16)
        worst = jnp.float32(0.0)
        for h in range(heads):
            worst = jnp.maximum(worst, jnp.max(tops[h]) * jnp.max(tops[heads + h]))
        calm[0] = (worst <= SAFE * SAFE).astype(jnp.int32)

    q_start = pl.multiple_of(step * FQ, FQ)
    here = pl.ds(q_start, FQ)
    low, high = doc_bounds(q_start + lax.broadcasted_iota(jnp.int32, (1, FQ), 1), (ends[0], ends[1]), length)
    first, tiles = key_span(q_start, FQ, (ends[0], ends[1]), length, FK)

    def score(h, keys):
        return jnp.dot(k_n[h, keys, :], qkv[h * HEAD : (h + 1) * HEAD, here], preferred_element_type=jnp.float32)

    def weigh(h, keys, p):
        return jnp.dot(
            qkv[2 * width + h * HEAD : 2 * width + (h + 1) * HEAD, keys], p.astype(jnp.bfloat16),
            preferred_element_type=jnp.float32,
        )

    def mask(t):
        k_start = pl.multiple_of(first + t * FK, 128)
        pos = k_start + lax.broadcasted_iota(jnp.int32, (FK, FQ), 0)
        return pl.ds(k_start, FK), (pos >= low) & (pos <= high)

    def finish(h, total, acc, log_sum):
        o_t[h * HEAD : (h + 1) * HEAD, here] = (acc / total).astype(jnp.bfloat16)
        lse[h : h + 1, here] = log_sum

    @pl.when(calm[0] == 1)
    def _():
        def tile(t, carry):
            keys, allowed = mask(t)
            new = []
            nxt = score(0, keys)
            for h in range(heads):
                total, acc = carry[h]
                s = nxt
                if h + 1 < heads:
                    nxt = score(h + 1, keys)
                p = jnp.where(allowed, jnp.exp(s), 0.0)
                new.append((total + jnp.sum(p, axis=0, keepdims=True), acc + weigh(h, keys, p)))
            return tuple(new)

        init = tuple((jnp.zeros((1, FQ), jnp.float32), jnp.zeros((HEAD, FQ), jnp.float32)) for _ in range(heads))
        for h, (total, acc) in enumerate(lax.fori_loop(0, tiles, tile, init)):
            finish(h, total, acc, jnp.log(total))

    @pl.when(calm[0] == 0)
    def _():
        def tile(t, carry):
            keys, allowed = mask(t)
            new = []
            for h in range(heads):
                top, total, acc = carry[h]
                s = jnp.where(allowed, score(h, keys), -1e30)
                new_top = jnp.maximum(top, jnp.max(s, axis=0, keepdims=True))
                p = jnp.exp(s - new_top)
                alpha = jnp.exp(top - new_top)
                total = total * alpha + jnp.sum(p, axis=0, keepdims=True)
                new.append((new_top, total, acc * alpha + weigh(h, keys, p)))
            return tuple(new)

        init = tuple(
            (jnp.full((1, FQ), -1e30, jnp.float32), jnp.zeros((1, FQ), jnp.float32), jnp.zeros((HEAD, FQ), jnp.float32))
            for _ in range(heads)
        )
        for h, (top, total, acc) in enumerate(lax.fori_loop(0, tiles, tile, init)):
            finish(h, total, acc, top + jnp.log(total))

    @pl.when(step == pl.num_programs(0) - 1)
    def _():
        for slab, out in enumerate((out0, out1, out2, out3)):
            out[...] = o_t[:, pl.ds(pl.multiple_of(place[slab] * rows, rows), rows)]


def whole_spec(a):
    return pl.BlockSpec(a.shape, lambda i: (0,) * len(a.shape))


def attn_fwd(place, ends, slabs, matrix, cos, sin):
    rows = slabs[0].shape[0]
    length = 4 * rows
    width = matrix.shape[1] // 4
    heads = width // HEAD
    smem = pl.BlockSpec(memory_space=pltpu.SMEM)
    ops = (*slabs, matrix, cos, sin)
    outs = (
        *[jax.ShapeDtypeStruct((width, rows), jnp.bfloat16)] * 4,
        jax.ShapeDtypeStruct((heads, length), jnp.float32),
        jax.ShapeDtypeStruct((3 * width, length), jnp.bfloat16),
    )
    return pl.pallas_call(
        functools.partial(attn_fwd_kernel, heads=heads),
        grid=(length // FQ,),
        in_specs=[smem, smem] + [whole_spec(a) for a in ops],
        out_specs=tuple(whole_spec(o) for o in outs),
        out_shape=outs,
        scratch_shapes=[
            pltpu.VMEM((3 * width, matrix.shape[0]), jnp.bfloat16),
            pltpu.VMEM((heads, length, HEAD), jnp.bfloat16),
            pltpu.VMEM((width, length), jnp.bfloat16),
            pltpu.SMEM((1,), jnp.int32),
        ],
        compiler_params=pltpu.CompilerParams(vmem_limit_bytes=48 << 20),
        cost_estimate=pl.CostEstimate(
            flops=6 * length * length * width, bytes_accessed=16 * length * width, transcendentals=heads * length * length
        ),
        name="attn_fwd",
    )(place, ends, *ops)


def attn_bwd_kernel(place, ends, qkv, do0, do1, do2, do3, out0, out1, out2, out3, lse, cos, sin, dproj, q_n, k_n, v_n, do_t, do_n, delta, dq_t, dk, dv, *, heads):
    step = pl.program_id(0)
    width = heads * HEAD
    length = qkv.shape[1]
    rows = length // 4
    half = HEAD // 2

    @pl.when(step == 0)
    def _():
        for slab, (dout, out) in enumerate(((do0, out0), (do1, out1), (do2, out2), (do3, out3))):
            start = pl.multiple_of(place[slab] * rows, rows)
            do_t[:, pl.ds(start, rows)] = dout[...]
            prod = dout[...].astype(jnp.float32) * out[...].astype(jnp.float32)
            for h in range(heads):
                piece = slice(h * HEAD, (h + 1) * HEAD)
                delta[h : h + 1, pl.ds(start, rows)] = jnp.sum(prod[piece], axis=0, keepdims=True)
                do_n[h, pl.ds(start, rows), :] = dout[piece, :].T
        for h in range(heads):
            q_n[h] = qkv[h * HEAD : (h + 1) * HEAD, :].T
            k_n[h] = qkv[width + h * HEAD : width + (h + 1) * HEAD, :].T
            v_n[h] = qkv[2 * width + h * HEAD : 2 * width + (h + 1) * HEAD, :].T
        dk[...] = jnp.zeros_like(dk)
        dv[...] = jnp.zeros_like(dv)

    q_start = pl.multiple_of(step * BQ, BQ)
    qs = pl.ds(q_start, BQ)
    low, high = doc_bounds(q_start + lax.broadcasted_iota(jnp.int32, (1, BQ), 1), (ends[0], ends[1]), length)
    first, tiles = key_span(q_start, BQ, (ends[0], ends[1]), length, BK)

    def tile(t, carry):
        k_start = pl.multiple_of(first + t * BK, 128)
        ks = pl.ds(k_start, BK)
        pos = k_start + lax.broadcasted_iota(jnp.int32, (BK, BQ), 0)
        allowed = (pos >= low) & (pos <= high)
        new = []

        def score(h):
            piece = slice(h * HEAD, (h + 1) * HEAD)
            return (
                jnp.dot(k_n[h, ks, :], qkv[piece, qs], preferred_element_type=jnp.float32),
                jnp.dot(v_n[h, ks, :], do_t[piece, qs], preferred_element_type=jnp.float32),
            )

        nxt = score(0)
        for h in range(heads):
            s, dp = nxt
            if h + 1 < heads:
                nxt = score(h + 1)
            p = jnp.where(allowed, jnp.exp(s - lse[h : h + 1, qs]), 0.0)
            ds = (p * (dp - delta[h : h + 1, qs])).astype(jnp.bfloat16)
            dv[h, ks, :] += jnp.dot(p.astype(jnp.bfloat16), do_n[h, qs, :], preferred_element_type=jnp.float32)
            dk[h, ks, :] += jnp.dot(ds, q_n[h, qs, :], preferred_element_type=jnp.float32)
            new.append(carry[h] + jnp.dot(qkv[width + h * HEAD : width + (h + 1) * HEAD, ks], ds, preferred_element_type=jnp.float32))
        return tuple(new)

    init = tuple(jnp.zeros((HEAD, BQ), jnp.float32) for _ in range(heads))
    done = lax.fori_loop(0, tiles, tile, init)
    for h in range(heads):
        dq_t[h * HEAD : (h + 1) * HEAD, qs] = done[h]

    @pl.when(step == pl.num_programs(0) - 1)
    def _():
        for slab in range(4):
            start = pl.multiple_of(place[slab] * rows, rows)
            c, s = cos[:, pl.ds(start, rows)], sin[:, pl.ds(start, rows)]
            for h in range(heads):
                gq = dq_t[h * HEAD : (h + 1) * HEAD, pl.ds(start, rows)] * HEAD**-0.5
                gk = dk[h, pl.ds(start, rows), :].T
                gv = dv[h, pl.ds(start, rows), :].T
                for kind, g in ((0, gq), (1, gk)):
                    g1, g2 = g[:half], g[half:]
                    at = kind * width + h * HEAD
                    dproj[slab, at : at + half, :] = (g1 * c + g2 * s).astype(jnp.bfloat16)
                    dproj[slab, at + half : at + HEAD, :] = (g2 * c - g1 * s).astype(jnp.bfloat16)
                at = 2 * width + h * HEAD
                dproj[slab, at : at + HEAD, :] = gv.astype(jnp.bfloat16)


def attn_bwd(place, ends, qkv, douts, outs, lse, cos, sin):
    length = qkv.shape[1]
    rows = length // 4
    width = qkv.shape[0] // 3
    heads = width // HEAD
    smem = pl.BlockSpec(memory_space=pltpu.SMEM)
    ops = (qkv, *douts, *outs, lse, cos, sin)
    natural = pltpu.VMEM((heads, length, HEAD), jnp.bfloat16)
    sums = pltpu.VMEM((heads, length, HEAD), jnp.float32)
    return pl.pallas_call(
        functools.partial(attn_bwd_kernel, heads=heads),
        grid=(length // BQ,),
        in_specs=[smem, smem] + [whole_spec(a) for a in ops],
        out_specs=pl.BlockSpec((4, 3 * width, rows), lambda i: (0, 0, 0)),
        out_shape=jax.ShapeDtypeStruct((4, 3 * width, rows), jnp.bfloat16),
        scratch_shapes=[natural, natural, natural, pltpu.VMEM((width, length), jnp.bfloat16), natural]
        + [pltpu.VMEM((heads, length), jnp.float32), pltpu.VMEM((width, length), jnp.float32), sums, sums],
        compiler_params=pltpu.CompilerParams(vmem_limit_bytes=56 << 20),
        cost_estimate=pl.CostEstimate(
            flops=10 * length * length * width, bytes_accessed=24 * length * width, transcendentals=heads * length * length
        ),
        name="attn_bwd",
    )(place, ends, *ops)


FT = 768


def ffn_specs(rows, deep, hidden, step_tiles):
    first = pl.BlockSpec((3, deep, FT), lambda b, j: (0, 0, jnp.where(b == 0, j, step_tiles - 1)))
    second = pl.BlockSpec((3, deep, FT), lambda b, j: (0, 0, jnp.where(b == 0, 0, j)))
    acts = pl.BlockSpec((1, rows, FT), lambda b, j: (b, 0, j))
    whole = pl.BlockSpec((rows, deep), lambda b, j: (0, 0))
    return first, second, acts, whole


NT = (((1,), (1,)), ((), ()))


def ffn_fwd_kernel(rows_ref, first, second, out, gate_out, up_out, total):
    b, j = pl.program_id(0), pl.program_id(1)

    def work(block, fresh):
        h = rows_ref[...]
        gate = jnp.dot(h, block[0], preferred_element_type=jnp.float32)
        up = jnp.dot(h, block[1], preferred_element_type=jnp.float32)
        gate_out[0] = gate.astype(jnp.bfloat16)
        up_out[0] = up.astype(jnp.bfloat16)
        inner = (gate / (1.0 + jnp.exp(-gate)) * up).astype(jnp.bfloat16)
        part = lax.dot_general(inner, block[2], NT, preferred_element_type=jnp.float32)
        total[...] = part if fresh else total[...] + part

    pl.when((b == 0) & (j == 0))(lambda: work(first, True))
    pl.when((b == 0) & (j > 0))(lambda: work(first, False))
    pl.when(b == 1)(lambda: work(second, False))

    @pl.when((b == 1) & (j == pl.num_programs(1) - 1))
    def _():
        out[...] = total[...].astype(out.dtype)


def ffn_fwd(rows, first, second, out_type):
    length, deep = rows.shape
    hidden = first.shape[2]
    tiles = hidden // FT
    w1, w2, acts, whole = ffn_specs(length, deep, hidden, tiles)
    act = jax.ShapeDtypeStruct((2, length, hidden), jnp.bfloat16)
    return pl.pallas_call(
        ffn_fwd_kernel,
        grid=(2, tiles),
        in_specs=[whole, w1, w2],
        out_specs=(whole, acts, acts),
        out_shape=(jax.ShapeDtypeStruct((length, deep), out_type), act, act),
        scratch_shapes=[pltpu.VMEM((length, deep), jnp.float32)],
        compiler_params=pltpu.CompilerParams(vmem_limit_bytes=40 << 20),
        cost_estimate=pl.CostEstimate(
            flops=12 * length * deep * hidden, bytes_accessed=12 * deep * hidden + 8 * length * hidden, transcendentals=2 * length * hidden
        ),
        name="ffn_fwd",
    )(rows, first, second)


def ffn_bwd_kernel(grad_ref, gate_ref, up_ref, first, second, out, grad_gate_out, grad_up_out, inner_out, total):
    b, j = pl.program_id(0), pl.program_id(1)

    def work(block, fresh):
        grad_inner = jnp.dot(grad_ref[...], block[2], preferred_element_type=jnp.float32)
        gate, up = gate_ref[0].astype(jnp.float32), up_ref[0].astype(jnp.float32)
        sig = 1.0 / (1.0 + jnp.exp(-gate))
        act = gate * sig
        grad_gate = (grad_inner * up * (sig + act * (1.0 - sig))).astype(jnp.bfloat16)
        grad_up = (grad_inner * act).astype(jnp.bfloat16)
        grad_gate_out[0] = grad_gate
        grad_up_out[0] = grad_up
        inner_out[0] = (act * up).astype(jnp.bfloat16)
        part = lax.dot_general(grad_gate, block[0], NT, preferred_element_type=jnp.float32)
        part += lax.dot_general(grad_up, block[1], NT, preferred_element_type=jnp.float32)
        total[...] = part if fresh else total[...] + part

    pl.when((b == 0) & (j == 0))(lambda: work(first, True))
    pl.when((b == 0) & (j > 0))(lambda: work(first, False))
    pl.when(b == 1)(lambda: work(second, False))

    @pl.when((b == 1) & (j == pl.num_programs(1) - 1))
    def _():
        out[...] = total[...].astype(out.dtype)


def ffn_bwd(grad, gate, up, first, second, out_type):
    length, deep = grad.shape
    hidden = first.shape[2]
    tiles = hidden // FT
    w1, w2, acts, whole = ffn_specs(length, deep, hidden, tiles)
    act = jax.ShapeDtypeStruct((2, length, hidden), jnp.bfloat16)
    return pl.pallas_call(
        ffn_bwd_kernel,
        grid=(2, tiles),
        in_specs=[whole, acts, acts, w1, w2],
        out_specs=(whole, acts, acts, acts),
        out_shape=(jax.ShapeDtypeStruct((length, deep), out_type), act, act, act),
        scratch_shapes=[pltpu.VMEM((length, deep), jnp.float32)],
        compiler_params=pltpu.CompilerParams(vmem_limit_bytes=40 << 20),
        cost_estimate=pl.CostEstimate(
            flops=12 * length * deep * hidden, bytes_accessed=12 * deep * hidden + 20 * length * hidden, transcendentals=2 * length * hidden
        ),
        name="ffn_bwd",
    )(grad, gate, up, first, second)


def ffn_grads_kernel(h0, h1, g0, g1, gate0, gate1, up0, up1, in0, in1, *rest, slot):
    *other, out, h_t, g_t = rest

    @pl.when(pl.program_id(0) == 0)
    def _():
        rows = h0.shape[0]
        h_t[:, :rows] = h0[...].T
        h_t[:, rows:] = h1[...].T
        g_t[:, :rows] = g0[...].T
        g_t[:, rows:] = g1[...].T

    for i, (left, a, b) in enumerate(((h_t, gate0, gate1), (h_t, up0, up1), (g_t, in0, in1))):
        both = jnp.concatenate([a[0], b[0]], axis=0)
        grad = jnp.dot(left[...], both, preferred_element_type=jnp.float32)
        if other:
            grad += other[0][i].astype(jnp.float32)
        out[i] = grad.astype(jnp.bfloat16)


def ffn_grads(slot, rows, grads, gates, ups, inners, *other):
    length, deep = rows[0].shape
    hidden = gates[0].shape[2]
    whole = pl.BlockSpec((length, deep), lambda j: (0, 0))
    acts = pl.BlockSpec((1, length, FT), lambda j: (slot, 0, j))
    weights = pl.BlockSpec((3, deep, FT), lambda j: (0, 0, j))
    both = pltpu.VMEM((deep, 2 * length), jnp.bfloat16)
    return pl.pallas_call(
        functools.partial(ffn_grads_kernel, slot=slot),
        grid=(hidden // FT,),
        in_specs=[whole] * 4 + [acts] * 6 + [weights] * len(other),
        out_specs=weights,
        out_shape=jax.ShapeDtypeStruct((3, deep, hidden), jnp.bfloat16),
        scratch_shapes=[both, both],
        compiler_params=pltpu.CompilerParams(vmem_limit_bytes=40 << 20),
        cost_estimate=pl.CostEstimate(
            flops=12 * length * deep * hidden, bytes_accessed=6 * deep * hidden + 12 * length * hidden, transcendentals=0
        ),
        name="ffn_grads",
    )(*rows, *grads, *gates, *ups, *inners, *other)


def proj_bwd_kernel(pair_grad, rest_grad, slab0, slab1, slab2, slab3, matrix, out_grad, made3, made1, made2, made0, grad, a_t, total):
    step = pl.program_id(0)
    width3 = total.shape[0]

    @pl.when(step == 0)
    def _():
        a_t[...] = matrix[:, :width3].T
        total[...] = jnp.zeros_like(total)

    def work(made, rows, out):
        total[...] += jnp.dot(made, rows, preferred_element_type=jnp.float32)
        out[...] = jnp.dot(made.T, a_t[...], preferred_element_type=jnp.float32).astype(jnp.bfloat16)

    pl.when(step == 0)(lambda: work(pair_grad[0], slab3[...], made3))
    pl.when(step == 1)(lambda: work(pair_grad[0], slab1[...], made1))
    pl.when(step == 2)(lambda: work(rest_grad[0], slab2[...], made2))
    pl.when(step == 3)(lambda: work(rest_grad[0], slab0[...], made0))

    @pl.when(step == 3)
    def _():
        grad[...] = jnp.concatenate([total[...], out_grad[...]], axis=0).astype(jnp.bfloat16).T


def proj_bwd(grad_proj, slabs, matrix, out_grad):
    _, width3, rows = grad_proj.shape
    features = matrix.shape[0]
    part = jax.ShapeDtypeStruct((rows, features), jnp.bfloat16)
    return pl.pallas_call(
        proj_bwd_kernel,
        grid=(4,),
        in_specs=[
            pl.BlockSpec((1, width3, rows), lambda i: (jnp.where(i == 0, 3, 1), 0, 0)),
            pl.BlockSpec((1, width3, rows), lambda i: (jnp.where(i == 3, 0, 2), 0, 0)),
            *[pl.BlockSpec((rows, features), lambda i: (0, 0))] * 4,
            pl.BlockSpec(matrix.shape, lambda i: (0, 0)),
            pl.BlockSpec(out_grad.shape, lambda i: (0, 0)),
        ],
        out_specs=(
            *[pl.BlockSpec((rows, features), lambda i: (0, 0))] * 4,
            pl.BlockSpec(matrix.shape, lambda i: (0, 0)),
        ),
        out_shape=(part, part, part, part, jax.ShapeDtypeStruct(matrix.shape, jnp.bfloat16)),
        scratch_shapes=[pltpu.VMEM((width3, features), jnp.bfloat16), pltpu.VMEM((width3, features), jnp.float32)],
        compiler_params=pltpu.CompilerParams(vmem_limit_bytes=60 << 20),
        cost_estimate=pl.CostEstimate(
            flops=16 * rows * features * width3, bytes_accessed=24 * rows * features, transcendentals=0
        ),
        name="proj_bwd",
    )(grad_proj, grad_proj, *slabs, matrix, out_grad)


def mean_of(v):
    return jnp.mean(v, axis=-1, keepdims=True)


def mix_fwd_kernel(head0, head1, head2, head3, matrix, out1, out2, out3, rows, params, hidden, low, normed, inv, *, width):
    heads = jnp.concatenate([head0[...], head1[...], head2[...], head3[...]], axis=0).T
    weights = jnp.concatenate([matrix[:, 3 * width :], out1[...], out2[...], out3[...]], axis=1)
    mixed = rows[...].astype(jnp.float32) + lax.dot_general(heads, weights, NT, preferred_element_type=jnp.float32)
    centred = mixed - mean_of(mixed)
    inv_std = lax.rsqrt(mean_of(centred * centred) + NORM_EPS)
    unit = centred * inv_std
    out = unit * params[0:1, :] + params[1:2, :]
    hidden[...] = out
    low[...] = out.astype(jnp.bfloat16)
    normed[...] = unit
    inv[...] = inv_std


def mix_fwd(heads, matrix, outs, own, params):
    width, rows = heads[0].shape
    features = matrix.shape[0]
    whole = lambda a: pl.BlockSpec(a.shape, lambda i: (0,) * len(a.shape))
    block = pl.BlockSpec((rows, features), lambda i: (0, 0))
    shape = lambda t: jax.ShapeDtypeStruct((rows, features), t)
    return pl.pallas_call(
        functools.partial(mix_fwd_kernel, width=width),
        grid=(1,),
        in_specs=[whole(a) for a in (*heads, matrix, *outs)] + [block, whole(params)],
        out_specs=(block, block, block, pl.BlockSpec((rows, 1), lambda i: (0, 0))),
        out_shape=(shape(jnp.float32), shape(jnp.bfloat16), shape(jnp.float32), jax.ShapeDtypeStruct((rows, 1), jnp.float32)),
        compiler_params=pltpu.CompilerParams(vmem_limit_bytes=60 << 20),
        cost_estimate=pl.CostEstimate(
            flops=2 * rows * features * features, bytes_accessed=14 * rows * features + 2 * features * features, transcendentals=rows
        ),
        name="mix_fwd",
    )(*heads, matrix, *outs, own, params)


def mix_bwd_kernel(
    grad_mixed, own_part, far_part, normed, inv, params, head0, head1, head2, head3, matrix, out1, out2, out3,
    grad_out, norms, made0, made1, made2, made3, og0, og1, og2, og3, *, width,
):
    grad = grad_mixed[...] + own_part[...] + far_part[...].astype(jnp.float32)
    unit = normed[...]
    norms[0:1, :] = jnp.sum(grad * unit, axis=0, keepdims=True)
    norms[1:2, :] = jnp.sum(grad, axis=0, keepdims=True)
    grad_unit = grad * params[0:1, :]
    back = inv[...] * (grad_unit - mean_of(grad_unit) - unit * mean_of(grad_unit * unit))
    grad_out[...] = back
    low = back.astype(jnp.bfloat16)
    weights = (matrix[:, 3 * width :], out1[...], out2[...], out3[...])
    for weight, head, made, og in zip(weights, (head0, head1, head2, head3), (made0, made1, made2, made3), (og0, og1, og2, og3)):
        made[...] = lax.dot_general(weight.T, low, NT, preferred_element_type=jnp.float32).astype(jnp.bfloat16)
        og[...] = jnp.dot(head[...], low, preferred_element_type=jnp.float32).astype(jnp.bfloat16)


def mix_bwd(grad_mixed, own_part, far_part, normed, inv, params, heads, matrix, outs):
    width, rows = heads[0].shape
    features = matrix.shape[0]
    whole = lambda a: pl.BlockSpec(a.shape, lambda i: (0,) * len(a.shape))
    shapes = (
        [jax.ShapeDtypeStruct((rows, features), jnp.float32), jax.ShapeDtypeStruct((2, features), jnp.float32)]
        + [jax.ShapeDtypeStruct((width, rows), jnp.bfloat16)] * 4
        + [jax.ShapeDtypeStruct((width, features), jnp.bfloat16)] * 4
    )
    ops = (grad_mixed, own_part, far_part, normed, inv, params, *heads, matrix, *outs)
    got = pl.pallas_call(
        functools.partial(mix_bwd_kernel, width=width),
        grid=(1,),
        in_specs=[whole(a) for a in ops],
        out_specs=tuple(whole(a) for a in shapes),
        out_shape=tuple(shapes),
        compiler_params=pltpu.CompilerParams(vmem_limit_bytes=60 << 20),
        cost_estimate=pl.CostEstimate(
            flops=4 * rows * features * features, bytes_accessed=22 * rows * features + 4 * features * features, transcendentals=0
        ),
        name="mix_bwd",
    )(*ops)
    return got[0], got[1], got[2:6], got[6:10]


def top_bwd_kernel(first, second, third, fourth, normed, inv, gain, low_in, back, low, norms):
    grad = first[...].astype(jnp.float32)
    for part in (second, third, fourth):
        if part is not None:
            grad += part[...].astype(jnp.float32)
    if low_in is not None:
        low_in[...] = grad.astype(jnp.bfloat16)
        grad = grad.astype(jnp.bfloat16).astype(jnp.float32)
    unit = normed[...]
    norms[0:1, :] = jnp.sum(grad * unit, axis=0, keepdims=True)
    norms[1:2, :] = jnp.sum(grad, axis=0, keepdims=True)
    grad_unit = grad * gain[...]
    out = inv[...] * (grad_unit - mean_of(grad_unit) - unit * mean_of(grad_unit * unit))
    back[...] = out
    low[...] = out.astype(jnp.bfloat16)


def top_bwd(parts, normed, inv, gain):
    rows, features = normed.shape
    several = len(parts) > 1
    whole = lambda a: pl.BlockSpec(a.shape, lambda i: (0,) * len(a.shape))
    shape = lambda t: jax.ShapeDtypeStruct((rows, features), t)
    shapes = [shape(jnp.bfloat16)] * several + [shape(jnp.float32), shape(jnp.bfloat16)]
    shapes.append(jax.ShapeDtypeStruct((2, features), jnp.float32))
    ops = (*parts, normed, inv, gain)

    def kernel(*refs):
        ins, outs = refs[: len(ops)], refs[len(ops) :]
        four = list(ins[: len(parts)]) + [None] * (4 - len(parts))
        top_bwd_kernel(*four, *ins[len(parts) :], *((None,) * (not several)), *outs)

    got = pl.pallas_call(
        kernel,
        grid=(1,),
        in_specs=[whole(a) for a in ops],
        out_specs=tuple(whole(a) for a in shapes),
        out_shape=tuple(shapes),
        compiler_params=pltpu.CompilerParams(vmem_limit_bytes=60 << 20),
        cost_estimate=pl.CostEstimate(flops=12 * rows * features, bytes_accessed=18 * rows * features, transcendentals=0),
        name="top_bwd",
    )(*ops)
    return tuple(got) if several else (None, *got)


def lamb_step(weight, gradient, first_old, second):
    first_new = BETA_ONE * first_old + (1.0 - BETA_ONE) * gradient
    second_new = BETA_TWO * second + (1.0 - BETA_TWO) * gradient * gradient
    update = (
        first_new
        / (1.0 - BETA_ONE**STEP)
        / (jnp.sqrt(second_new / (1.0 - BETA_TWO**STEP)) + ADAM_EPS)
        + DECAY_RATE * weight
    )
    return first_new, second_new, update


def lamb_kernel(*refs, kinds, shards):
    count = len(kinds)
    made, refs = refs[:shards], refs[shards:]
    olds, news, late = refs[: 3 * count], refs[3 * count : 6 * count], refs[6 * count]
    late[...] = jnp.zeros_like(late)
    for i, (turned, parts) in enumerate(kinds):
        weight, first, second = olds[3 * i : 3 * i + 3]
        first_out, second_out, update_out = news[3 * i : 3 * i + 3]
        row = None
        for at, (index, columns) in enumerate(parts):
            gradient = sum(shard[index, :, columns].astype(jnp.float32) for shard in made)
            gradient = gradient.T if turned else gradient
            where = (at,) if len(weight.shape) == 3 else (slice(None),)
            first_new, second_new, update = lamb_step(weight[where], gradient, first[where], second[where])
            first_out[where] = first_new
            second_out[where] = second_new
            update_out[where] = update
            sums = jnp.sum(update * update, axis=0, keepdims=True)
            row = sums if row is None else row + sums
        late[i : i + 1, : row.shape[1]] = row


def lamb(made, kinds, olds, features):
    whole = lambda a: pl.BlockSpec(a.shape, lambda i: (0,) * len(a.shape))
    shapes = [jax.ShapeDtypeStruct(a.shape, jnp.float32) for a in olds]
    shapes.append(jax.ShapeDtypeStruct((len(kinds), features), jnp.float32))
    ops = (*made, *olds)
    return pl.pallas_call(
        functools.partial(lamb_kernel, kinds=kinds, shards=len(made)),
        grid=(1,),
        in_specs=[whole(a) for a in ops],
        out_specs=tuple(whole(a) for a in shapes),
        out_shape=tuple(shapes),
        compiler_params=pltpu.CompilerParams(vmem_limit_bytes=60 << 20),
        cost_estimate=pl.CostEstimate(flops=20 * made[0].size, bytes_accessed=28 * made[0].size, transcendentals=made[0].size),
        name="lamb",
    )(*ops)


def finish_kernel(totals, now, first, second, *refs, count):
    weights, updates = refs[:count], refs[count : 2 * count]
    norm_out, first_out, second_out, trust = refs[2 * count : 2 * count + 4]
    news = refs[2 * count + 4 :]
    for i in range(2):
        first_new, second_new, update = lamb_step(now[i], totals[2 * i : 2 * i + 2, :], first[i], second[i])
        norms = [jnp.sqrt(jnp.sum(v * v, axis=-1, keepdims=True)) for v in (now[i], update)]
        norm_out[i] = now[i] - LEARN_RATE * (norms[0] / norms[1]) * update
        first_out[i] = first_new
        second_out[i] = second_new
    sizes = jnp.sqrt(jnp.sum(totals[4:12, :], axis=-1, keepdims=True))
    trust[...] = jnp.concatenate([sizes[0:4], sizes[4:8]], axis=1).T
    for i in range(count):
        ratio = LEARN_RATE * (sizes[i : i + 1] / sizes[4 + i : 5 + i])
        for at in range(weights[i].shape[0]) if len(weights[i].shape) == 3 else (slice(None),):
            news[i][at] = weights[i][at] - ratio * updates[i][at]


def finish(totals, now, first, second, weights, updates):
    whole = lambda a: pl.BlockSpec(a.shape, lambda i: (0,) * len(a.shape))
    shapes = [jax.ShapeDtypeStruct(now.shape, jnp.float32)] * 3 + [jax.ShapeDtypeStruct((2, 4), jnp.float32)]
    shapes += [jax.ShapeDtypeStruct(a.shape, jnp.float32) for a in weights]
    ops = (totals, now, first, second, *weights, *updates)
    size = sum(a.size for a in weights)
    return pl.pallas_call(
        functools.partial(finish_kernel, count=len(weights)),
        grid=(1,),
        in_specs=[whole(a) for a in ops],
        out_specs=tuple(whole(a) for a in shapes),
        out_shape=tuple(shapes),
        compiler_params=pltpu.CompilerParams(vmem_limit_bytes=60 << 20),
        cost_estimate=pl.CostEstimate(flops=3 * size, bytes_accessed=12 * size, transcendentals=0),
        name="finish",
    )(*ops)


STEP = 10

BETA_ONE = 0.9
BETA_TWO = 0.999
ADAM_EPS = 1e-06
DECAY_RATE = 0.01
LEARN_RATE = 0.2
NORM_EPS = 1e-05
ROPE_BASE = 1000.0

bf16 = jnp.bfloat16
f32 = jnp.float32

BOTH = ("section", "tensor")
CELLS = [(c, y, x) for c in range(2) for y in range(2) for x in range(2)]


def number(c, y, x):
    return c * 4 + y * 2 + x


def moves(target):
    return [(number(*cell), number(*target(*cell))) for cell in CELLS]


SWAP = moves(lambda c, y, x: (y, c, x))
SWAP_BACK = moves(lambda c, y, x: (1 - y, c, x))
SWAP_OUT = moves(lambda c, y, x: (y, 1 - c, x))
CORNER = moves(lambda c, y, x: (1 - c, y, 1 - x))


def over_section(v):
    return lax.ppermute(v, "section", [(0, 1), (1, 0)])


def over_x(v):
    return lax.ppermute(v, "tensor", [(0, 1), (1, 0), (2, 3), (3, 2)])


def over_y(v):
    return lax.ppermute(v, "tensor", [(0, 2), (1, 3), (2, 0), (3, 1)])


def over_diag(v):
    return lax.ppermute(v, "tensor", [(0, 3), (1, 2), (2, 1), (3, 0)])


def over_both(v, pairs):
    return lax.ppermute(v, BOTH, pairs)


def over_z(v, k):
    return lax.ppermute(v, "dp", [(i, i ^ k) for i in range(4)])


def quad():
    return lax.axis_size("dp") == 4


def gather_later(piece, axis):
    return lax.all_gather(piece, "dp", axis=axis, tiled=True)


def scatter_later(whole, axis):
    return lax.psum_scatter(whole, "dp", scatter_dimension=axis, tiled=True)


def to_owner(shard, layer):
    same = [pair for pair in SWAP if pair[1] // 4 == layer]
    other = [pair for pair in SWAP_BACK if pair[1] // 4 == layer]
    return over_both(shard, same), over_both(shard, other)


def chips_total(v):
    v = (v + over_x(v)) + (over_y(v) + over_diag(v))
    if not quad():
        return lax.psum(v, "dp")
    return (v + over_z(v, 1)) + (over_z(v, 2) + over_z(v, 3))


def rope_tables(length):
    half_size = HEAD // 2
    freq_vals = np.float32(ROPE_BASE) ** (-np.arange(half_size, dtype=np.float32) * np.float32(2.0 / HEAD))
    angles = freq_vals[:, None] * np.arange(length, dtype=np.float32)[None, :]
    return jnp.asarray(np.cos(angles)), jnp.asarray(np.sin(angles))


def norm_fwd(values, gain_row, bias_row):
    mean_val = jnp.mean(values, axis=-1, keepdims=True)
    centred = values - mean_val
    variance = jnp.mean(centred * centred, axis=-1, keepdims=True)
    inv_std = lax.rsqrt(variance + NORM_EPS)
    normed = centred * inv_std
    return (normed * gain_row + bias_row, normed, inv_std)


def dot(spec, a, b):
    return jnp.einsum(spec, a, b, preferred_element_type=f32)


def after(value, *others):
    return lax.optimization_barrier((value,) + others)[0]


def layer_forward(slabs, matrix, ffn, params, env, late):
    place, ends, cos, sin = env
    *mine, log_sums, qkv = attn_fwd(place, ends, slabs, matrix, cos, sin)
    out_own = matrix[:, 3 * (matrix.shape[1] // 4) :]
    out_across = over_x(out_own)
    outs = (over_section(out_own), out_across, over_section(after(out_across, log_sums)))
    all_heads = [mine[0], over_section(mine[1]), over_x(mine[2]), over_both(mine[3], CORNER)]
    hidden, hidden_low, normed_one, inv_one = mix_fwd(all_heads, matrix, outs, slabs[0], params[:, 0])
    hidden_rows = [hidden_low, over_x(hidden_low)]
    ffn = (ffn, over_section(after(ffn, hidden_rows[late])))
    own_part, *own_acts = ffn_fwd(hidden_rows[0], *ffn, f32)
    far_part, *far_acts = ffn_fwd(hidden_rows[1], *ffn, bf16)
    ffn_out = own_part + over_x(far_part).astype(f32)
    output, normed_two, inv_two = norm_fwd(hidden + ffn_out, params[0, 1], params[1, 1])
    kept = (slabs, qkv, mine, log_sums, all_heads, normed_one, inv_one, hidden_rows, (own_acts, far_acts))
    return output.astype(bf16), outs, kept + (normed_two, inv_two, ffn)


def layer_backward(grad_parts, kept, matrix, outs, params, env, early=(), late=()):
    place, ends, cos, sin = env
    (slabs, qkv, mine, log_sums, all_heads, normed_one, inv_one, hidden_rows, acts, normed_two, inv_two, ffn) = kept
    sent, grad_mixed, grad_low, norm_two = top_bwd(grad_parts, normed_two, inv_two, params[0, 1:2])
    grad_rows = [grad_low, over_x(grad_low)]
    own_part, *own_grads = ffn_bwd(grad_rows[0], *acts[0], *ffn, f32)
    far_part, *far_grads = ffn_bwd(after(grad_rows[1], own_part, *early), *acts[1], *ffn, bf16)
    made = list(zip(own_grads, far_grads))
    ffn_other = ffn_grads(1, hidden_rows, grad_rows, *made)
    ffn_grad = ffn_grads(0, hidden_rows, grad_rows, *made, over_section(ffn_other))
    far_part = over_x(far_part)
    ffn_grad = after(ffn_grad, far_part)
    grad_mixed_one, norm_one, grad_heads, out_grad = mix_bwd(
        grad_mixed, own_part, far_part, normed_one, inv_one, params[:, 0], all_heads, matrix, outs
    )
    grad_mine = (
        grad_heads[0], over_section(grad_heads[1]), over_x(grad_heads[2]), over_both(grad_heads[3], CORNER)
    )
    *out_grad, _ = lax.optimization_barrier((*out_grad, grad_mine))
    out_own = (out_grad[0], over_section(out_grad[1]), over_x(out_grad[2]), over_both(out_grad[3], CORNER))
    grad_proj = attn_bwd(place, ends, qkv, after(grad_mine, *late), mine, log_sums, cos, sin)
    out_own = sum(g.astype(f32) for g in after(out_own, grad_proj))
    part3, part1, part2, part0, matrix_grad = proj_bwd(grad_proj, slabs, matrix, out_own)
    far_sum = over_x((part2.astype(f32) + over_section(part3).astype(f32)).astype(bf16))
    norm_grads = jnp.stack([jnp.stack([norm_one[0], norm_two[0]]), jnp.stack([norm_one[1], norm_two[1]])])
    return sent, (grad_mixed_one, part0, over_section(part1), far_sum), matrix_grad, ffn_grad, norm_grads


def body(
    tokens,
    cotangent,
    segments,
    heads_in,
    heads_out,
    gate_up,
    project_down,
    norm_gain,
    norm_bias,
    heads_in_first,
    heads_in_second,
    heads_out_first,
    heads_out_second,
    gate_up_first,
    gate_up_second,
    project_down_first,
    project_down_second,
    norm_first,
    norm_second,
):
    section = lax.axis_index("section")
    spot = lax.axis_index("tensor")
    y, x = spot // 2, spot % 2
    rows = tokens.shape[1]
    length = segments.shape[-1]
    masters = (heads_in[0], heads_out[0], gate_up[0], project_down[0].T)
    deep, width = masters[0].shape[1:]

    attn_piece = jnp.concatenate(
        [masters[0].transpose(1, 0, 2).reshape(deep, 3 * width), masters[1].T], axis=1
    ).astype(bf16)
    ffn_piece = jnp.concatenate([masters[2], masters[3][None]], axis=0).astype(bf16)

    def to_block(piece, layer):
        got = []
        for to_y in range(2):
            pairs = [(number(layer, c, x), number(c, to_y, x)) for c in range(2) for x in range(2)]
            got.append(over_both(piece, pairs))
        return got

    def for_y(got):
        return jnp.where(y == 0, got[0], got[1])

    def four_slabs(rows, *along):
        across, *along = lax.optimization_barrier((over_x(rows), *along))
        return (rows, over_section(rows), across, over_section(across)), along

    own = over_both(lax.dynamic_index_in_dim(tokens, section, 0, keepdims=False), SWAP)
    first_matrix = gather_later(for_y(to_block(attn_piece, 0)), 0)
    slabs_zero, ffn_pieces = four_slabs(own, *to_block(after(ffn_piece, own), 0))
    ffn_first = gather_later(for_y(ffn_pieces), 1)

    both_params = jnp.stack([norm_gain[0], norm_bias[0]])
    other_params = over_section(both_params)
    params = [
        jnp.where(section == 0, both_params, other_params),
        jnp.where(section == 0, other_params, both_params),
    ]

    block = 2 * section + x
    place = jnp.stack([block, block ^ 2, block ^ 1, block ^ 3]).astype(jnp.int32)
    seq_seg = lax.dynamic_index_in_dim(segments, y, 0, keepdims=False)[0]
    ends = jnp.stack([jnp.sum((seq_seg <= d).astype(jnp.int32)) for d in range(2)])
    env = (place, ends) + rope_tables(length)

    low_zero, outs_zero, kept_zero = layer_forward(slabs_zero, first_matrix, ffn_first, params[0], env, 1)
    hidden_rows = kept_zero[7]
    second_piece = for_y(to_block(after(jnp.concatenate([attn_piece[None], ffn_piece]), slabs_zero[3]), 1))
    second_matrix = gather_later(after(second_piece[0], hidden_rows[0]), 0)
    ffn_second = gather_later(after(second_piece[1:], hidden_rows[1]), 1)
    slabs_one, _ = four_slabs(low_zero)
    low_one, outs_one, kept_one = layer_forward(slabs_one, second_matrix, ffn_second, params[1], env, 0)
    grad_top = over_both(after(lax.dynamic_index_in_dim(cotangent, section, 0, keepdims=False), low_zero), SWAP)
    def home(zero, one):
        same = over_both(jnp.where(y == 0, zero, one), SWAP)
        other = over_both(jnp.where(y == 0, one, zero), SWAP_BACK)
        return same, other

    def by_micro(zero, one):
        same, other = home(zero, one)
        return jnp.stack([jnp.where(section == 0, same, other), jnp.where(section == 0, other, same)])

    layer_out = by_micro(low_zero, low_one)
    _, grads_one, matrix_one, ffn_one, norm_one = layer_backward(
        (grad_top,), kept_one, second_matrix, outs_one, params[1], env, (layer_out,)
    )
    ffn_one = to_owner(scatter_later(ffn_one, 1), 1)
    matrix_one = to_owner(scatter_later(matrix_one, 0)[None], 1)
    sent, grads_zero, matrix_zero, ffn_zero, norm_zero = layer_backward(
        grads_one, kept_zero, first_matrix, outs_zero, params[0], env, ffn_one, matrix_one
    )
    ffn_home = to_owner(scatter_later(ffn_zero, 1), 0) + ffn_one
    attn_home = to_owner(scatter_later(matrix_zero, 0)[None], 0)
    grad_zero = sum(g.astype(f32) for g in grads_zero)


    norm_mine = jnp.where(section == 0, norm_zero, norm_one) + over_section(
        jnp.where(section == 0, norm_one, norm_zero)
    )
    features = norm_mine.shape[-1]
    firsts = (heads_in_first[0], heads_out_first[0], gate_up_first[0], project_down_first[0].T)
    seconds = (heads_in_second[0], heads_out_second[0], gate_up_second[0], project_down_second[0].T)
    olds = list(zip(masters, firsts, seconds))

    def squares(matrix):
        row = jnp.sum((matrix * matrix).reshape(-1, matrix.shape[-1]), axis=0)
        return jnp.pad(row, (0, features - row.shape[0]))

    columns = slice(0, masters[2].shape[-1])
    ffn_new = lamb(
        ffn_home, ((False, ((0, columns), (1, columns))), (False, ((2, columns),))), olds[2] + olds[3], features
    )
    early = jnp.stack([squares(m) for m in masters])
    early = jnp.concatenate([norm_mine.reshape(4, -1), early], axis=0)
    attn_home = lax.optimization_barrier((*attn_home, early, ffn_new[-1]))[:2] + matrix_one
    pieces = tuple((0, slice(i * width, (i + 1) * width)) for i in range(4))
    attn_new = lamb(attn_home, ((False, pieces[:3]), (True, pieces[3:])), olds[0] + olds[1], features)
    totals = chips_total(jnp.concatenate([early, attn_new[-1], ffn_new[-1]], axis=0))
    made = [attn_new[:3], attn_new[3:6], ffn_new[:3], ffn_new[3:6]]
    *norms, trust_norms, in_new, out_new, gate_new, down_new = finish(
        totals, both_params, norm_first[0], norm_second[0], masters, [m[2] for m in made]
    )
    new_mats = (in_new, out_new, gate_new, down_new.T)
    made[3] = [v.T for v in made[3]]
    input_grads = by_micro(after(grad_zero.astype(bf16), attn_home[0]), sent).astype(f32)
    outs = [layer_out, input_grads]
    for i in range(4):
        outs += [new_mats[i], made[i][0], made[i][1]]
    outs += [*norms, trust_norms.T]
    return tuple(item[None] for item in outs)


def solution(mesh):
    rows = P(None, ("dp", "tensor"), None)
    out_rows = P("section", None, ("dp", "tensor"), None)
    columns = P("section", None, "dp", "tensor")
    turned = P("section", "tensor", "dp")
    vectors = P("section", None, None)
    pairs = P("section", None, None, None)
    return jax.shard_map(
        body,
        mesh=mesh,
        in_specs=(rows, rows, P(None, "dp", None), columns, turned, columns, turned, vectors, vectors)
        + (columns, columns, turned, turned, columns, columns, turned, turned, pairs, pairs),
        out_specs=(out_rows, out_rows)
        + (columns,) * 3
        + (turned,) * 3
        + (columns,) * 3
        + (turned,) * 3
        + (pairs,) * 3
        + (vectors,),
        check_vma=False,
    )
```

```python
import functools

import jax
import jax.numpy as jnp
import numpy as np
from jax import lax
from jax.experimental import pallas as pl
from jax.experimental.pallas import tpu as pltpu
from jax.sharding import PartitionSpec as P

HEAD = 64
FQ, FK = 512, 512
BQ, BK = 256, 512
SAFE = 40.0
WINDOW = 1024


def doc_bounds(pos, ends, length):
    start = jnp.where(pos < ends[0], 0, jnp.where(pos < ends[1], ends[0], ends[1]))
    last = jnp.where(pos < ends[0], ends[0], jnp.where(pos < ends[1], ends[1], length)) - 1
    return jnp.maximum(start, pos - (WINDOW - 1)), jnp.minimum(last, pos + (WINDOW - 1))


def key_span(q_start, rows, ends, length, deep):
    low, _ = doc_bounds(q_start, ends, length)
    _, high = doc_bounds(q_start + rows - 1, ends, length)
    first = low // 128 * 128
    tiles = (high + 1 - first + deep - 1) // deep
    return jnp.minimum(first, length - tiles * deep), tiles


def attn_fwd_kernel(place, ends, slab0, slab1, slab2, slab3, matrix, cos, sin, out0, out1, out2, out3, lse, qkv, a_t, k_n, o_t, calm, *, heads):
    step = pl.program_id(0)
    width = heads * HEAD
    half = HEAD // 2
    length = qkv.shape[1]
    rows = length // 4

    @pl.when(step == 0)
    def _():
        a_t[...] = matrix[:, : 3 * width].T
        tops = [jnp.zeros((1, rows), jnp.float32) for _ in range(2 * heads)]
        for slab, src in enumerate((slab0, slab1, slab2, slab3)):
            start = pl.multiple_of(place[slab] * rows, rows)
            here = pl.ds(start, rows)
            proj = lax.dot_general(a_t[...], src[...], (((1,), (1,)), ((), ())), preferred_element_type=jnp.float32)
            c, s = cos[:, here], sin[:, here]
            for i in range(2 * heads):
                first, second = proj[i * HEAD : i * HEAD + half], proj[i * HEAD + half : (i + 1) * HEAD]
                turned = jnp.concatenate([first * c - second * s, second * c + first * s], axis=0).astype(jnp.bfloat16)
                if i < heads:
                    turned = turned * jnp.bfloat16(HEAD**-0.5)
                else:
                    k_n[i - heads, here, :] = turned.T
                qkv[i * HEAD : (i + 1) * HEAD, here] = turned
                size = turned.astype(jnp.float32)
                tops[i] = jnp.maximum(tops[i], jnp.sum(size * size, axis=0, keepdims=True))
            qkv[2 * width :, here] = proj[2 * width :].astype(jnp.bfloat16)
        worst = jnp.float32(0.0)
        for h in range(heads):
            worst = jnp.maximum(worst, jnp.max(tops[h]) * jnp.max(tops[heads + h]))
        calm[0] = (worst <= SAFE * SAFE).astype(jnp.int32)

    q_start = pl.multiple_of(step * FQ, FQ)
    here = pl.ds(q_start, FQ)
    low, high = doc_bounds(q_start + lax.broadcasted_iota(jnp.int32, (1, FQ), 1), (ends[0], ends[1]), length)
    first, tiles = key_span(q_start, FQ, (ends[0], ends[1]), length, FK)

    def score(h, keys):
        return jnp.dot(k_n[h, keys, :], qkv[h * HEAD : (h + 1) * HEAD, here], preferred_element_type=jnp.float32)

    def weigh(h, keys, p):
        return jnp.dot(
            qkv[2 * width + h * HEAD : 2 * width + (h + 1) * HEAD, keys], p.astype(jnp.bfloat16),
            preferred_element_type=jnp.float32,
        )

    def mask(t):
        k_start = pl.multiple_of(first + t * FK, 128)
        pos = k_start + lax.broadcasted_iota(jnp.int32, (FK, FQ), 0)
        return pl.ds(k_start, FK), (pos >= low) & (pos <= high)

    def finish(h, total, acc, log_sum):
        o_t[h * HEAD : (h + 1) * HEAD, here] = (acc / total).astype(jnp.bfloat16)
        lse[h : h + 1, here] = log_sum

    @pl.when(calm[0] == 1)
    def _():
        def tile(t, carry):
            keys, allowed = mask(t)
            new = []
            nxt = score(0, keys)
            for h in range(heads):
                total, acc = carry[h]
                s = nxt
                if h + 1 < heads:
                    nxt = score(h + 1, keys)
                p = jnp.where(allowed, jnp.exp(s), 0.0)
                new.append((total + jnp.sum(p, axis=0, keepdims=True), acc + weigh(h, keys, p)))
            return tuple(new)

        init = tuple((jnp.zeros((1, FQ), jnp.float32), jnp.zeros((HEAD, FQ), jnp.float32)) for _ in range(heads))
        for h, (total, acc) in enumerate(lax.fori_loop(0, tiles, tile, init)):
            finish(h, total, acc, jnp.log(total))

    @pl.when(calm[0] == 0)
    def _():
        def tile(t, carry):
            keys, allowed = mask(t)
            new = []
            for h in range(heads):
                top, total, acc = carry[h]
                s = jnp.where(allowed, score(h, keys), -1e30)
                new_top = jnp.maximum(top, jnp.max(s, axis=0, keepdims=True))
                p = jnp.exp(s - new_top)
                alpha = jnp.exp(top - new_top)
                total = total * alpha + jnp.sum(p, axis=0, keepdims=True)
                new.append((new_top, total, acc * alpha + weigh(h, keys, p)))
            return tuple(new)

        init = tuple(
            (jnp.full((1, FQ), -1e30, jnp.float32), jnp.zeros((1, FQ), jnp.float32), jnp.zeros((HEAD, FQ), jnp.float32))
            for _ in range(heads)
        )
        for h, (top, total, acc) in enumerate(lax.fori_loop(0, tiles, tile, init)):
            finish(h, total, acc, top + jnp.log(total))

    @pl.when(step == pl.num_programs(0) - 1)
    def _():
        for slab, out in enumerate((out0, out1, out2, out3)):
            out[...] = o_t[:, pl.ds(pl.multiple_of(place[slab] * rows, rows), rows)]


def whole_spec(a):
    return pl.BlockSpec(a.shape, lambda i: (0,) * len(a.shape))


def attn_fwd(place, ends, slabs, matrix, cos, sin):
    rows = slabs[0].shape[0]
    length = 4 * rows
    width = matrix.shape[1] // 4
    heads = width // HEAD
    smem = pl.BlockSpec(memory_space=pltpu.SMEM)
    ops = (*slabs, matrix, cos, sin)
    outs = (
        *[jax.ShapeDtypeStruct((width, rows), jnp.bfloat16)] * 4,
        jax.ShapeDtypeStruct((heads, length), jnp.float32),
        jax.ShapeDtypeStruct((3 * width, length), jnp.bfloat16),
    )
    return pl.pallas_call(
        functools.partial(attn_fwd_kernel, heads=heads),
        grid=(length // FQ,),
        in_specs=[smem, smem] + [whole_spec(a) for a in ops],
        out_specs=tuple(whole_spec(o) for o in outs),
        out_shape=outs,
        scratch_shapes=[
            pltpu.VMEM((3 * width, matrix.shape[0]), jnp.bfloat16),
            pltpu.VMEM((heads, length, HEAD), jnp.bfloat16),
            pltpu.VMEM((width, length), jnp.bfloat16),
            pltpu.SMEM((1,), jnp.int32),
        ],
        compiler_params=pltpu.CompilerParams(vmem_limit_bytes=48 << 20),
        cost_estimate=pl.CostEstimate(
            flops=6 * length * length * width, bytes_accessed=16 * length * width, transcendentals=heads * length * length
        ),
        name="attn_fwd",
    )(place, ends, *ops)


def attn_bwd_kernel(place, ends, qkv, do0, do1, do2, do3, out0, out1, out2, out3, lse, cos, sin, dproj, q_n, k_n, v_n, do_t, do_n, delta, dq_t, dk, dv, *, heads):
    step = pl.program_id(0)
    width = heads * HEAD
    length = qkv.shape[1]
    rows = length // 4
    half = HEAD // 2

    @pl.when(step == 0)
    def _():
        for slab, (dout, out) in enumerate(((do0, out0), (do1, out1), (do2, out2), (do3, out3))):
            start = pl.multiple_of(place[slab] * rows, rows)
            do_t[:, pl.ds(start, rows)] = dout[...]
            prod = dout[...].astype(jnp.float32) * out[...].astype(jnp.float32)
            for h in range(heads):
                piece = slice(h * HEAD, (h + 1) * HEAD)
                delta[h : h + 1, pl.ds(start, rows)] = jnp.sum(prod[piece], axis=0, keepdims=True)
                do_n[h, pl.ds(start, rows), :] = dout[piece, :].T
        for h in range(heads):
            q_n[h] = qkv[h * HEAD : (h + 1) * HEAD, :].T
            k_n[h] = qkv[width + h * HEAD : width + (h + 1) * HEAD, :].T
            v_n[h] = qkv[2 * width + h * HEAD : 2 * width + (h + 1) * HEAD, :].T
        dk[...] = jnp.zeros_like(dk)
        dv[...] = jnp.zeros_like(dv)

    q_start = pl.multiple_of(step * BQ, BQ)
    qs = pl.ds(q_start, BQ)
    low, high = doc_bounds(q_start + lax.broadcasted_iota(jnp.int32, (1, BQ), 1), (ends[0], ends[1]), length)
    first, tiles = key_span(q_start, BQ, (ends[0], ends[1]), length, BK)

    def tile(t, carry):
        k_start = pl.multiple_of(first + t * BK, 128)
        ks = pl.ds(k_start, BK)
        pos = k_start + lax.broadcasted_iota(jnp.int32, (BK, BQ), 0)
        allowed = (pos >= low) & (pos <= high)
        new = []

        def score(h):
            piece = slice(h * HEAD, (h + 1) * HEAD)
            return (
                jnp.dot(k_n[h, ks, :], qkv[piece, qs], preferred_element_type=jnp.float32),
                jnp.dot(v_n[h, ks, :], do_t[piece, qs], preferred_element_type=jnp.float32),
            )

        nxt = score(0)
        for h in range(heads):
            s, dp = nxt
            if h + 1 < heads:
                nxt = score(h + 1)
            p = jnp.where(allowed, jnp.exp(s - lse[h : h + 1, qs]), 0.0)
            ds = (p * (dp - delta[h : h + 1, qs])).astype(jnp.bfloat16)
            dv[h, ks, :] += jnp.dot(p.astype(jnp.bfloat16), do_n[h, qs, :], preferred_element_type=jnp.float32)
            dk[h, ks, :] += jnp.dot(ds, q_n[h, qs, :], preferred_element_type=jnp.float32)
            new.append(carry[h] + jnp.dot(qkv[width + h * HEAD : width + (h + 1) * HEAD, ks], ds, preferred_element_type=jnp.float32))
        return tuple(new)

    init = tuple(jnp.zeros((HEAD, BQ), jnp.float32) for _ in range(heads))
    done = lax.fori_loop(0, tiles, tile, init)
    for h in range(heads):
        dq_t[h * HEAD : (h + 1) * HEAD, qs] = done[h]

    @pl.when(step == pl.num_programs(0) - 1)
    def _():
        for slab in range(4):
            start = pl.multiple_of(place[slab] * rows, rows)
            c, s = cos[:, pl.ds(start, rows)], sin[:, pl.ds(start, rows)]
            for h in range(heads):
                gq = dq_t[h * HEAD : (h + 1) * HEAD, pl.ds(start, rows)] * HEAD**-0.5
                gk = dk[h, pl.ds(start, rows), :].T
                gv = dv[h, pl.ds(start, rows), :].T
                for kind, g in ((0, gq), (1, gk)):
                    g1, g2 = g[:half], g[half:]
                    at = kind * width + h * HEAD
                    dproj[slab, at : at + half, :] = (g1 * c + g2 * s).astype(jnp.bfloat16)
                    dproj[slab, at + half : at + HEAD, :] = (g2 * c - g1 * s).astype(jnp.bfloat16)
                at = 2 * width + h * HEAD
                dproj[slab, at : at + HEAD, :] = gv.astype(jnp.bfloat16)


def attn_bwd(place, ends, qkv, douts, outs, lse, cos, sin):
    length = qkv.shape[1]
    rows = length // 4
    width = qkv.shape[0] // 3
    heads = width // HEAD
    smem = pl.BlockSpec(memory_space=pltpu.SMEM)
    ops = (qkv, *douts, *outs, lse, cos, sin)
    natural = pltpu.VMEM((heads, length, HEAD), jnp.bfloat16)
    sums = pltpu.VMEM((heads, length, HEAD), jnp.float32)
    return pl.pallas_call(
        functools.partial(attn_bwd_kernel, heads=heads),
        grid=(length // BQ,),
        in_specs=[smem, smem] + [whole_spec(a) for a in ops],
        out_specs=pl.BlockSpec((4, 3 * width, rows), lambda i: (0, 0, 0)),
        out_shape=jax.ShapeDtypeStruct((4, 3 * width, rows), jnp.bfloat16),
        scratch_shapes=[natural, natural, natural, pltpu.VMEM((width, length), jnp.bfloat16), natural]
        + [pltpu.VMEM((heads, length), jnp.float32), pltpu.VMEM((width, length), jnp.float32), sums, sums],
        compiler_params=pltpu.CompilerParams(vmem_limit_bytes=56 << 20),
        cost_estimate=pl.CostEstimate(
            flops=10 * length * length * width, bytes_accessed=24 * length * width, transcendentals=heads * length * length
        ),
        name="attn_bwd",
    )(place, ends, *ops)


FT = 768


def ffn_specs(rows, deep, hidden, step_tiles):
    first = pl.BlockSpec((3, deep, FT), lambda b, j: (0, 0, jnp.where(b == 0, j, step_tiles - 1)))
    second = pl.BlockSpec((3, deep, FT), lambda b, j: (0, 0, jnp.where(b == 0, 0, j)))
    acts = pl.BlockSpec((1, rows, FT), lambda b, j: (b, 0, j))
    whole = pl.BlockSpec((rows, deep), lambda b, j: (0, 0))
    return first, second, acts, whole


NT = (((1,), (1,)), ((), ()))


def ffn_fwd_kernel(rows_ref, first, second, out, gate_out, up_out, total):
    b, j = pl.program_id(0), pl.program_id(1)

    def work(block, fresh):
        h = rows_ref[...]
        gate = jnp.dot(h, block[0], preferred_element_type=jnp.float32)
        up = jnp.dot(h, block[1], preferred_element_type=jnp.float32)
        gate_out[0] = gate.astype(jnp.bfloat16)
        up_out[0] = up.astype(jnp.bfloat16)
        inner = (gate / (1.0 + jnp.exp(-gate)) * up).astype(jnp.bfloat16)
        part = lax.dot_general(inner, block[2], NT, preferred_element_type=jnp.float32)
        total[...] = part if fresh else total[...] + part

    pl.when((b == 0) & (j == 0))(lambda: work(first, True))
    pl.when((b == 0) & (j > 0))(lambda: work(first, False))
    pl.when(b == 1)(lambda: work(second, False))

    @pl.when((b == 1) & (j == pl.num_programs(1) - 1))
    def _():
        out[...] = total[...].astype(out.dtype)


def ffn_fwd(rows, first, second, out_type):
    length, deep = rows.shape
    hidden = first.shape[2]
    tiles = hidden // FT
    w1, w2, acts, whole = ffn_specs(length, deep, hidden, tiles)
    act = jax.ShapeDtypeStruct((2, length, hidden), jnp.bfloat16)
    return pl.pallas_call(
        ffn_fwd_kernel,
        grid=(2, tiles),
        in_specs=[whole, w1, w2],
        out_specs=(whole, acts, acts),
        out_shape=(jax.ShapeDtypeStruct((length, deep), out_type), act, act),
        scratch_shapes=[pltpu.VMEM((length, deep), jnp.float32)],
        compiler_params=pltpu.CompilerParams(vmem_limit_bytes=32 << 20),
        cost_estimate=pl.CostEstimate(
            flops=12 * length * deep * hidden, bytes_accessed=12 * deep * hidden + 8 * length * hidden, transcendentals=2 * length * hidden
        ),
        name="ffn_fwd",
    )(rows, first, second)


def ffn_bwd_kernel(grad_ref, gate_ref, up_ref, first, second, out, grad_gate_out, grad_up_out, inner_out, total):
    b, j = pl.program_id(0), pl.program_id(1)

    def work(block, fresh):
        grad_inner = jnp.dot(grad_ref[...], block[2], preferred_element_type=jnp.float32)
        gate, up = gate_ref[0].astype(jnp.float32), up_ref[0].astype(jnp.float32)
        sig = 1.0 / (1.0 + jnp.exp(-gate))
        act = gate * sig
        grad_gate = (grad_inner * up * (sig + act * (1.0 - sig))).astype(jnp.bfloat16)
        grad_up = (grad_inner * act).astype(jnp.bfloat16)
        grad_gate_out[0] = grad_gate
        grad_up_out[0] = grad_up
        inner_out[0] = (act * up).astype(jnp.bfloat16)
        part = lax.dot_general(grad_gate, block[0], NT, preferred_element_type=jnp.float32)
        part += lax.dot_general(grad_up, block[1], NT, preferred_element_type=jnp.float32)
        total[...] = part if fresh else total[...] + part

    pl.when((b == 0) & (j == 0))(lambda: work(first, True))
    pl.when((b == 0) & (j > 0))(lambda: work(first, False))
    pl.when(b == 1)(lambda: work(second, False))

    @pl.when((b == 1) & (j == pl.num_programs(1) - 1))
    def _():
        out[...] = total[...].astype(out.dtype)


def ffn_bwd(grad, gate, up, first, second, out_type):
    length, deep = grad.shape
    hidden = first.shape[2]
    tiles = hidden // FT
    w1, w2, acts, whole = ffn_specs(length, deep, hidden, tiles)
    act = jax.ShapeDtypeStruct((2, length, hidden), jnp.bfloat16)
    return pl.pallas_call(
        ffn_bwd_kernel,
        grid=(2, tiles),
        in_specs=[whole, acts, acts, w1, w2],
        out_specs=(whole, acts, acts, acts),
        out_shape=(jax.ShapeDtypeStruct((length, deep), out_type), act, act, act),
        scratch_shapes=[pltpu.VMEM((length, deep), jnp.float32)],
        compiler_params=pltpu.CompilerParams(vmem_limit_bytes=32 << 20),
        cost_estimate=pl.CostEstimate(
            flops=12 * length * deep * hidden, bytes_accessed=12 * deep * hidden + 20 * length * hidden, transcendentals=2 * length * hidden
        ),
        name="ffn_bwd",
    )(grad, gate, up, first, second)


def ffn_grads_kernel(h0, h1, g0, g1, gate0, gate1, up0, up1, in0, in1, *rest, slot):
    *other, out, h_t, g_t = rest

    @pl.when(pl.program_id(0) == 0)
    def _():
        rows = h0.shape[0]
        h_t[:, :rows] = h0[...].T
        h_t[:, rows:] = h1[...].T
        g_t[:, :rows] = g0[...].T
        g_t[:, rows:] = g1[...].T

    for i, (left, a, b) in enumerate(((h_t, gate0, gate1), (h_t, up0, up1), (g_t, in0, in1))):
        both = jnp.concatenate([a[0], b[0]], axis=0)
        grad = jnp.dot(left[...], both, preferred_element_type=jnp.float32)
        if other:
            grad += other[0][i].astype(jnp.float32)
        out[i] = grad.astype(jnp.bfloat16)


def ffn_grads(slot, rows, grads, gates, ups, inners, *other):
    length, deep = rows[0].shape
    hidden = gates[0].shape[2]
    whole = pl.BlockSpec((length, deep), lambda j: (0, 0))
    acts = pl.BlockSpec((1, length, FT), lambda j: (slot, 0, j))
    weights = pl.BlockSpec((3, deep, FT), lambda j: (0, 0, j))
    both = pltpu.VMEM((deep, 2 * length), jnp.bfloat16)
    return pl.pallas_call(
        functools.partial(ffn_grads_kernel, slot=slot),
        grid=(hidden // FT,),
        in_specs=[whole] * 4 + [acts] * 6 + [weights] * len(other),
        out_specs=weights,
        out_shape=jax.ShapeDtypeStruct((3, deep, hidden), jnp.bfloat16),
        scratch_shapes=[both, both],
        compiler_params=pltpu.CompilerParams(vmem_limit_bytes=32 << 20),
        cost_estimate=pl.CostEstimate(
            flops=12 * length * deep * hidden, bytes_accessed=6 * deep * hidden + 12 * length * hidden, transcendentals=0
        ),
        name="ffn_grads",
    )(*rows, *grads, *gates, *ups, *inners, *other)


def proj_bwd_kernel(pair_grad, rest_grad, slab0, slab1, slab2, slab3, matrix, out_grad, made3, made1, made2, made0, grad, a_t, total):
    step = pl.program_id(0)
    width3 = total.shape[0]

    @pl.when(step == 0)
    def _():
        a_t[...] = matrix[:, :width3].T
        total[...] = jnp.zeros_like(total)

    def work(made, rows, out):
        total[...] += jnp.dot(made, rows, preferred_element_type=jnp.float32)
        out[...] = jnp.dot(made.T, a_t[...], preferred_element_type=jnp.float32).astype(jnp.bfloat16)

    pl.when(step == 0)(lambda: work(pair_grad[0], slab3[...], made3))
    pl.when(step == 1)(lambda: work(pair_grad[0], slab1[...], made1))
    pl.when(step == 2)(lambda: work(rest_grad[0], slab2[...], made2))
    pl.when(step == 3)(lambda: work(rest_grad[0], slab0[...], made0))

    @pl.when(step == 3)
    def _():
        grad[...] = jnp.concatenate([total[...], out_grad[...]], axis=0).astype(jnp.bfloat16).T


def proj_bwd(grad_proj, slabs, matrix, out_grad):
    _, width3, rows = grad_proj.shape
    features = matrix.shape[0]
    part = jax.ShapeDtypeStruct((rows, features), jnp.bfloat16)
    return pl.pallas_call(
        proj_bwd_kernel,
        grid=(4,),
        in_specs=[
            pl.BlockSpec((1, width3, rows), lambda i: (jnp.where(i == 0, 3, 1), 0, 0)),
            pl.BlockSpec((1, width3, rows), lambda i: (jnp.where(i == 3, 0, 2), 0, 0)),
            *[pl.BlockSpec((rows, features), lambda i: (0, 0))] * 4,
            pl.BlockSpec(matrix.shape, lambda i: (0, 0)),
            pl.BlockSpec(out_grad.shape, lambda i: (0, 0)),
        ],
        out_specs=(
            *[pl.BlockSpec((rows, features), lambda i: (0, 0))] * 4,
            pl.BlockSpec(matrix.shape, lambda i: (0, 0)),
        ),
        out_shape=(part, part, part, part, jax.ShapeDtypeStruct(matrix.shape, jnp.bfloat16)),
        scratch_shapes=[pltpu.VMEM((width3, features), jnp.bfloat16), pltpu.VMEM((width3, features), jnp.float32)],
        compiler_params=pltpu.CompilerParams(vmem_limit_bytes=60 << 20),
        cost_estimate=pl.CostEstimate(
            flops=16 * rows * features * width3, bytes_accessed=24 * rows * features, transcendentals=0
        ),
        name="proj_bwd",
    )(grad_proj, grad_proj, *slabs, matrix, out_grad)


ROW_TILE = 256


def mean_of(v):
    return jnp.mean(v, axis=-1, keepdims=True)


def mix_fwd_kernel(head0, head1, head2, head3, matrix, out1, out2, out3, rows, params, hidden, low, normed, inv, weights, *, width):
    @pl.when(pl.program_id(0) == 0)
    def _():
        weights[...] = jnp.concatenate([matrix[:, 3 * width :], out1[...], out2[...], out3[...]], axis=1)

    heads = jnp.concatenate([head0[...], head1[...], head2[...], head3[...]], axis=0).T
    mixed = rows[...].astype(jnp.float32) + lax.dot_general(heads, weights[...], NT, preferred_element_type=jnp.float32)
    centred = mixed - mean_of(mixed)
    inv_std = lax.rsqrt(mean_of(centred * centred) + NORM_EPS)
    unit = centred * inv_std
    out = unit * params[0:1, :] + params[1:2, :]
    hidden[...] = out
    low[...] = out.astype(jnp.bfloat16)
    normed[...] = unit
    inv[...] = inv_std


def mix_fwd(heads, matrix, outs, own, params):
    width, rows = heads[0].shape
    features = matrix.shape[0]
    whole = lambda a: pl.BlockSpec(a.shape, lambda i: (0,) * len(a.shape))
    block = pl.BlockSpec((ROW_TILE, features), lambda i: (i, 0))
    shape = lambda t: jax.ShapeDtypeStruct((rows, features), t)
    return pl.pallas_call(
        functools.partial(mix_fwd_kernel, width=width),
        grid=(rows // ROW_TILE,),
        in_specs=[pl.BlockSpec((width, ROW_TILE), lambda i: (0, i))] * 4
        + [whole(a) for a in (matrix, *outs)]
        + [block, whole(params)],
        out_specs=(block, block, block, pl.BlockSpec((ROW_TILE, 1), lambda i: (i, 0))),
        scratch_shapes=[pltpu.VMEM((features, 4 * width), jnp.bfloat16)],
        out_shape=(shape(jnp.float32), shape(jnp.bfloat16), shape(jnp.float32), jax.ShapeDtypeStruct((rows, 1), jnp.float32)),
        compiler_params=pltpu.CompilerParams(vmem_limit_bytes=60 << 20),
        cost_estimate=pl.CostEstimate(
            flops=2 * rows * features * features, bytes_accessed=14 * rows * features + 2 * features * features, transcendentals=rows
        ),
        name="mix_fwd",
    )(*heads, matrix, *outs, own, params)


def mix_bwd_kernel(
    grad_mixed, own_part, far_part, normed, inv, params, head0, head1, head2, head3, matrix, out1, out2, out3,
    grad_out, norms, made0, made1, made2, made3, og0, og1, og2, og3, turned, total, *, width,
):
    step = pl.program_id(0)

    @pl.when(step == 0)
    def _():
        for i, weight in enumerate((matrix[:, 3 * width :], out1[...], out2[...], out3[...])):
            turned[i * width : (i + 1) * width, :] = weight.T
        total[...] = jnp.zeros_like(total)
        norms[...] = jnp.zeros_like(norms)

    grad = grad_mixed[...] + own_part[...] + far_part[...].astype(jnp.float32)
    unit = normed[...]
    norms[0:1, :] += jnp.sum(grad * unit, axis=0, keepdims=True)
    norms[1:2, :] += jnp.sum(grad, axis=0, keepdims=True)
    grad_unit = grad * params[0:1, :]
    back = inv[...] * (grad_unit - mean_of(grad_unit) - unit * mean_of(grad_unit * unit))
    grad_out[...] = back
    low = back.astype(jnp.bfloat16)
    made = lax.dot_general(turned[...], low, NT, preferred_element_type=jnp.float32).astype(jnp.bfloat16)
    for i, out in enumerate((made0, made1, made2, made3)):
        out[...] = made[i * width : (i + 1) * width]
    heads = jnp.concatenate([head0[...], head1[...], head2[...], head3[...]], axis=0)
    total[...] += jnp.dot(heads, low, preferred_element_type=jnp.float32)

    @pl.when(step == pl.num_programs(0) - 1)
    def _():
        for i, og in enumerate((og0, og1, og2, og3)):
            og[...] = total[i * width : (i + 1) * width, :].astype(jnp.bfloat16)


def mix_bwd(grad_mixed, own_part, far_part, normed, inv, params, heads, matrix, outs):
    width, rows = heads[0].shape
    features = matrix.shape[0]
    whole = lambda a: pl.BlockSpec(a.shape, lambda i: (0,) * len(a.shape))
    shapes = (
        [jax.ShapeDtypeStruct((rows, features), jnp.float32), jax.ShapeDtypeStruct((2, features), jnp.float32)]
        + [jax.ShapeDtypeStruct((width, rows), jnp.bfloat16)] * 4
        + [jax.ShapeDtypeStruct((width, features), jnp.bfloat16)] * 4
    )
    ops = (grad_mixed, own_part, far_part, normed, inv, params, *heads, matrix, *outs)
    block = pl.BlockSpec((ROW_TILE, features), lambda i: (i, 0))
    slab = pl.BlockSpec((width, ROW_TILE), lambda i: (0, i))
    got = pl.pallas_call(
        functools.partial(mix_bwd_kernel, width=width),
        grid=(rows // ROW_TILE,),
        in_specs=[block] * 4
        + [pl.BlockSpec((ROW_TILE, 1), lambda i: (i, 0)), whole(params)]
        + [slab] * 4
        + [whole(a) for a in (matrix, *outs)],
        out_specs=(block, whole(shapes[1]), *[slab] * 4, *[whole(a) for a in shapes[6:]]),
        out_shape=tuple(shapes),
        scratch_shapes=[pltpu.VMEM((4 * width, features), jnp.bfloat16), pltpu.VMEM((4 * width, features), jnp.float32)],
        compiler_params=pltpu.CompilerParams(vmem_limit_bytes=60 << 20),
        cost_estimate=pl.CostEstimate(
            flops=4 * rows * features * features, bytes_accessed=22 * rows * features + 4 * features * features, transcendentals=0
        ),
        name="mix_bwd",
    )(*ops)
    return got[0], got[1], got[2:6], got[6:10]


def top_bwd_kernel(first, second, third, fourth, normed, inv, gain, low_in, back, low, norms):
    grad = first[...].astype(jnp.float32)
    for part in (second, third, fourth):
        if part is not None:
            grad += part[...].astype(jnp.float32)
    if low_in is not None:
        low_in[...] = grad.astype(jnp.bfloat16)
        grad = grad.astype(jnp.bfloat16).astype(jnp.float32)
    unit = normed[...]

    @pl.when(pl.program_id(0) == 0)
    def _():
        norms[...] = jnp.zeros_like(norms)

    norms[0:1, :] += jnp.sum(grad * unit, axis=0, keepdims=True)
    norms[1:2, :] += jnp.sum(grad, axis=0, keepdims=True)
    grad_unit = grad * gain[...]
    out = inv[...] * (grad_unit - mean_of(grad_unit) - unit * mean_of(grad_unit * unit))
    back[...] = out
    low[...] = out.astype(jnp.bfloat16)


def top_bwd(parts, normed, inv, gain):
    rows, features = normed.shape
    several = len(parts) > 1
    whole = lambda a: pl.BlockSpec(a.shape, lambda i: (0,) * len(a.shape))
    shape = lambda t: jax.ShapeDtypeStruct((rows, features), t)
    shapes = [shape(jnp.bfloat16)] * several + [shape(jnp.float32), shape(jnp.bfloat16)]
    shapes.append(jax.ShapeDtypeStruct((2, features), jnp.float32))
    ops = (*parts, normed, inv, gain)
    block = pl.BlockSpec((ROW_TILE, features), lambda i: (i, 0))

    def kernel(*refs):
        ins, outs = refs[: len(ops)], refs[len(ops) :]
        four = list(ins[: len(parts)]) + [None] * (4 - len(parts))
        top_bwd_kernel(*four, *ins[len(parts) :], *((None,) * (not several)), *outs)

    got = pl.pallas_call(
        kernel,
        grid=(rows // ROW_TILE,),
        in_specs=[block] * (len(parts) + 1) + [pl.BlockSpec((ROW_TILE, 1), lambda i: (i, 0)), whole(gain)],
        out_specs=(*[block] * (len(shapes) - 1), whole(shapes[-1])),
        out_shape=tuple(shapes),
        compiler_params=pltpu.CompilerParams(vmem_limit_bytes=60 << 20),
        cost_estimate=pl.CostEstimate(flops=12 * rows * features, bytes_accessed=18 * rows * features, transcendentals=0),
        name="top_bwd",
    )(*ops)
    return tuple(got) if several else (None, *got)


def lamb_step(weight, gradient, first_old, second):
    first_new = BETA_ONE * first_old + (1.0 - BETA_ONE) * gradient
    second_new = BETA_TWO * second + (1.0 - BETA_TWO) * gradient * gradient
    update = (
        first_new
        / (1.0 - BETA_ONE**STEP)
        / (jnp.sqrt(second_new / (1.0 - BETA_TWO**STEP)) + ADAM_EPS)
        + DECAY_RATE * weight
    )
    return first_new, second_new, update


def lamb_kernel(*refs, kinds, shards):
    count = len(kinds)
    made, refs = refs[:shards], refs[shards:]
    olds, news, late = refs[: 3 * count], refs[3 * count : 6 * count], refs[6 * count]
    late[...] = jnp.zeros_like(late)
    for i, (turned, parts) in enumerate(kinds):
        weight, first, second = olds[3 * i : 3 * i + 3]
        first_out, second_out, update_out = news[3 * i : 3 * i + 3]
        row = None
        for at, (index, columns) in enumerate(parts):
            gradient = sum(shard[index, :, columns].astype(jnp.float32) for shard in made)
            gradient = gradient.T if turned else gradient
            where = (at,) if len(weight.shape) == 3 else (slice(None),)
            first_new, second_new, update = lamb_step(weight[where], gradient, first[where], second[where])
            first_out[where] = first_new
            second_out[where] = second_new
            update_out[where] = update
            sums = jnp.sum(update * update, axis=0, keepdims=True)
            row = sums if row is None else row + sums
        late[i : i + 1, : row.shape[1]] = row


def lamb(made, kinds, olds, features):
    whole = lambda a: pl.BlockSpec(a.shape, lambda i: (0,) * len(a.shape))
    shapes = [jax.ShapeDtypeStruct(a.shape, jnp.float32) for a in olds]
    shapes.append(jax.ShapeDtypeStruct((len(kinds), features), jnp.float32))
    ops = (*made, *olds)
    return pl.pallas_call(
        functools.partial(lamb_kernel, kinds=kinds, shards=len(made)),
        grid=(1,),
        in_specs=[whole(a) for a in ops],
        out_specs=tuple(whole(a) for a in shapes),
        out_shape=tuple(shapes),
        compiler_params=pltpu.CompilerParams(vmem_limit_bytes=60 << 20),
        cost_estimate=pl.CostEstimate(flops=20 * made[0].size, bytes_accessed=28 * made[0].size, transcendentals=made[0].size),
        name="lamb",
    )(*ops)


def finish_kernel(totals, now, first, second, *refs, count):
    weights, updates = refs[:count], refs[count : 2 * count]
    norm_out, first_out, second_out, trust = refs[2 * count : 2 * count + 4]
    news = refs[2 * count + 4 :]
    for i in range(2):
        first_new, second_new, update = lamb_step(now[i], totals[2 * i : 2 * i + 2, :], first[i], second[i])
        norms = [jnp.sqrt(jnp.sum(v * v, axis=-1, keepdims=True)) for v in (now[i], update)]
        norm_out[i] = now[i] - LEARN_RATE * (norms[0] / norms[1]) * update
        first_out[i] = first_new
        second_out[i] = second_new
    sizes = jnp.sqrt(jnp.sum(totals[4:12, :], axis=-1, keepdims=True))
    trust[...] = jnp.concatenate([sizes[0:4], sizes[4:8]], axis=1).T
    for i in range(count):
        ratio = LEARN_RATE * (sizes[i : i + 1] / sizes[4 + i : 5 + i])
        for at in range(weights[i].shape[0]) if len(weights[i].shape) == 3 else (slice(None),):
            news[i][at] = weights[i][at] - ratio * updates[i][at]


def finish(totals, now, first, second, weights, updates):
    whole = lambda a: pl.BlockSpec(a.shape, lambda i: (0,) * len(a.shape))
    shapes = [jax.ShapeDtypeStruct(now.shape, jnp.float32)] * 3 + [jax.ShapeDtypeStruct((2, 4), jnp.float32)]
    shapes += [jax.ShapeDtypeStruct(a.shape, jnp.float32) for a in weights]
    ops = (totals, now, first, second, *weights, *updates)
    size = sum(a.size for a in weights)
    return pl.pallas_call(
        functools.partial(finish_kernel, count=len(weights)),
        grid=(1,),
        in_specs=[whole(a) for a in ops],
        out_specs=tuple(whole(a) for a in shapes),
        out_shape=tuple(shapes),
        compiler_params=pltpu.CompilerParams(vmem_limit_bytes=60 << 20),
        cost_estimate=pl.CostEstimate(flops=3 * size, bytes_accessed=12 * size, transcendentals=0),
        name="finish",
    )(*ops)


STEP = 10

BETA_ONE = 0.9
BETA_TWO = 0.999
ADAM_EPS = 1e-06
DECAY_RATE = 0.01
LEARN_RATE = 0.2
NORM_EPS = 1e-05
ROPE_BASE = 1000.0

bf16 = jnp.bfloat16
f32 = jnp.float32

BOTH = ("section", "tensor")
CELLS = [(c, y, x) for c in range(2) for y in range(2) for x in range(2)]


def number(c, y, x):
    return c * 4 + y * 2 + x


def moves(target):
    return [(number(*cell), number(*target(*cell))) for cell in CELLS]


SWAP = moves(lambda c, y, x: (y, c, x))
SWAP_BACK = moves(lambda c, y, x: (1 - y, c, x))
SWAP_OUT = moves(lambda c, y, x: (y, 1 - c, x))
CORNER = moves(lambda c, y, x: (1 - c, y, 1 - x))


def over_section(v):
    return lax.ppermute(v, "section", [(0, 1), (1, 0)])


def over_x(v):
    return lax.ppermute(v, "tensor", [(0, 1), (1, 0), (2, 3), (3, 2)])


def over_y(v):
    return lax.ppermute(v, "tensor", [(0, 2), (1, 3), (2, 0), (3, 1)])


def over_diag(v):
    return lax.ppermute(v, "tensor", [(0, 3), (1, 2), (2, 1), (3, 0)])


def over_both(v, pairs):
    return lax.ppermute(v, BOTH, pairs)


def over_z(v, k):
    return lax.ppermute(v, "dp", [(i, i ^ k) for i in range(4)])


def quad():
    return lax.axis_size("dp") == 4


def gather_later(piece, axis):
    return lax.all_gather(piece, "dp", axis=axis, tiled=True)


def scatter_later(whole, axis):
    return lax.psum_scatter(whole, "dp", scatter_dimension=axis, tiled=True)


def to_owner(shard, layer):
    same = [pair for pair in SWAP if pair[1] // 4 == layer]
    other = [pair for pair in SWAP_BACK if pair[1] // 4 == layer]
    return over_both(shard, same), over_both(shard, other)


def chips_total(v):
    v = (v + over_x(v)) + (over_y(v) + over_diag(v))
    if not quad():
        return lax.psum(v, "dp")
    return (v + over_z(v, 1)) + (over_z(v, 2) + over_z(v, 3))


def rope_tables(length):
    half_size = HEAD // 2
    freq_vals = np.float32(ROPE_BASE) ** (-np.arange(half_size, dtype=np.float32) * np.float32(2.0 / HEAD))
    angles = freq_vals[:, None] * np.arange(length, dtype=np.float32)[None, :]
    return jnp.asarray(np.cos(angles)), jnp.asarray(np.sin(angles))


def norm_fwd(values, gain_row, bias_row):
    mean_val = jnp.mean(values, axis=-1, keepdims=True)
    centred = values - mean_val
    variance = jnp.mean(centred * centred, axis=-1, keepdims=True)
    inv_std = lax.rsqrt(variance + NORM_EPS)
    normed = centred * inv_std
    return (normed * gain_row + bias_row, normed, inv_std)


def dot(spec, a, b):
    return jnp.einsum(spec, a, b, preferred_element_type=f32)


def after(value, *others):
    return lax.optimization_barrier((value,) + others)[0]


def layer_forward(slabs, matrix, ffn, params, env, late):
    place, ends, cos, sin = env
    *mine, log_sums, qkv = attn_fwd(place, ends, slabs, matrix, cos, sin)
    out_own = matrix[:, 3 * (matrix.shape[1] // 4) :]
    out_across = over_x(out_own)
    outs = (over_section(out_own), out_across, over_section(after(out_across, log_sums)))
    all_heads = [mine[0], over_section(mine[1]), over_x(mine[2]), over_both(mine[3], CORNER)]
    hidden, hidden_low, normed_one, inv_one = mix_fwd(all_heads, matrix, outs, slabs[0], params[:, 0])
    hidden_rows = [hidden_low, over_x(hidden_low)]
    ffn = (ffn, over_section(after(ffn, hidden_rows[late])))
    own_part, *own_acts = ffn_fwd(hidden_rows[0], *ffn, f32)
    far_part, *far_acts = ffn_fwd(hidden_rows[1], *ffn, bf16)
    ffn_out = own_part + over_x(far_part).astype(f32)
    output, normed_two, inv_two = norm_fwd(hidden + ffn_out, params[0, 1], params[1, 1])
    kept = (slabs, qkv, mine, log_sums, all_heads, normed_one, inv_one, hidden_rows, (own_acts, far_acts))
    return output.astype(bf16), outs, kept + (normed_two, inv_two, ffn)


def layer_backward(grad_parts, kept, matrix, outs, params, env, early=(), late=()):
    place, ends, cos, sin = env
    (slabs, qkv, mine, log_sums, all_heads, normed_one, inv_one, hidden_rows, acts, normed_two, inv_two, ffn) = kept
    sent, grad_mixed, grad_low, norm_two = top_bwd(grad_parts, normed_two, inv_two, params[0, 1:2])
    grad_rows = [grad_low, over_x(grad_low)]
    own_part, *own_grads = ffn_bwd(grad_rows[0], *acts[0], *ffn, f32)
    far_part, *far_grads = ffn_bwd(after(grad_rows[1], own_part, *early), *acts[1], *ffn, bf16)
    made = list(zip(own_grads, far_grads))
    ffn_other = ffn_grads(1, hidden_rows, grad_rows, *made)
    ffn_grad = ffn_grads(0, hidden_rows, grad_rows, *made, over_section(ffn_other))
    far_part = over_x(far_part)
    ffn_grad = after(ffn_grad, far_part)
    grad_mixed_one, norm_one, grad_heads, out_grad = mix_bwd(
        grad_mixed, own_part, far_part, normed_one, inv_one, params[:, 0], all_heads, matrix, outs
    )
    grad_mine = (
        grad_heads[0], over_section(grad_heads[1]), over_x(grad_heads[2]), over_both(grad_heads[3], CORNER)
    )
    *out_grad, _ = lax.optimization_barrier((*out_grad, grad_mine))
    out_own = (out_grad[0], over_section(out_grad[1]), over_x(out_grad[2]), over_both(out_grad[3], CORNER))
    grad_proj = attn_bwd(place, ends, qkv, grad_mine, mine, log_sums, cos, sin)
    out_own = sum(g.astype(f32) for g in after(out_own, grad_proj, *late))
    part3, part1, part2, part0, matrix_grad = proj_bwd(grad_proj, slabs, matrix, out_own)
    far_sum = over_x((part2.astype(f32) + over_section(part3).astype(f32)).astype(bf16))
    norm_grads = jnp.stack([jnp.stack([norm_one[0], norm_two[0]]), jnp.stack([norm_one[1], norm_two[1]])])
    return sent, (grad_mixed_one, part0, over_section(part1), far_sum), matrix_grad, ffn_grad, norm_grads


def body(
    tokens,
    cotangent,
    segments,
    heads_in,
    heads_out,
    gate_up,
    project_down,
    norm_gain,
    norm_bias,
    heads_in_first,
    heads_in_second,
    heads_out_first,
    heads_out_second,
    gate_up_first,
    gate_up_second,
    project_down_first,
    project_down_second,
    norm_first,
    norm_second,
):
    section = lax.axis_index("section")
    spot = lax.axis_index("tensor")
    y, x = spot // 2, spot % 2
    rows = tokens.shape[1]
    length = segments.shape[-1]
    masters = (heads_in[0], heads_out[0], gate_up[0], project_down[0].T)
    deep, width = masters[0].shape[1:]

    attn_piece = jnp.concatenate(
        [masters[0].transpose(1, 0, 2).reshape(deep, 3 * width), masters[1].T], axis=1
    ).astype(bf16)
    ffn_piece = jnp.concatenate([masters[2], masters[3][None]], axis=0).astype(bf16)

    def to_block(piece, layer):
        got = []
        for to_y in range(2):
            pairs = [(number(layer, c, x), number(c, to_y, x)) for c in range(2) for x in range(2)]
            got.append(over_both(piece, pairs))
        return got

    def for_y(got):
        return jnp.where(y == 0, got[0], got[1])

    def four_slabs(rows, *along):
        across, *along = lax.optimization_barrier((over_x(rows), *along))
        return (rows, over_section(rows), across, over_section(across)), along

    own = over_both(lax.dynamic_index_in_dim(tokens, section, 0, keepdims=False), SWAP)
    first_matrix = gather_later(for_y(to_block(attn_piece, 0)), 0)
    slabs_zero, ffn_pieces = four_slabs(own, *to_block(after(ffn_piece, own), 0))
    ffn_first = gather_later(for_y(ffn_pieces), 1)

    both_params = jnp.stack([norm_gain[0], norm_bias[0]])
    other_params = over_section(both_params)
    params = [
        jnp.where(section == 0, both_params, other_params),
        jnp.where(section == 0, other_params, both_params),
    ]

    block = 2 * section + x
    place = jnp.stack([block, block ^ 2, block ^ 1, block ^ 3]).astype(jnp.int32)
    seq_seg = lax.dynamic_index_in_dim(segments, y, 0, keepdims=False)[0]
    ends = jnp.stack([jnp.sum((seq_seg <= d).astype(jnp.int32)) for d in range(2)])
    env = (place, ends) + rope_tables(length)

    low_zero, outs_zero, kept_zero = layer_forward(slabs_zero, first_matrix, ffn_first, params[0], env, 1)
    hidden_rows = kept_zero[7]
    second_piece = for_y(to_block(after(jnp.concatenate([attn_piece[None], ffn_piece]), slabs_zero[3]), 1))
    second_matrix = gather_later(after(second_piece[0], hidden_rows[0]), 0)
    ffn_second = gather_later(after(second_piece[1:], hidden_rows[1]), 1)
    slabs_one, _ = four_slabs(low_zero)
    low_one, outs_one, kept_one = layer_forward(slabs_one, second_matrix, ffn_second, params[1], env, 0)
    grad_top = over_both(after(lax.dynamic_index_in_dim(cotangent, section, 0, keepdims=False), low_zero), SWAP)
    def home(zero, one):
        same = over_both(jnp.where(y == 0, zero, one), SWAP)
        other = over_both(jnp.where(y == 0, one, zero), SWAP_BACK)
        return same, other

    def by_micro(same, other):
        return jnp.stack([jnp.where(section == 0, same, other), jnp.where(section == 0, other, same)])

    layer_home = home(low_zero, low_one)
    layer_out = by_micro(*layer_home)
    _, grads_one, matrix_one, ffn_one, norm_one = layer_backward(
        (grad_top,), kept_one, second_matrix, outs_one, params[1], env, layer_home
    )
    ffn_one = to_owner(scatter_later(ffn_one, 1), 1)
    matrix_one = to_owner(scatter_later(matrix_one, 0)[None], 1)
    sent, grads_zero, matrix_zero, ffn_zero, norm_zero = layer_backward(
        grads_one, kept_zero, first_matrix, outs_zero, params[0], env, ffn_one, matrix_one
    )
    ffn_home = to_owner(scatter_later(ffn_zero, 1), 0) + ffn_one
    attn_home = to_owner(scatter_later(matrix_zero, 0)[None], 0)
    grad_zero = sum(g.astype(f32) for g in grads_zero)


    norm_mine = jnp.where(section == 0, norm_zero, norm_one) + over_section(
        jnp.where(section == 0, norm_one, norm_zero)
    )
    features = norm_mine.shape[-1]
    firsts = (heads_in_first[0], heads_out_first[0], gate_up_first[0], project_down_first[0].T)
    seconds = (heads_in_second[0], heads_out_second[0], gate_up_second[0], project_down_second[0].T)
    olds = list(zip(masters, firsts, seconds))

    def squares(matrix):
        row = jnp.sum((matrix * matrix).reshape(-1, matrix.shape[-1]), axis=0)
        return jnp.pad(row, (0, features - row.shape[0]))

    columns = slice(0, masters[2].shape[-1])
    ffn_new = lamb(
        ffn_home, ((False, ((0, columns), (1, columns))), (False, ((2, columns),))), olds[2] + olds[3], features
    )
    early = jnp.stack([squares(m) for m in masters])
    early = jnp.concatenate([norm_mine.reshape(4, -1), early], axis=0)
    attn_home = lax.optimization_barrier((*attn_home, early, ffn_new[-1]))[:2] + matrix_one
    pieces = tuple((0, slice(i * width, (i + 1) * width)) for i in range(4))
    attn_new = lamb(attn_home, ((False, pieces[:3]), (True, pieces[3:])), olds[0] + olds[1], features)
    totals = chips_total(jnp.concatenate([early, attn_new[-1], ffn_new[-1]], axis=0))
    made = [attn_new[:3], attn_new[3:6], ffn_new[:3], ffn_new[3:6]]
    *norms, trust_norms, in_new, out_new, gate_new, down_new = finish(
        totals, both_params, norm_first[0], norm_second[0], masters, [m[2] for m in made]
    )
    new_mats = (in_new, out_new, gate_new, down_new.T)
    made[3] = [v.T for v in made[3]]
    input_grads = by_micro(*home(after(grad_zero.astype(bf16), attn_home[0]), sent)).astype(f32)
    outs = [layer_out, input_grads]
    for i in range(4):
        outs += [new_mats[i], made[i][0], made[i][1]]
    outs += [*norms, trust_norms.T]
    return tuple(item[None] for item in outs)


def solution(mesh):
    rows = P(None, ("dp", "tensor"), None)
    out_rows = P("section", None, ("dp", "tensor"), None)
    columns = P("section", None, "dp", "tensor")
    turned = P("section", "tensor", "dp")
    vectors = P("section", None, None)
    pairs = P("section", None, None, None)
    return jax.shard_map(
        body,
        mesh=mesh,
        in_specs=(rows, rows, P(None, "dp", None), columns, turned, columns, turned, vectors, vectors)
        + (columns, columns, turned, turned, columns, columns, turned, turned, pairs, pairs),
        out_specs=(out_rows, out_rows)
        + (columns,) * 3
        + (turned,) * 3
        + (columns,) * 3
        + (turned,) * 3
        + (pairs,) * 3
        + (vectors,),
        check_vma=False,
    )
```

```python
import functools

import jax
import jax.numpy as jnp
import numpy as np
from jax import lax
from jax.experimental import pallas as pl
from jax.experimental.pallas import tpu as pltpu
from jax.sharding import PartitionSpec as P

HEAD = 64
FQ, FK = 512, 512
BQ, BK = 256, 512
SAFE = 40.0
WINDOW = 1024


def doc_bounds(pos, ends, length):
    start = jnp.where(pos < ends[0], 0, jnp.where(pos < ends[1], ends[0], ends[1]))
    last = jnp.where(pos < ends[0], ends[0], jnp.where(pos < ends[1], ends[1], length)) - 1
    return jnp.maximum(start, pos - (WINDOW - 1)), jnp.minimum(last, pos + (WINDOW - 1))


def key_span(q_start, rows, ends, length, deep):
    low, _ = doc_bounds(q_start, ends, length)
    _, high = doc_bounds(q_start + rows - 1, ends, length)
    first = low // 128 * 128
    tiles = (high + 1 - first + deep - 1) // deep
    return jnp.minimum(first, length - tiles * deep), tiles


def attn_fwd_kernel(place, ends, slab0, slab1, slab2, slab3, matrix, cos, sin, out0, out1, out2, out3, lse, qkv, a_t, k_n, o_t, calm, *, heads):
    step = pl.program_id(0)
    width = heads * HEAD
    half = HEAD // 2
    length = qkv.shape[1]
    rows = length // 4

    @pl.when(step == 0)
    def _():
        a_t[...] = matrix[:, : 3 * width].T
        tops = [jnp.zeros((1, rows), jnp.float32) for _ in range(2 * heads)]
        for slab, src in enumerate((slab0, slab1, slab2, slab3)):
            start = pl.multiple_of(place[slab] * rows, rows)
            here = pl.ds(start, rows)
            proj = lax.dot_general(a_t[...], src[...], (((1,), (1,)), ((), ())), preferred_element_type=jnp.float32)
            c, s = cos[:, here], sin[:, here]
            for i in range(2 * heads):
                first, second = proj[i * HEAD : i * HEAD + half], proj[i * HEAD + half : (i + 1) * HEAD]
                turned = jnp.concatenate([first * c - second * s, second * c + first * s], axis=0).astype(jnp.bfloat16)
                if i < heads:
                    turned = turned * jnp.bfloat16(HEAD**-0.5)
                else:
                    k_n[i - heads, here, :] = turned.T
                qkv[i * HEAD : (i + 1) * HEAD, here] = turned
                size = turned.astype(jnp.float32)
                tops[i] = jnp.maximum(tops[i], jnp.sum(size * size, axis=0, keepdims=True))
            qkv[2 * width :, here] = proj[2 * width :].astype(jnp.bfloat16)
        worst = jnp.float32(0.0)
        for h in range(heads):
            worst = jnp.maximum(worst, jnp.max(tops[h]) * jnp.max(tops[heads + h]))
        calm[0] = (worst <= SAFE * SAFE).astype(jnp.int32)

    q_start = pl.multiple_of(step * FQ, FQ)
    here = pl.ds(q_start, FQ)
    low, high = doc_bounds(q_start + lax.broadcasted_iota(jnp.int32, (1, FQ), 1), (ends[0], ends[1]), length)
    first, tiles = key_span(q_start, FQ, (ends[0], ends[1]), length, FK)

    def score(h, keys):
        return jnp.dot(k_n[h, keys, :], qkv[h * HEAD : (h + 1) * HEAD, here], preferred_element_type=jnp.float32)

    def weigh(h, keys, p):
        return jnp.dot(
            qkv[2 * width + h * HEAD : 2 * width + (h + 1) * HEAD, keys], p.astype(jnp.bfloat16),
            preferred_element_type=jnp.float32,
        )

    def mask(t):
        k_start = pl.multiple_of(first + t * FK, 128)
        pos = k_start + lax.broadcasted_iota(jnp.int32, (FK, FQ), 0)
        return pl.ds(k_start, FK), (pos >= low) & (pos <= high)

    def finish(h, total, acc, log_sum):
        o_t[h * HEAD : (h + 1) * HEAD, here] = (acc / total).astype(jnp.bfloat16)
        lse[h : h + 1, here] = log_sum

    @pl.when(calm[0] == 1)
    def _():
        def tile(t, carry):
            keys, allowed = mask(t)
            new = []
            nxt = score(0, keys)
            for h in range(heads):
                total, acc = carry[h]
                s = nxt
                if h + 1 < heads:
                    nxt = score(h + 1, keys)
                p = jnp.where(allowed, jnp.exp(s), 0.0)
                new.append((total + jnp.sum(p, axis=0, keepdims=True), acc + weigh(h, keys, p)))
            return tuple(new)

        init = tuple((jnp.zeros((1, FQ), jnp.float32), jnp.zeros((HEAD, FQ), jnp.float32)) for _ in range(heads))
        for h, (total, acc) in enumerate(lax.fori_loop(0, tiles, tile, init)):
            finish(h, total, acc, jnp.log(total))

    @pl.when(calm[0] == 0)
    def _():
        def tile(t, carry):
            keys, allowed = mask(t)
            new = []
            for h in range(heads):
                top, total, acc = carry[h]
                s = jnp.where(allowed, score(h, keys), -1e30)
                new_top = jnp.maximum(top, jnp.max(s, axis=0, keepdims=True))
                p = jnp.exp(s - new_top)
                alpha = jnp.exp(top - new_top)
                total = total * alpha + jnp.sum(p, axis=0, keepdims=True)
                new.append((new_top, total, acc * alpha + weigh(h, keys, p)))
            return tuple(new)

        init = tuple(
            (jnp.full((1, FQ), -1e30, jnp.float32), jnp.zeros((1, FQ), jnp.float32), jnp.zeros((HEAD, FQ), jnp.float32))
            for _ in range(heads)
        )
        for h, (top, total, acc) in enumerate(lax.fori_loop(0, tiles, tile, init)):
            finish(h, total, acc, top + jnp.log(total))

    @pl.when(step == pl.num_programs(0) - 1)
    def _():
        for slab, out in enumerate((out0, out1, out2, out3)):
            out[...] = o_t[:, pl.ds(pl.multiple_of(place[slab] * rows, rows), rows)]


def whole_spec(a):
    return pl.BlockSpec(a.shape, lambda i: (0,) * len(a.shape))


def attn_fwd(place, ends, slabs, matrix, cos, sin):
    rows = slabs[0].shape[0]
    length = 4 * rows
    width = matrix.shape[1] // 4
    heads = width // HEAD
    smem = pl.BlockSpec(memory_space=pltpu.SMEM)
    ops = (*slabs, matrix, cos, sin)
    outs = (
        *[jax.ShapeDtypeStruct((width, rows), jnp.bfloat16)] * 4,
        jax.ShapeDtypeStruct((heads, length), jnp.float32),
        jax.ShapeDtypeStruct((3 * width, length), jnp.bfloat16),
    )
    return pl.pallas_call(
        functools.partial(attn_fwd_kernel, heads=heads),
        grid=(length // FQ,),
        in_specs=[smem, smem] + [whole_spec(a) for a in ops],
        out_specs=tuple(whole_spec(o) for o in outs),
        out_shape=outs,
        scratch_shapes=[
            pltpu.VMEM((3 * width, matrix.shape[0]), jnp.bfloat16),
            pltpu.VMEM((heads, length, HEAD), jnp.bfloat16),
            pltpu.VMEM((width, length), jnp.bfloat16),
            pltpu.SMEM((1,), jnp.int32),
        ],
        compiler_params=pltpu.CompilerParams(vmem_limit_bytes=48 << 20),
        cost_estimate=pl.CostEstimate(
            flops=6 * length * length * width, bytes_accessed=16 * length * width, transcendentals=heads * length * length
        ),
        name="attn_fwd",
    )(place, ends, *ops)


def attn_bwd_kernel(place, ends, qkv, do0, do1, do2, do3, out0, out1, out2, out3, lse, cos, sin, dproj, q_n, k_n, v_n, do_t, do_n, delta, dq_t, dk, dv, *, heads):
    step = pl.program_id(0)
    width = heads * HEAD
    length = qkv.shape[1]
    rows = length // 4
    half = HEAD // 2

    @pl.when(step == 0)
    def _():
        for slab, (dout, out) in enumerate(((do0, out0), (do1, out1), (do2, out2), (do3, out3))):
            start = pl.multiple_of(place[slab] * rows, rows)
            do_t[:, pl.ds(start, rows)] = dout[...]
            prod = dout[...].astype(jnp.float32) * out[...].astype(jnp.float32)
            for h in range(heads):
                piece = slice(h * HEAD, (h + 1) * HEAD)
                delta[h : h + 1, pl.ds(start, rows)] = jnp.sum(prod[piece], axis=0, keepdims=True)
                do_n[h, pl.ds(start, rows), :] = dout[piece, :].T
        for h in range(heads):
            q_n[h] = qkv[h * HEAD : (h + 1) * HEAD, :].T
            k_n[h] = qkv[width + h * HEAD : width + (h + 1) * HEAD, :].T
            v_n[h] = qkv[2 * width + h * HEAD : 2 * width + (h + 1) * HEAD, :].T
        dk[...] = jnp.zeros_like(dk)
        dv[...] = jnp.zeros_like(dv)

    q_start = pl.multiple_of(step * BQ, BQ)
    qs = pl.ds(q_start, BQ)
    low, high = doc_bounds(q_start + lax.broadcasted_iota(jnp.int32, (1, BQ), 1), (ends[0], ends[1]), length)
    first, tiles = key_span(q_start, BQ, (ends[0], ends[1]), length, BK)

    def tile(t, carry):
        k_start = pl.multiple_of(first + t * BK, 128)
        ks = pl.ds(k_start, BK)
        pos = k_start + lax.broadcasted_iota(jnp.int32, (BK, BQ), 0)
        allowed = (pos >= low) & (pos <= high)
        new = []

        def score(h):
            piece = slice(h * HEAD, (h + 1) * HEAD)
            return (
                jnp.dot(k_n[h, ks, :], qkv[piece, qs], preferred_element_type=jnp.float32),
                jnp.dot(v_n[h, ks, :], do_t[piece, qs], preferred_element_type=jnp.float32),
            )

        nxt = score(0)
        for h in range(heads):
            s, dp = nxt
            if h + 1 < heads:
                nxt = score(h + 1)
            p = jnp.where(allowed, jnp.exp(s - lse[h : h + 1, qs]), 0.0)
            ds = (p * (dp - delta[h : h + 1, qs])).astype(jnp.bfloat16)
            dv[h, ks, :] += jnp.dot(p.astype(jnp.bfloat16), do_n[h, qs, :], preferred_element_type=jnp.float32)
            dk[h, ks, :] += jnp.dot(ds, q_n[h, qs, :], preferred_element_type=jnp.float32)
            new.append(carry[h] + jnp.dot(qkv[width + h * HEAD : width + (h + 1) * HEAD, ks], ds, preferred_element_type=jnp.float32))
        return tuple(new)

    init = tuple(jnp.zeros((HEAD, BQ), jnp.float32) for _ in range(heads))
    done = lax.fori_loop(0, tiles, tile, init)
    for h in range(heads):
        dq_t[h * HEAD : (h + 1) * HEAD, qs] = done[h]

    @pl.when(step == pl.num_programs(0) - 1)
    def _():
        for slab in range(4):
            start = pl.multiple_of(place[slab] * rows, rows)
            c, s = cos[:, pl.ds(start, rows)], sin[:, pl.ds(start, rows)]
            for h in range(heads):
                gq = dq_t[h * HEAD : (h + 1) * HEAD, pl.ds(start, rows)] * HEAD**-0.5
                gk = dk[h, pl.ds(start, rows), :].T
                gv = dv[h, pl.ds(start, rows), :].T
                for kind, g in ((0, gq), (1, gk)):
                    g1, g2 = g[:half], g[half:]
                    at = kind * width + h * HEAD
                    dproj[slab, at : at + half, :] = (g1 * c + g2 * s).astype(jnp.bfloat16)
                    dproj[slab, at + half : at + HEAD, :] = (g2 * c - g1 * s).astype(jnp.bfloat16)
                at = 2 * width + h * HEAD
                dproj[slab, at : at + HEAD, :] = gv.astype(jnp.bfloat16)


def attn_bwd(place, ends, qkv, douts, outs, lse, cos, sin):
    length = qkv.shape[1]
    rows = length // 4
    width = qkv.shape[0] // 3
    heads = width // HEAD
    smem = pl.BlockSpec(memory_space=pltpu.SMEM)
    ops = (qkv, *douts, *outs, lse, cos, sin)
    natural = pltpu.VMEM((heads, length, HEAD), jnp.bfloat16)
    sums = pltpu.VMEM((heads, length, HEAD), jnp.float32)
    return pl.pallas_call(
        functools.partial(attn_bwd_kernel, heads=heads),
        grid=(length // BQ,),
        in_specs=[smem, smem] + [whole_spec(a) for a in ops],
        out_specs=pl.BlockSpec((4, 3 * width, rows), lambda i: (0, 0, 0)),
        out_shape=jax.ShapeDtypeStruct((4, 3 * width, rows), jnp.bfloat16),
        scratch_shapes=[natural, natural, natural, pltpu.VMEM((width, length), jnp.bfloat16), natural]
        + [pltpu.VMEM((heads, length), jnp.float32), pltpu.VMEM((width, length), jnp.float32), sums, sums],
        compiler_params=pltpu.CompilerParams(vmem_limit_bytes=56 << 20),
        cost_estimate=pl.CostEstimate(
            flops=10 * length * length * width, bytes_accessed=24 * length * width, transcendentals=heads * length * length
        ),
        name="attn_bwd",
    )(place, ends, *ops)


FT = 768


def ffn_specs(rows, deep, hidden, step_tiles):
    first = pl.BlockSpec((3, deep, FT), lambda b, j: (0, 0, jnp.where(b == 0, j, step_tiles - 1)))
    second = pl.BlockSpec((3, deep, FT), lambda b, j: (0, 0, jnp.where(b == 0, 0, j)))
    acts = pl.BlockSpec((1, rows, FT), lambda b, j: (b, 0, j))
    whole = pl.BlockSpec((rows, deep), lambda b, j: (0, 0))
    return first, second, acts, whole


NT = (((1,), (1,)), ((), ()))


def ffn_fwd_kernel(rows_ref, first, second, out, gate_out, up_out, total):
    b, j = pl.program_id(0), pl.program_id(1)

    def work(block, fresh):
        h = rows_ref[...]
        gate = jnp.dot(h, block[0], preferred_element_type=jnp.float32)
        up = jnp.dot(h, block[1], preferred_element_type=jnp.float32)
        gate_out[0] = gate.astype(jnp.bfloat16)
        up_out[0] = up.astype(jnp.bfloat16)
        inner = (gate / (1.0 + jnp.exp(-gate)) * up).astype(jnp.bfloat16)
        part = lax.dot_general(inner, block[2], NT, preferred_element_type=jnp.float32)
        total[...] = part if fresh else total[...] + part

    pl.when((b == 0) & (j == 0))(lambda: work(first, True))
    pl.when((b == 0) & (j > 0))(lambda: work(first, False))
    pl.when(b == 1)(lambda: work(second, False))

    @pl.when((b == 1) & (j == pl.num_programs(1) - 1))
    def _():
        out[...] = total[...].astype(out.dtype)


def ffn_fwd(rows, first, second, out_type):
    length, deep = rows.shape
    hidden = first.shape[2]
    tiles = hidden // FT
    w1, w2, acts, whole = ffn_specs(length, deep, hidden, tiles)
    act = jax.ShapeDtypeStruct((2, length, hidden), jnp.bfloat16)
    return pl.pallas_call(
        ffn_fwd_kernel,
        grid=(2, tiles),
        in_specs=[whole, w1, w2],
        out_specs=(whole, acts, acts),
        out_shape=(jax.ShapeDtypeStruct((length, deep), out_type), act, act),
        scratch_shapes=[pltpu.VMEM((length, deep), jnp.float32)],
        compiler_params=pltpu.CompilerParams(vmem_limit_bytes=32 << 20),
        cost_estimate=pl.CostEstimate(
            flops=12 * length * deep * hidden, bytes_accessed=12 * deep * hidden + 8 * length * hidden, transcendentals=2 * length * hidden
        ),
        name="ffn_fwd",
    )(rows, first, second)


def ffn_bwd_kernel(grad_ref, gate_ref, up_ref, first, second, out, grad_gate_out, grad_up_out, inner_out, total):
    b, j = pl.program_id(0), pl.program_id(1)

    def work(block, fresh):
        grad_inner = jnp.dot(grad_ref[...], block[2], preferred_element_type=jnp.float32)
        gate, up = gate_ref[0].astype(jnp.float32), up_ref[0].astype(jnp.float32)
        sig = 1.0 / (1.0 + jnp.exp(-gate))
        act = gate * sig
        grad_gate = (grad_inner * up * (sig + act * (1.0 - sig))).astype(jnp.bfloat16)
        grad_up = (grad_inner * act).astype(jnp.bfloat16)
        grad_gate_out[0] = grad_gate
        grad_up_out[0] = grad_up
        inner_out[0] = (act * up).astype(jnp.bfloat16)
        part = lax.dot_general(grad_gate, block[0], NT, preferred_element_type=jnp.float32)
        part += lax.dot_general(grad_up, block[1], NT, preferred_element_type=jnp.float32)
        total[...] = part if fresh else total[...] + part

    pl.when((b == 0) & (j == 0))(lambda: work(first, True))
    pl.when((b == 0) & (j > 0))(lambda: work(first, False))
    pl.when(b == 1)(lambda: work(second, False))

    @pl.when((b == 1) & (j == pl.num_programs(1) - 1))
    def _():
        out[...] = total[...].astype(out.dtype)


def ffn_bwd(grad, gate, up, first, second, out_type):
    length, deep = grad.shape
    hidden = first.shape[2]
    tiles = hidden // FT
    w1, w2, acts, whole = ffn_specs(length, deep, hidden, tiles)
    act = jax.ShapeDtypeStruct((2, length, hidden), jnp.bfloat16)
    return pl.pallas_call(
        ffn_bwd_kernel,
        grid=(2, tiles),
        in_specs=[whole, acts, acts, w1, w2],
        out_specs=(whole, acts, acts, acts),
        out_shape=(jax.ShapeDtypeStruct((length, deep), out_type), act, act, act),
        scratch_shapes=[pltpu.VMEM((length, deep), jnp.float32)],
        compiler_params=pltpu.CompilerParams(vmem_limit_bytes=32 << 20),
        cost_estimate=pl.CostEstimate(
            flops=12 * length * deep * hidden, bytes_accessed=12 * deep * hidden + 20 * length * hidden, transcendentals=2 * length * hidden
        ),
        name="ffn_bwd",
    )(grad, gate, up, first, second)


def ffn_grads_kernel(*refs, sets, other):
    rows, grads, gates, ups, inners = (refs[i * sets : (i + 1) * sets] for i in range(5))
    more, (out, h_t, g_t) = refs[5 * sets : 5 * sets + other], refs[5 * sets + other :]
    at = 0
    for h, g in zip(rows, grads):
        size = h.shape[0]
        h_t[:, at : at + size] = h[...].T
        g_t[:, at : at + size] = g[...].T
        at += size
    for i, (left, acts) in enumerate(((h_t, gates), (h_t, ups), (g_t, inners))):
        whole = jnp.concatenate([a[0] for a in acts], axis=0)
        grad = jnp.dot(left[...], whole, preferred_element_type=jnp.float32)
        if other:
            grad += more[0][i].astype(jnp.float32)
        out[i] = grad.astype(jnp.bfloat16)


def ffn_grads(slot, rows, grads, gates, ups, inners, *other):
    deep, hidden = rows[0].shape[1], gates[0].shape[2]
    length = sum(r.shape[0] for r in rows)
    whole = [pl.BlockSpec(r.shape, lambda i: (0, 0)) for r in rows]
    acts = [pl.BlockSpec((1, r.shape[0], hidden), lambda i: (slot, 0, 0)) for r in rows]
    weights = pl.BlockSpec((3, deep, hidden), lambda i: (0, 0, 0))
    both = pltpu.VMEM((deep, length), jnp.bfloat16)
    return pl.pallas_call(
        functools.partial(ffn_grads_kernel, sets=len(rows), other=len(other)),
        grid=(1,),
        in_specs=whole * 2 + acts * 3 + [weights] * len(other),
        out_specs=weights,
        out_shape=jax.ShapeDtypeStruct((3, deep, hidden), jnp.bfloat16),
        scratch_shapes=[both, both],
        compiler_params=pltpu.CompilerParams(vmem_limit_bytes=32 << 20),
        cost_estimate=pl.CostEstimate(
            flops=6 * length * deep * hidden, bytes_accessed=6 * deep * hidden + 6 * length * hidden, transcendentals=0
        ),
        name="ffn_grads",
    )(*rows, *grads, *gates, *ups, *inners, *other)


def proj_bwd_kernel(pair_grad, rest_grad, slab0, slab1, slab2, slab3, matrix, out_grad, made3, made1, made2, made0, grad, a_t, total):
    step = pl.program_id(0)
    width3 = total.shape[0]

    @pl.when(step == 0)
    def _():
        a_t[...] = matrix[:, :width3].T
        total[...] = jnp.zeros_like(total)

    def work(made, rows, out):
        total[...] += jnp.dot(made, rows, preferred_element_type=jnp.float32)
        out[...] = jnp.dot(made.T, a_t[...], preferred_element_type=jnp.float32).astype(jnp.bfloat16)

    pl.when(step == 0)(lambda: work(pair_grad[0], slab3[...], made3))
    pl.when(step == 1)(lambda: work(pair_grad[0], slab1[...], made1))
    pl.when(step == 2)(lambda: work(rest_grad[0], slab2[...], made2))
    pl.when(step == 3)(lambda: work(rest_grad[0], slab0[...], made0))

    @pl.when(step == 3)
    def _():
        grad[...] = jnp.concatenate([total[...], out_grad[...]], axis=0).astype(jnp.bfloat16).T


def proj_bwd(grad_proj, slabs, matrix, out_grad):
    _, width3, rows = grad_proj.shape
    features = matrix.shape[0]
    part = jax.ShapeDtypeStruct((rows, features), jnp.bfloat16)
    return pl.pallas_call(
        proj_bwd_kernel,
        grid=(4,),
        in_specs=[
            pl.BlockSpec((1, width3, rows), lambda i: (jnp.where(i == 0, 3, 1), 0, 0)),
            pl.BlockSpec((1, width3, rows), lambda i: (jnp.where(i == 3, 0, 2), 0, 0)),
            *[pl.BlockSpec((rows, features), lambda i: (0, 0))] * 4,
            pl.BlockSpec(matrix.shape, lambda i: (0, 0)),
            pl.BlockSpec(out_grad.shape, lambda i: (0, 0)),
        ],
        out_specs=(
            *[pl.BlockSpec((rows, features), lambda i: (0, 0))] * 4,
            pl.BlockSpec(matrix.shape, lambda i: (0, 0)),
        ),
        out_shape=(part, part, part, part, jax.ShapeDtypeStruct(matrix.shape, jnp.bfloat16)),
        scratch_shapes=[pltpu.VMEM((width3, features), jnp.bfloat16), pltpu.VMEM((width3, features), jnp.float32)],
        compiler_params=pltpu.CompilerParams(vmem_limit_bytes=60 << 20),
        cost_estimate=pl.CostEstimate(
            flops=16 * rows * features * width3, bytes_accessed=24 * rows * features, transcendentals=0
        ),
        name="proj_bwd",
    )(grad_proj, grad_proj, *slabs, matrix, out_grad)


ROW_TILE = 256


def mean_of(v):
    return jnp.mean(v, axis=-1, keepdims=True)


def mix_fwd_kernel(head0, head1, head2, head3, matrix, out1, out2, out3, rows, params, hidden, low, normed, inv, weights, *, width):
    @pl.when(pl.program_id(0) == 0)
    def _():
        weights[...] = jnp.concatenate([matrix[:, 3 * width :], out1[...], out2[...], out3[...]], axis=1)

    heads = jnp.concatenate([head0[...], head1[...], head2[...], head3[...]], axis=0).T
    mixed = rows[...].astype(jnp.float32) + lax.dot_general(heads, weights[...], NT, preferred_element_type=jnp.float32)
    centred = mixed - mean_of(mixed)
    inv_std = lax.rsqrt(mean_of(centred * centred) + NORM_EPS)
    unit = centred * inv_std
    out = unit * params[0:1, :] + params[1:2, :]
    hidden[...] = out
    low[...] = out.astype(jnp.bfloat16)
    normed[...] = unit
    inv[...] = inv_std


def mix_fwd(heads, matrix, outs, own, params):
    width, rows = heads[0].shape
    features = matrix.shape[0]
    whole = lambda a: pl.BlockSpec(a.shape, lambda i: (0,) * len(a.shape))
    block = pl.BlockSpec((ROW_TILE, features), lambda i: (i, 0))
    shape = lambda t: jax.ShapeDtypeStruct((rows, features), t)
    return pl.pallas_call(
        functools.partial(mix_fwd_kernel, width=width),
        grid=(rows // ROW_TILE,),
        in_specs=[pl.BlockSpec((width, ROW_TILE), lambda i: (0, i))] * 4
        + [whole(a) for a in (matrix, *outs)]
        + [block, whole(params)],
        out_specs=(block, block, block, pl.BlockSpec((ROW_TILE, 1), lambda i: (i, 0))),
        scratch_shapes=[pltpu.VMEM((features, 4 * width), jnp.bfloat16)],
        out_shape=(shape(jnp.float32), shape(jnp.bfloat16), shape(jnp.float32), jax.ShapeDtypeStruct((rows, 1), jnp.float32)),
        compiler_params=pltpu.CompilerParams(vmem_limit_bytes=60 << 20),
        cost_estimate=pl.CostEstimate(
            flops=2 * rows * features * features, bytes_accessed=14 * rows * features + 2 * features * features, transcendentals=rows
        ),
        name="mix_fwd",
    )(*heads, matrix, *outs, own, params)


def mix_bwd_kernel(
    grad_mixed, own_part, far_part, normed, inv, params, head0, head1, head2, head3, matrix, out1, out2, out3,
    grad_out, norms, made0, made1, made2, made3, og0, og1, og2, og3, turned, total, *, width,
):
    step = pl.program_id(0)

    @pl.when(step == 0)
    def _():
        for i, weight in enumerate((matrix[:, 3 * width :], out1[...], out2[...], out3[...])):
            turned[i * width : (i + 1) * width, :] = weight.T
        total[...] = jnp.zeros_like(total)
        norms[...] = jnp.zeros_like(norms)

    grad = grad_mixed[...] + own_part[...] + far_part[...].astype(jnp.float32)
    unit = normed[...]
    norms[0:1, :] += jnp.sum(grad * unit, axis=0, keepdims=True)
    norms[1:2, :] += jnp.sum(grad, axis=0, keepdims=True)
    grad_unit = grad * params[0:1, :]
    back = inv[...] * (grad_unit - mean_of(grad_unit) - unit * mean_of(grad_unit * unit))
    grad_out[...] = back
    low = back.astype(jnp.bfloat16)
    made = lax.dot_general(turned[...], low, NT, preferred_element_type=jnp.float32).astype(jnp.bfloat16)
    for i, out in enumerate((made0, made1, made2, made3)):
        out[...] = made[i * width : (i + 1) * width]
    heads = jnp.concatenate([head0[...], head1[...], head2[...], head3[...]], axis=0)
    total[...] += jnp.dot(heads, low, preferred_element_type=jnp.float32)

    @pl.when(step == pl.num_programs(0) - 1)
    def _():
        for i, og in enumerate((og0, og1, og2, og3)):
            og[...] = total[i * width : (i + 1) * width, :].astype(jnp.bfloat16)


def mix_bwd(grad_mixed, own_part, far_part, normed, inv, params, heads, matrix, outs):
    width, rows = heads[0].shape
    features = matrix.shape[0]
    whole = lambda a: pl.BlockSpec(a.shape, lambda i: (0,) * len(a.shape))
    shapes = (
        [jax.ShapeDtypeStruct((rows, features), jnp.float32), jax.ShapeDtypeStruct((2, features), jnp.float32)]
        + [jax.ShapeDtypeStruct((width, rows), jnp.bfloat16)] * 4
        + [jax.ShapeDtypeStruct((width, features), jnp.bfloat16)] * 4
    )
    ops = (grad_mixed, own_part, far_part, normed, inv, params, *heads, matrix, *outs)
    block = pl.BlockSpec((ROW_TILE, features), lambda i: (i, 0))
    slab = pl.BlockSpec((width, ROW_TILE), lambda i: (0, i))
    got = pl.pallas_call(
        functools.partial(mix_bwd_kernel, width=width),
        grid=(rows // ROW_TILE,),
        in_specs=[block] * 4
        + [pl.BlockSpec((ROW_TILE, 1), lambda i: (i, 0)), whole(params)]
        + [slab] * 4
        + [whole(a) for a in (matrix, *outs)],
        out_specs=(block, whole(shapes[1]), *[slab] * 4, *[whole(a) for a in shapes[6:]]),
        out_shape=tuple(shapes),
        scratch_shapes=[pltpu.VMEM((4 * width, features), jnp.bfloat16), pltpu.VMEM((4 * width, features), jnp.float32)],
        compiler_params=pltpu.CompilerParams(vmem_limit_bytes=60 << 20),
        cost_estimate=pl.CostEstimate(
            flops=4 * rows * features * features, bytes_accessed=22 * rows * features + 4 * features * features, transcendentals=0
        ),
        name="mix_bwd",
    )(*ops)
    return got[0], got[1], got[2:6], got[6:10]


def top_bwd_kernel(first, second, third, fourth, normed, inv, gain, low_in, back, low, norms):
    grad = first[...].astype(jnp.float32)
    for part in (second, third, fourth):
        if part is not None:
            grad += part[...].astype(jnp.float32)
    if low_in is not None:
        low_in[...] = grad.astype(jnp.bfloat16)
        grad = grad.astype(jnp.bfloat16).astype(jnp.float32)
    unit = normed[...]

    @pl.when(pl.program_id(0) == 0)
    def _():
        norms[...] = jnp.zeros_like(norms)

    norms[0:1, :] += jnp.sum(grad * unit, axis=0, keepdims=True)
    norms[1:2, :] += jnp.sum(grad, axis=0, keepdims=True)
    grad_unit = grad * gain[...]
    out = inv[...] * (grad_unit - mean_of(grad_unit) - unit * mean_of(grad_unit * unit))
    back[...] = out
    low[...] = out.astype(jnp.bfloat16)


def top_bwd(parts, normed, inv, gain):
    rows, features = normed.shape
    several = len(parts) > 1
    whole = lambda a: pl.BlockSpec(a.shape, lambda i: (0,) * len(a.shape))
    shape = lambda t: jax.ShapeDtypeStruct((rows, features), t)
    shapes = [shape(jnp.bfloat16)] * several + [shape(jnp.float32), shape(jnp.bfloat16)]
    shapes.append(jax.ShapeDtypeStruct((2, features), jnp.float32))
    ops = (*parts, normed, inv, gain)
    block = pl.BlockSpec((ROW_TILE, features), lambda i: (i, 0))

    def kernel(*refs):
        ins, outs = refs[: len(ops)], refs[len(ops) :]
        four = list(ins[: len(parts)]) + [None] * (4 - len(parts))
        top_bwd_kernel(*four, *ins[len(parts) :], *((None,) * (not several)), *outs)

    got = pl.pallas_call(
        kernel,
        grid=(rows // ROW_TILE,),
        in_specs=[block] * (len(parts) + 1) + [pl.BlockSpec((ROW_TILE, 1), lambda i: (i, 0)), whole(gain)],
        out_specs=(*[block] * (len(shapes) - 1), whole(shapes[-1])),
        out_shape=tuple(shapes),
        compiler_params=pltpu.CompilerParams(vmem_limit_bytes=60 << 20),
        cost_estimate=pl.CostEstimate(flops=12 * rows * features, bytes_accessed=18 * rows * features, transcendentals=0),
        name="top_bwd",
    )(*ops)
    return tuple(got) if several else (None, *got)


def lamb_step(weight, gradient, first_old, second):
    first_new = BETA_ONE * first_old + (1.0 - BETA_ONE) * gradient
    second_new = BETA_TWO * second + (1.0 - BETA_TWO) * gradient * gradient
    update = (
        first_new
        / (1.0 - BETA_ONE**STEP)
        / (jnp.sqrt(second_new / (1.0 - BETA_TWO**STEP)) + ADAM_EPS)
        + DECAY_RATE * weight
    )
    return first_new, second_new, update


def lamb_kernel(*refs, kinds, shards):
    count = len(kinds)
    made, refs = refs[:shards], refs[shards:]
    olds, news, late = refs[: 3 * count], refs[3 * count : 6 * count], refs[6 * count]
    late[...] = jnp.zeros_like(late)
    for i, (turned, parts) in enumerate(kinds):
        weight, first, second = olds[3 * i : 3 * i + 3]
        first_out, second_out, update_out = news[3 * i : 3 * i + 3]
        row = None
        for at, (index, columns) in enumerate(parts):
            gradient = sum(shard[index, :, columns].astype(jnp.float32) for shard in made)
            gradient = gradient.T if turned else gradient
            where = (at,) if len(weight.shape) == 3 else (slice(None),)
            first_new, second_new, update = lamb_step(weight[where], gradient, first[where], second[where])
            first_out[where] = first_new
            second_out[where] = second_new
            update_out[where] = update
            sums = jnp.sum(update * update, axis=0, keepdims=True)
            row = sums if row is None else row + sums
        late[i : i + 1, : row.shape[1]] = row


def lamb(made, kinds, olds, features):
    whole = lambda a: pl.BlockSpec(a.shape, lambda i: (0,) * len(a.shape))
    shapes = [jax.ShapeDtypeStruct(a.shape, jnp.float32) for a in olds]
    shapes.append(jax.ShapeDtypeStruct((len(kinds), features), jnp.float32))
    ops = (*made, *olds)
    return pl.pallas_call(
        functools.partial(lamb_kernel, kinds=kinds, shards=len(made)),
        grid=(1,),
        in_specs=[whole(a) for a in ops],
        out_specs=tuple(whole(a) for a in shapes),
        out_shape=tuple(shapes),
        compiler_params=pltpu.CompilerParams(vmem_limit_bytes=60 << 20),
        cost_estimate=pl.CostEstimate(flops=20 * made[0].size, bytes_accessed=28 * made[0].size, transcendentals=made[0].size),
        name="lamb",
    )(*ops)


def finish_kernel(totals, now, first, second, *refs, count):
    weights, updates = refs[:count], refs[count : 2 * count]
    norm_out, first_out, second_out, trust = refs[2 * count : 2 * count + 4]
    news = refs[2 * count + 4 :]
    for i in range(2):
        first_new, second_new, update = lamb_step(now[i], totals[2 * i : 2 * i + 2, :], first[i], second[i])
        norms = [jnp.sqrt(jnp.sum(v * v, axis=-1, keepdims=True)) for v in (now[i], update)]
        norm_out[i] = now[i] - LEARN_RATE * (norms[0] / norms[1]) * update
        first_out[i] = first_new
        second_out[i] = second_new
    sizes = jnp.sqrt(jnp.sum(totals[4:12, :], axis=-1, keepdims=True))
    trust[...] = jnp.concatenate([sizes[0:4], sizes[4:8]], axis=1).T
    for i in range(count):
        ratio = LEARN_RATE * (sizes[i : i + 1] / sizes[4 + i : 5 + i])
        for at in range(weights[i].shape[0]) if len(weights[i].shape) == 3 else (slice(None),):
            news[i][at] = weights[i][at] - ratio * updates[i][at]


def finish(totals, now, first, second, weights, updates):
    whole = lambda a: pl.BlockSpec(a.shape, lambda i: (0,) * len(a.shape))
    shapes = [jax.ShapeDtypeStruct(now.shape, jnp.float32)] * 3 + [jax.ShapeDtypeStruct((2, 4), jnp.float32)]
    shapes += [jax.ShapeDtypeStruct(a.shape, jnp.float32) for a in weights]
    ops = (totals, now, first, second, *weights, *updates)
    size = sum(a.size for a in weights)
    return pl.pallas_call(
        functools.partial(finish_kernel, count=len(weights)),
        grid=(1,),
        in_specs=[whole(a) for a in ops],
        out_specs=tuple(whole(a) for a in shapes),
        out_shape=tuple(shapes),
        compiler_params=pltpu.CompilerParams(vmem_limit_bytes=60 << 20),
        cost_estimate=pl.CostEstimate(flops=3 * size, bytes_accessed=12 * size, transcendentals=0),
        name="finish",
    )(*ops)


STEP = 10

BETA_ONE = 0.9
BETA_TWO = 0.999
ADAM_EPS = 1e-06
DECAY_RATE = 0.01
LEARN_RATE = 0.2
NORM_EPS = 1e-05
ROPE_BASE = 1000.0

bf16 = jnp.bfloat16
f32 = jnp.float32

BOTH = ("section", "tensor")
CELLS = [(c, y, x) for c in range(2) for y in range(2) for x in range(2)]


def number(c, y, x):
    return c * 4 + y * 2 + x


def moves(target):
    return [(number(*cell), number(*target(*cell))) for cell in CELLS]


SWAP = moves(lambda c, y, x: (y, c, x))
SWAP_BACK = moves(lambda c, y, x: (1 - y, c, x))
SWAP_OUT = moves(lambda c, y, x: (y, 1 - c, x))
CORNER = moves(lambda c, y, x: (1 - c, y, 1 - x))


def over_section(v):
    return lax.ppermute(v, "section", [(0, 1), (1, 0)])


def over_x(v):
    return lax.ppermute(v, "tensor", [(0, 1), (1, 0), (2, 3), (3, 2)])


def over_y(v):
    return lax.ppermute(v, "tensor", [(0, 2), (1, 3), (2, 0), (3, 1)])


def over_diag(v):
    return lax.ppermute(v, "tensor", [(0, 3), (1, 2), (2, 1), (3, 0)])


def over_both(v, pairs):
    return lax.ppermute(v, BOTH, pairs)


def over_z(v, k):
    return lax.ppermute(v, "dp", [(i, i ^ k) for i in range(4)])


def quad():
    return lax.axis_size("dp") == 4


def gather_later(piece, axis):
    return lax.all_gather(piece, "dp", axis=axis, tiled=True)


def scatter_later(whole, axis):
    return lax.psum_scatter(whole, "dp", scatter_dimension=axis, tiled=True)


def to_owner(shard, layer):
    same = [pair for pair in SWAP if pair[1] // 4 == layer]
    other = [pair for pair in SWAP_BACK if pair[1] // 4 == layer]
    return over_both(shard, same), over_both(shard, other)


def chips_total(v):
    v = (v + over_x(v)) + (over_y(v) + over_diag(v))
    if not quad():
        return lax.psum(v, "dp")
    return (v + over_z(v, 1)) + (over_z(v, 2) + over_z(v, 3))


def rope_tables(length):
    half_size = HEAD // 2
    freq_vals = np.float32(ROPE_BASE) ** (-np.arange(half_size, dtype=np.float32) * np.float32(2.0 / HEAD))
    angles = freq_vals[:, None] * np.arange(length, dtype=np.float32)[None, :]
    return jnp.asarray(np.cos(angles)), jnp.asarray(np.sin(angles))


def norm_fwd(values, gain_row, bias_row):
    mean_val = jnp.mean(values, axis=-1, keepdims=True)
    centred = values - mean_val
    variance = jnp.mean(centred * centred, axis=-1, keepdims=True)
    inv_std = lax.rsqrt(variance + NORM_EPS)
    normed = centred * inv_std
    return (normed * gain_row + bias_row, normed, inv_std)


def dot(spec, a, b):
    return jnp.einsum(spec, a, b, preferred_element_type=f32)


def after(value, *others):
    return lax.optimization_barrier((value,) + others)[0]


def halves(v):
    return jnp.split(v, 2, axis=0)


def layer_forward(slabs, matrix, ffn, params, env, late):
    place, ends, cos, sin = env
    *mine, log_sums, qkv = attn_fwd(place, ends, slabs, matrix, cos, sin)
    out_own = matrix[:, 3 * (matrix.shape[1] // 4) :]
    out_across = over_x(out_own)
    outs = (over_section(out_own), out_across, over_section(after(out_across, log_sums)))
    all_heads = [mine[0], over_section(mine[1]), over_x(mine[2]), over_both(mine[3], CORNER)]
    hidden, hidden_low, normed_one, inv_one = mix_fwd(all_heads, matrix, outs, slabs[0], params[:, 0])
    hidden_rows = [hidden_low] + [over_x(part) for part in halves(hidden_low)]
    ffn = (ffn, over_section(after(ffn, hidden_rows[late])))
    own_part, *own_acts = ffn_fwd(hidden_rows[0], *ffn, f32)
    first_part, *first_acts = ffn_fwd(hidden_rows[1], *ffn, bf16)
    second_part, *second_acts = ffn_fwd(after(hidden_rows[2], first_part), *ffn, bf16)
    ffn_out = own_part + jnp.concatenate([over_x(first_part), over_x(second_part)]).astype(f32)
    output, normed_two, inv_two = norm_fwd(hidden + ffn_out, params[0, 1], params[1, 1])
    kept = (slabs, qkv, mine, log_sums, all_heads, normed_one, inv_one, hidden_rows, (own_acts, first_acts, second_acts))
    return output.astype(bf16), outs, kept + (normed_two, inv_two, ffn)


def layer_backward(grad_parts, kept, matrix, outs, params, env, early=(), late=()):
    place, ends, cos, sin = env
    (slabs, qkv, mine, log_sums, all_heads, normed_one, inv_one, hidden_rows, acts, normed_two, inv_two, ffn) = kept
    sent, grad_mixed, grad_low, norm_two = top_bwd(grad_parts, normed_two, inv_two, params[0, 1:2])
    grad_rows = [grad_low] + [over_x(part) for part in halves(grad_low)]
    own_part, *own_grads = ffn_bwd(grad_rows[0], *acts[0], *ffn, f32)
    first_part, *first_grads = ffn_bwd(after(grad_rows[1], own_part, *early), *acts[1], *ffn, bf16)
    second_part, *second_grads = ffn_bwd(after(grad_rows[2], first_part), *acts[2], *ffn, bf16)
    made = list(zip(own_grads, first_grads, second_grads))
    ffn_other = ffn_grads(1, hidden_rows, grad_rows, *made)
    ffn_grad = ffn_grads(0, hidden_rows, grad_rows, *made, over_section(ffn_other))
    far_part = jnp.concatenate([over_x(first_part), over_x(second_part)])
    ffn_grad = after(ffn_grad, far_part)
    grad_mixed_one, norm_one, grad_heads, out_grad = mix_bwd(
        grad_mixed, own_part, far_part, normed_one, inv_one, params[:, 0], all_heads, matrix, outs
    )
    grad_mine = (
        grad_heads[0], over_section(grad_heads[1]), over_x(grad_heads[2]), over_both(grad_heads[3], CORNER)
    )
    *out_grad, _ = lax.optimization_barrier((*out_grad, grad_mine))
    out_own = (out_grad[0], over_section(out_grad[1]), over_x(out_grad[2]), over_both(out_grad[3], CORNER))
    grad_proj = attn_bwd(place, ends, qkv, grad_mine, mine, log_sums, cos, sin)
    out_own = sum(g.astype(f32) for g in after(out_own, grad_proj, *late))
    part3, part1, part2, part0, matrix_grad = proj_bwd(grad_proj, slabs, matrix, out_own)
    far_sum = over_x((part2.astype(f32) + over_section(part3).astype(f32)).astype(bf16))
    norm_grads = jnp.stack([jnp.stack([norm_one[0], norm_two[0]]), jnp.stack([norm_one[1], norm_two[1]])])
    return sent, (grad_mixed_one, part0, over_section(part1), far_sum), matrix_grad, ffn_grad, norm_grads


def body(
    tokens,
    cotangent,
    segments,
    heads_in,
    heads_out,
    gate_up,
    project_down,
    norm_gain,
    norm_bias,
    heads_in_first,
    heads_in_second,
    heads_out_first,
    heads_out_second,
    gate_up_first,
    gate_up_second,
    project_down_first,
    project_down_second,
    norm_first,
    norm_second,
):
    section = lax.axis_index("section")
    spot = lax.axis_index("tensor")
    y, x = spot // 2, spot % 2
    rows = tokens.shape[1]
    length = segments.shape[-1]
    masters = (heads_in[0], heads_out[0], gate_up[0], project_down[0].T)
    deep, width = masters[0].shape[1:]

    attn_piece = jnp.concatenate(
        [masters[0].transpose(1, 0, 2).reshape(deep, 3 * width), masters[1].T], axis=1
    ).astype(bf16)
    ffn_piece = jnp.concatenate([masters[2], masters[3][None]], axis=0).astype(bf16)

    def to_block(piece, layer):
        got = []
        for to_y in range(2):
            pairs = [(number(layer, c, x), number(c, to_y, x)) for c in range(2) for x in range(2)]
            got.append(over_both(piece, pairs))
        return got

    def for_y(got):
        return jnp.where(y == 0, got[0], got[1])

    def four_slabs(rows, *along):
        across, *along = lax.optimization_barrier((over_x(rows), *along))
        return (rows, over_section(rows), across, over_section(across)), along

    own = over_both(lax.dynamic_index_in_dim(tokens, section, 0, keepdims=False), SWAP)
    first_matrix = gather_later(for_y(to_block(attn_piece, 0)), 0)
    slabs_zero, ffn_pieces = four_slabs(own, *to_block(after(ffn_piece, own), 0))
    ffn_first = gather_later(for_y(ffn_pieces), 1)

    both_params = jnp.stack([norm_gain[0], norm_bias[0]])
    other_params = over_section(both_params)
    params = [
        jnp.where(section == 0, both_params, other_params),
        jnp.where(section == 0, other_params, both_params),
    ]

    block = 2 * section + x
    place = jnp.stack([block, block ^ 2, block ^ 1, block ^ 3]).astype(jnp.int32)
    seq_seg = lax.dynamic_index_in_dim(segments, y, 0, keepdims=False)[0]
    ends = jnp.stack([jnp.sum((seq_seg <= d).astype(jnp.int32)) for d in range(2)])
    env = (place, ends) + rope_tables(length)

    low_zero, outs_zero, kept_zero = layer_forward(slabs_zero, first_matrix, ffn_first, params[0], env, 1)
    hidden_rows = kept_zero[7]
    second_piece = for_y(to_block(after(jnp.concatenate([attn_piece[None], ffn_piece]), slabs_zero[3]), 1))
    second_matrix = gather_later(after(second_piece[0], hidden_rows[0]), 0)
    ffn_second = gather_later(after(second_piece[1:], hidden_rows[1]), 1)
    slabs_one, _ = four_slabs(low_zero)
    low_one, outs_one, kept_one = layer_forward(slabs_one, second_matrix, ffn_second, params[1], env, 0)
    grad_top = over_both(after(lax.dynamic_index_in_dim(cotangent, section, 0, keepdims=False), low_zero), SWAP)
    def home(zero, one):
        same = over_both(jnp.where(y == 0, zero, one), SWAP)
        other = over_both(jnp.where(y == 0, one, zero), SWAP_BACK)
        return same, other

    def by_micro(same, other):
        return jnp.stack([jnp.where(section == 0, same, other), jnp.where(section == 0, other, same)])

    layer_home = home(low_zero, low_one)
    layer_out = by_micro(*layer_home)
    _, grads_one, matrix_one, ffn_one, norm_one = layer_backward(
        (grad_top,), kept_one, second_matrix, outs_one, params[1], env, layer_home
    )
    ffn_one = to_owner(scatter_later(ffn_one, 1), 1)
    matrix_one = to_owner(scatter_later(matrix_one, 0)[None], 1)
    sent, grads_zero, matrix_zero, ffn_zero, norm_zero = layer_backward(
        grads_one, kept_zero, first_matrix, outs_zero, params[0], env, ffn_one, matrix_one
    )
    ffn_home = to_owner(scatter_later(ffn_zero, 1), 0) + ffn_one
    attn_home = to_owner(scatter_later(matrix_zero, 0)[None], 0)
    grad_zero = sum(g.astype(f32) for g in grads_zero)


    norm_mine = jnp.where(section == 0, norm_zero, norm_one) + over_section(
        jnp.where(section == 0, norm_one, norm_zero)
    )
    features = norm_mine.shape[-1]
    firsts = (heads_in_first[0], heads_out_first[0], gate_up_first[0], project_down_first[0].T)
    seconds = (heads_in_second[0], heads_out_second[0], gate_up_second[0], project_down_second[0].T)
    olds = list(zip(masters, firsts, seconds))

    def squares(matrix):
        row = jnp.sum((matrix * matrix).reshape(-1, matrix.shape[-1]), axis=0)
        return jnp.pad(row, (0, features - row.shape[0]))

    columns = slice(0, masters[2].shape[-1])
    ffn_new = lamb(
        ffn_home, ((False, ((0, columns), (1, columns))), (False, ((2, columns),))), olds[2] + olds[3], features
    )
    early = jnp.stack([squares(m) for m in masters])
    early = jnp.concatenate([norm_mine.reshape(4, -1), early], axis=0)
    attn_home = lax.optimization_barrier((*attn_home, early, ffn_new[-1]))[:2] + matrix_one
    pieces = tuple((0, slice(i * width, (i + 1) * width)) for i in range(4))
    attn_new = lamb(attn_home, ((False, pieces[:3]), (True, pieces[3:])), olds[0] + olds[1], features)
    totals = chips_total(jnp.concatenate([early, attn_new[-1], ffn_new[-1]], axis=0))
    made = [attn_new[:3], attn_new[3:6], ffn_new[:3], ffn_new[3:6]]
    *norms, trust_norms, in_new, out_new, gate_new, down_new = finish(
        totals, both_params, norm_first[0], norm_second[0], masters, [m[2] for m in made]
    )
    new_mats = (in_new, out_new, gate_new, down_new.T)
    made[3] = [v.T for v in made[3]]
    input_grads = by_micro(*home(after(grad_zero.astype(bf16), attn_home[0]), sent)).astype(f32)
    outs = [layer_out, input_grads]
    for i in range(4):
        outs += [new_mats[i], made[i][0], made[i][1]]
    outs += [*norms, trust_norms.T]
    return tuple(item[None] for item in outs)


def solution(mesh):
    rows = P(None, ("dp", "tensor"), None)
    out_rows = P("section", None, ("dp", "tensor"), None)
    columns = P("section", None, "dp", "tensor")
    turned = P("section", "tensor", "dp")
    vectors = P("section", None, None)
    pairs = P("section", None, None, None)
    return jax.shard_map(
        body,
        mesh=mesh,
        in_specs=(rows, rows, P(None, "dp", None), columns, turned, columns, turned, vectors, vectors)
        + (columns, columns, turned, turned, columns, columns, turned, turned, pairs, pairs),
        out_specs=(out_rows, out_rows)
        + (columns,) * 3
        + (turned,) * 3
        + (columns,) * 3
        + (turned,) * 3
        + (pairs,) * 3
        + (vectors,),
        check_vma=False,
    )
```
